32 devices in a mesh: dp: 8 (over y, x, core), seq: 4 (over z).
Axes of the slice: x: 2, y: 2, z: 4, core: 2. Of those that a mesh axis runs over, the one named last changes fastest.
Arguments:
- inputs: bfloat16 [8, 512, 2048], P('dp', 'seq'), may hold values from -6 to 6
- cotangent: bfloat16 [8, 512, 2048], P('dp', 'seq'), may hold values from -6 to 6
- segments: int32 [8, 512], P('dp', 'seq'), may hold values from 0 to 16, as said below
- labels: int32 [8, 512], P('dp', 'seq'), may hold values from 0 to 1
- step_ends: int32 [8, 512], P('dp', 'seq'), may hold values 0 or 1
- attend_gain: bfloat16 [2048], P(('dp', 'seq')), may hold values from 0.5 to 1.5
- attend_shift: bfloat16 [2048], P(('dp', 'seq')), may hold values from -1 to 1
- project_in: bfloat16 [2048, 6144], P(('dp', 'seq')), may hold values from -0.1875 to 0.1875
- project_bias: bfloat16 [4096], P(('dp', 'seq')), may hold values from -1 to 1
- project_out: bfloat16 [2048, 2048], P(('dp', 'seq')), may hold values from -1 to 1
- output_bias: bfloat16 [2048], P(('dp', 'seq')), may hold values from -1 to 1
- dense_gain: bfloat16 [2048], P(('dp', 'seq')), may hold values from 0.5 to 1.5
- dense_shift: bfloat16 [2048], P(('dp', 'seq')), may hold values from -1 to 1
- up_weight: bfloat16 [2048, 8192], P(('dp', 'seq')), may hold values from -0.125 to 0.125
- up_bias: bfloat16 [8192], P(('dp', 'seq')), may hold values from -1 to 1
- down_weight: bfloat16 [8192, 2048], P(('dp', 'seq')), may hold values from -0.0625 to 0.0625
- down_bias: bfloat16 [2048], P(('dp', 'seq')), may hold values from -1 to 1
- reward_weight: bfloat16 [2048], P(('dp', 'seq')), may hold values from -0.125 to 0.125
Outputs:
- outputs: bfloat16 [8, 512, 2048], P('dp', 'seq')
- rewards: float32 [8, 512], P('dp', 'seq')
- inputs_gradient: float32 [8, 512, 2048], P('dp', 'seq')
- attend_gain_gradient: float32 [2048], P(('dp', 'seq'))
- attend_shift_gradient: float32 [2048], P(('dp', 'seq'))
- project_in_gradient: float32 [2048, 6144], P(('dp', 'seq'))
- project_bias_gradient: float32 [4096], P(('dp', 'seq'))
- project_out_gradient: float32 [2048, 2048], P(('dp', 'seq'))
- output_bias_gradient: float32 [2048], P(('dp', 'seq'))
- dense_gain_gradient: float32 [2048], P(('dp', 'seq'))
- dense_shift_gradient: float32 [2048], P(('dp', 'seq'))
- up_weight_gradient: float32 [2048, 8192], P(('dp', 'seq'))
- up_bias_gradient: float32 [8192], P(('dp', 'seq'))
- down_weight_gradient: float32 [8192, 2048], P(('dp', 'seq'))
- down_bias_gradient: float32 [2048], P(('dp', 'seq'))
- reward_weight_gradient: float32 [2048], P(('dp', 'seq'))
The draws below stay inside these ranges and needn't reach their ends.
Inputs may be any that keep to these rules, and one draw needn't show every extreme that they name: `segments`: in each row, the positions before a prefix length of 64 to 128 hold 0; then come 4 to 16 solutions numbered 1 upward in order, each a run of one or more positions; one row has 16 solutions.
All inputs are finite; a program needn't handle non-finite values. No bound on the sum of `step_ends` on one device may be relied on, other than what follows from the above.
Results may differ from the reference program's by a relative error of at most 0.013.
Values may be sent and summed in bfloat16 or wider, within the bound.
No kernel may reach another device: no remote copies, remote signals or barrier semaphores. Data moves between devices by JAX's collectives and lax.ppermute only.
A program may use at most 272 MiB of HBM per device.

```python
import jax
import jax.numpy as jnp
from jax import lax

D = 2048
HEADS = 16
HEAD_DIM = 128
FF = 8192
SOLUTIONS = 16
ROWS = 8
LENGTH = 512


def draw_segments(key, part):
    key = jax.random.fold_in(key, 7)
    split_keys = jax.random.split(key, 5)
    count = jax.random.randint(split_keys[0], (ROWS,), 4, SOLUTIONS + 1)
    full_row = jax.random.randint(split_keys[1], (), 0, ROWS)
    count = jnp.where(jnp.arange(ROWS) == full_row, SOLUTIONS, count)
    prefix = jax.random.randint(split_keys[2], (ROWS,), LENGTH // 8, LENGTH // 4 + 1)
    slot = jnp.arange(SOLUTIONS)
    live = slot[None, :] < count[:, None]
    bound_short = jnp.maximum((LENGTH - prefix) // (2 * SOLUTIONS), 1)
    raw_bits = jax.random.randint(split_keys[3], (ROWS, SOLUTIONS), 0, 1 << 20)
    short_runs = 1 + raw_bits % bound_short[:, None]
    longest = jax.random.randint(split_keys[4], (ROWS,), 0, count)
    is_long = slot[None, :] == longest[:, None]
    short_runs = jnp.where(live & jnp.logical_not(is_long), short_runs, 0)
    long_run = LENGTH - prefix - jnp.sum(short_runs, axis=1)
    run_lengths = jnp.where(is_long, long_run[:, None], short_runs)
    run_ends = prefix[:, None] + jnp.cumsum(run_lengths, axis=1)
    places = jnp.arange(LENGTH)
    passed = jnp.sum((run_ends[:, None, :] <= places[None, :, None]).astype(jnp.int32), axis=2)
    return jnp.where(places[None, :] < prefix[:, None], 0, 1 + passed).astype(jnp.int32)


def plant(values, stream_key, least, high):
    place = [jax.random.randint(jax.random.fold_in(stream_key, axis), (), 0, length) for axis, length in enumerate(values.shape)]
    widest = values.shape.index(max(values.shape))
    next_to = place[:widest] + [(place[widest] + 1) % values.shape[widest]] + place[widest + 1:]
    return values.at[tuple(place)].set(least).at[tuple(next_to)].set(high)


def steps_of(rng, shape, shards, low, high):
    def one(position, parts):
        heights = jax.random.uniform(jax.random.fold_in(jax.random.fold_in(rng, 6), position), (parts,), jnp.float32, low / len(shards), high / len(shards))
        return jnp.repeat(jnp.exp(heights), shape[position] // parts).reshape((-1,) + (1,) * (len(shape) - position - 1))

    loudness = one(*shards[0])
    for cut in shards[1:]:
        loudness = loudness * one(*cut)
    return loudness


def gaussian(own_key, shape, deviation, limit, cuts=(), held_as=jnp.bfloat16):
    factor_of = steps_of(own_key, shape, cuts, -0.22, 0.18) if cuts else 1.0
    values = jax.random.normal(own_key, shape, jnp.float32) * deviation * factor_of
    return jnp.minimum(jnp.maximum(values, -limit), limit).astype(held_as)


def setup_inputs(seed: int = 0) -> dict:
    seeds = jax.random.split(jax.random.key(seed), 19)
    return {
        "inputs": gaussian(seeds[0], (ROWS, LENGTH, D), 1.0, 6.0, ((0, 8), (1, 4))),
        "cotangent": gaussian(seeds[1], (ROWS, LENGTH, D), 1.0, 6.0, ((0, 8), (1, 4))),
        "segments": draw_segments(jax.random.fold_in(seeds[18], 71), 0),
        "labels": plant(jax.random.randint(seeds[3], (ROWS, LENGTH), 0, 2), jax.random.fold_in(seeds[3], 1), 0, 1).astype(jnp.int32),
        "step_ends": plant((jax.random.randint(seeds[4], (ROWS, LENGTH), 0, 8) < 1).astype(jnp.int32), jax.random.fold_in(seeds[4], 1), 0, 1),
        "attend_gain": jnp.clip(1.0 + 0.1 * jax.random.normal(seeds[5], (D,), jnp.float32), 0.5, 1.5).astype(jnp.bfloat16),
        "attend_shift": gaussian(seeds[6], (D,), 0.2, 1.0, ((0, 32),)),
        "project_in": gaussian(seeds[7], (D, 3 * D), (D // 2) ** -0.5, 0.1875, ((0, 32),)),
        "project_bias": gaussian(seeds[8], (2 * D,), 0.2, 1.0, ((0, 32),)),
        "project_out": gaussian(seeds[9], (D, D), (D // 64) ** -0.5, 1.0, ((0, 32),)),
        "output_bias": gaussian(seeds[10], (D,), 0.2, 1.0, ((0, 32),)),
        "dense_gain": jnp.clip(1.0 + 0.1 * jax.random.normal(seeds[11], (D,), jnp.float32), 0.5, 1.5).astype(jnp.bfloat16),
        "dense_shift": gaussian(seeds[12], (D,), 0.2, 1.0, ((0, 32),)),
        "up_weight": gaussian(seeds[13], (D, FF), D ** -0.5, 0.125, ((0, 32),)),
        "up_bias": gaussian(seeds[14], (FF,), 0.2, 1.0, ((0, 32),)),
        "down_weight": gaussian(seeds[15], (FF, D), FF ** -0.5, 0.0625, ((0, 32),)),
        "down_bias": gaussian(seeds[16], (D,), 0.2, 1.0, ((0, 32),)),
        "reward_weight": gaussian(seeds[17], (D,), D ** -0.5, 0.125, ((0, 32),)),
    }


@jax.custom_vjp
def low(v):
    return lax.optimization_barrier(v.astype(jnp.bfloat16)).astype(jnp.float32)

@jax.custom_vjp
def low_back(v):
    return v

def low_keep(v):
    return (low(v), None)

def low_pass(kept, grad):
    return (grad,)

def back_keep(v):
    return (v, None)

def back_low(kept, grad):
    return (low(grad),)
low.defvjp(low_keep, low_pass)
low_back.defvjp(back_keep, back_low)
PRECISE = lax.Precision.HIGHEST
EPSILON = 1e-05
MASKED = -1e+30

def matmul(left, right):
    return jnp.dot(left, right, precision=PRECISE, preferred_element_type=jnp.float32)

def normalize(field, gain, shift):
    center = field - lax.optimization_barrier(jnp.mean(field, axis=-1, keepdims=True))
    spread = lax.optimization_barrier(jnp.mean(center * center, axis=-1, keepdims=True))
    return center * lax.rsqrt(spread + EPSILON) * gain + shift

def attend_row(bundle):
    query_row, key_row, value_row, segment_row = bundle
    places = jnp.arange(segment_row.shape[0])
    same_group = (segment_row[None, :] == 0) | (segment_row[None, :] == segment_row[:, None])
    allowed = same_group & (places[None, :] <= places[:, None])
    scores = jnp.einsum('qhd,khd->hqk', query_row, key_row, precision=PRECISE) * query_row.shape[-1] ** (-0.5)
    scores = low_back(jnp.where(allowed[None], scores, MASKED))
    chances = low(jax.nn.softmax(scores, axis=-1))
    return jnp.einsum('hqk,khd->qhd', chances, value_row, precision=PRECISE)

def forward(flat_inputs, attend_gain, attend_shift, project_in, project_bias, project_out, output_bias, dense_gain, dense_shift, up_weight, up_bias, down_weight, down_bias, reward_weight, segments, targets, scored):
    first = low(normalize(flat_inputs, attend_gain, attend_shift))
    projected = matmul(first, project_in)
    queries = low(low_back(projected[:, :D] + project_bias[:D]))
    keys_only = low(low_back(projected[:, D:2 * D]))
    values = low(low_back(projected[:, 2 * D:] + project_bias[D:]))
    head_shape = (ROWS, LENGTH, HEADS, HEAD_DIM)
    mixture = lax.map(jax.checkpoint(attend_row), (queries.reshape(head_shape), keys_only.reshape(head_shape), values.reshape(head_shape), segments))
    mixture = low(low_back(mixture.reshape(ROWS * LENGTH, D)))
    branch = low_back(matmul(mixture, project_out) + output_bias)
    hidden = flat_inputs + branch
    second = low(normalize(hidden, dense_gain, dense_shift))
    upward = low_back(matmul(second, up_weight) + up_bias)
    activated = low(jax.nn.gelu(upward, approximate=True))
    dense_out = low_back(matmul(activated, down_weight) + down_bias)
    result = hidden + dense_out
    rewards = lax.optimization_barrier(jnp.sum(result * reward_weight, axis=-1))
    loss = jnp.sum(scored * (jax.nn.softplus(rewards) - targets * rewards)) / ROWS
    return (result, rewards, loss)

def reference(inputs, cotangent, segments, labels, step_ends, attend_gain, attend_shift, project_in, project_bias, project_out, output_bias, dense_gain, dense_shift, up_weight, up_bias, down_weight, down_bias, reward_weight):
    scored = (step_ends * (segments > 0)).astype(jnp.float32).reshape(ROWS * LENGTH)
    targets = labels.astype(jnp.float32).reshape(ROWS * LENGTH)

    def objective(flat_inputs, *weights):
        return forward(flat_inputs, *weights, segments, targets, scored)
    weights = (attend_gain.astype(jnp.float32), attend_shift.astype(jnp.float32), project_in.astype(jnp.float32), project_bias.astype(jnp.float32), project_out.astype(jnp.float32), output_bias.astype(jnp.float32), dense_gain.astype(jnp.float32), dense_shift.astype(jnp.float32), up_weight.astype(jnp.float32), up_bias.astype(jnp.float32), down_weight.astype(jnp.float32), down_bias.astype(jnp.float32), reward_weight.astype(jnp.float32))
    flat_inputs = inputs.astype(jnp.float32).reshape(ROWS * LENGTH, D)
    (result, rewards, loss), pullback = jax.vjp(objective, flat_inputs, *weights)
    grads = pullback((cotangent.astype(jnp.float32).reshape(ROWS * LENGTH, D), jnp.zeros_like(rewards), jnp.ones_like(loss)))
    return (result.astype(jnp.bfloat16).reshape(ROWS, LENGTH, D), rewards.reshape(ROWS, LENGTH), grads[0].reshape(ROWS, LENGTH, D), grads[1], grads[2], grads[3], grads[4], grads[5], grads[6], grads[7], grads[8], grads[9], grads[10], grads[11], grads[12], grads[13])
```

```python
from functools import partial

import jax
import jax.numpy as jnp
from jax import lax
from jax.sharding import PartitionSpec as P

HEADS = 16
EPSILON = 1e-05
MASKED = -1e30
LOW = jnp.bfloat16
WIDE = jnp.float32
EVERY = ("dp", "seq")


def product(left, right):
    return jnp.dot(left, right, preferred_element_type=WIDE)


def inner_rows(left, right):
    return jnp.einsum("ta,tb->ab", left, right, preferred_element_type=WIDE)


def against_rows(left, right):
    return jnp.einsum("tb,ab->ta", left, right, preferred_element_type=WIDE)


def normalize_parts(field, gain, shift):
    center = field - jnp.mean(field, axis=-1, keepdims=True)
    spread = jnp.mean(center * center, axis=-1, keepdims=True)
    inverse = lax.rsqrt(spread + EPSILON)
    normal = center * inverse
    return (normal * gain + shift, normal, inverse)


def normalize_back(upstream, normal, inverse, gain):
    scaled = upstream * gain
    mean_scaled = jnp.mean(scaled, axis=-1, keepdims=True)
    mean_cross = jnp.mean(scaled * normal, axis=-1, keepdims=True)
    return inverse * (scaled - mean_scaled - normal * mean_cross)


def ring_next():
    size = lax.axis_size("seq")
    return [(place, (place + 1) % size) for place in range(size)]


def ring_gather(block):
    blocks = [block]
    for _ in range(lax.axis_size("seq") - 1):
        block = lax.ppermute(block, "seq", ring_next())
        blocks.append(block)
    return blocks


def ring_sum(parts):
    total = parts[1]
    for part in parts[2:] + parts[:1]:
        total = lax.ppermute(total.astype(LOW), "seq", ring_next()).astype(WIDE) + part
    return total


def to_ring(table):
    size = lax.axis_size("seq")
    me = lax.axis_index("seq")
    return jnp.stack(
        [lax.dynamic_index_in_dim(table, (me - k) % size, 0, keepdims=False) for k in range(size)]
    )


def head_split():
    groups, ranks = lax.axis_size("dp"), lax.axis_size("seq")
    blocks = groups * ranks // HEADS
    if blocks <= ranks:
        return ((blocks, groups // blocks, ranks // blocks), (2, 0, 1))
    return ((HEADS // ranks, ranks), (1, 0))


def heads_by_rank(table):
    split, order = head_split()
    width = table.shape[-1]
    moved = table.reshape(split + (width,)).transpose(order + (len(split),))
    return moved.reshape(lax.axis_size("seq"), -1)


def heads_from_rank(table):
    split, order = head_split()
    width = table.size // HEADS
    back = [order.index(axis) for axis in range(len(order))]
    moved = table.reshape(tuple(split[axis] for axis in order) + (width,))
    return moved.transpose(tuple(back) + (len(split),)).reshape(HEADS, width)


def out_route():
    groups, ranks = lax.axis_size("dp"), lax.axis_size("seq")
    blocks = groups * ranks // HEADS
    route = []
    for group in range(groups):
        for rank in range(ranks):
            if blocks <= ranks:
                held = groups // blocks
                high, low = divmod(group, held)
                pair, part = divmod(rank, blocks)
                target = (part * held + low, pair * blocks + high)
            else:
                span = blocks // ranks
                head, extra = divmod(group, span)
                high, low = divmod(head, ranks)
                target = ((high * ranks + rank) * span + extra, low)
            route.append((group * ranks + rank, target[0] * ranks + target[1]))
    return route


def out_parts():
    groups, ranks = lax.axis_size("dp"), lax.axis_size("seq")
    blocks = groups * ranks // HEADS
    if blocks <= ranks:
        return ((blocks, groups // blocks), (1, 0))
    return ((HEADS // ranks, ranks, blocks // ranks), (0, 2, 1))


def out_gather(block):
    moved = lax.ppermute(block, EVERY, out_route())
    whole = lax.all_gather(moved, "dp", axis=0, tiled=False)
    split, order = out_parts()
    tail = tuple(range(len(split), len(split) + 2))
    return whole.reshape(split + block.shape).transpose(order + tail).reshape(-1, block.shape[1])


def out_scatter(gradient, rows):
    split, order = out_parts()
    back = tuple(order.index(axis) for axis in range(len(order)))
    tail = tuple(range(len(split), len(split) + 2))
    width = gradient.shape[1]
    parted = gradient.reshape(tuple(split[axis] for axis in order) + (rows, width))
    parted = parted.transpose(back + tail).reshape(-1, width)
    summed = scatter_groups(parted)
    return lax.ppermute(summed, EVERY, [(there, here) for here, there in out_route()])


def gather_groups(block):
    return lax.all_gather(block, "dp", axis=0, tiled=True)


def scatter_groups(gradient):
    return lax.psum_scatter(gradient.astype(LOW), "dp", scatter_dimension=0, tiled=True)


def swap_ranks(blocks):
    return lax.all_to_all(blocks, "seq", split_axis=0, concat_axis=0, tiled=True)


def spread_path(
    inputs,
    cotangent,
    segments,
    labels,
    step_ends,
    attend_gain,
    attend_shift,
    project_in,
    project_bias,
    project_out,
    output_bias,
    dense_gain,
    dense_shift,
    up_weight,
    up_bias,
    down_weight,
    down_bias,
    reward_weight,
):
    groups, ranks = lax.axis_size("dp"), lax.axis_size("seq")
    rank = lax.axis_index("seq")
    rows_here, places_here, width = inputs.shape
    all_rows = rows_here * groups
    head_width = width // HEADS
    heads_here = HEADS // ranks
    share = heads_here * head_width
    rows_in = project_in.shape[0]
    hidden_here = down_weight.shape[0]
    length = ranks * places_here
    score_scale = head_width ** (-0.5)

    small = (
        attend_gain,
        attend_shift,
        project_bias,
        output_bias,
        dense_gain,
        dense_shift,
        up_bias,
        down_bias,
        reward_weight,
    )
    sizes = [vector.shape[0] for vector in small]
    gathered = lax.all_gather(jnp.concatenate(small), EVERY, axis=0, tiled=False).astype(WIDE)
    vectors = []
    start = 0
    for size in sizes:
        vectors.append(gathered[:, start : start + size].reshape(-1))
        start += size
    gain_one, shift_one, bias_in, bias_out, gain_two, shift_two, bias_up, bias_down, reward_wide = (
        vectors
    )

    def own_heads(vector):
        return lax.dynamic_index_in_dim(
            heads_by_rank(vector.reshape(HEADS, head_width)), rank, 0, keepdims=False
        )

    bias_full = jnp.concatenate(
        [own_heads(bias_in[:width]), jnp.zeros((share,), WIDE), own_heads(bias_in[width:])]
    )
    bias_up_here = lax.dynamic_index_in_dim(
        bias_up.reshape(groups, ranks, hidden_here), rank, 1, keepdims=False
    ).reshape(-1)
    marks = lax.all_gather(
        jnp.stack([segments[0], labels[0], step_ends[0]]), "seq", axis=0, tiled=False
    )
    marks_ring = to_ring(marks)
    segments_ring = marks_ring[:, 0].reshape(-1)
    places_ring = to_ring(jnp.arange(length).reshape(ranks, places_here)).reshape(-1)

    pieces = project_in.reshape(rows_in, 3, HEADS, head_width)
    columns_in = jnp.stack(
        [
            jnp.concatenate([part[rank_] for part in parts], axis=1)
            for parts in [
                [
                    heads_by_rank(
                        pieces[:, which].transpose(1, 0, 2).reshape(HEADS, rows_in * head_width)
                    )
                    .reshape(ranks, heads_here, rows_in, head_width)
                    .transpose(0, 2, 1, 3)
                    .reshape(ranks, rows_in, share)
                    for which in range(3)
                ]
            ]
            for rank_ in range(ranks)
        ]
    )
    weight_in = gather_groups(swap_ranks(columns_in).reshape(ranks * rows_in, 3 * share))
    weight_out = out_gather(project_out)
    columns_up = up_weight.reshape(rows_in, groups, ranks, hidden_here).transpose(2, 0, 1, 3)
    columns_up = columns_up.reshape(ranks, rows_in, groups * hidden_here)
    weight_up = gather_groups(swap_ranks(columns_up).reshape(ranks * rows_in, groups * hidden_here))
    weight_down = gather_groups(down_weight)

    inputs_ring = ring_gather(inputs[0])
    own = inputs[0].astype(WIDE)
    firsts = []
    shifted = []
    for block in inputs_ring:
        value, normal, inverse = normalize_parts(block.astype(WIDE), gain_one, shift_one)
        if not firsts:
            first_normal, first_inverse = normal, inverse
        firsts.append(value.astype(LOW))
        shifted.append((product(firsts[-1], weight_in) + bias_full).astype(LOW))
    first_low = jnp.concatenate(firsts)
    projected = jnp.concatenate(shifted)

    def heads(block):
        return block.reshape(length, heads_here, head_width)

    queries, keys, values = (
        heads(projected[:, :share]),
        heads(projected[:, share : 2 * share]),
        heads(projected[:, 2 * share :]),
    )
    same = (segments_ring[None, :] == 0) | (segments_ring[None, :] == segments_ring[:, None])
    allowed = same & (places_ring[None, :] <= places_ring[:, None])
    scores = jnp.einsum("qhd,khd->hqk", queries, keys, preferred_element_type=WIDE) * score_scale
    scores = jnp.where(allowed[None], scores, MASKED)
    highest = jnp.max(scores, axis=-1, keepdims=True)
    exponent = jnp.exp(scores - highest)
    totals = jnp.sum(exponent, axis=-1, keepdims=True)
    chances = exponent / totals
    chances_low = chances.astype(LOW)
    mixture = jnp.einsum("hqk,khd->qhd", chances_low, values, preferred_element_type=WIDE)
    mixture = mixture.reshape(length, share).astype(LOW)

    def block_of(array, k):
        return array[k * places_here : (k + 1) * places_here]

    branch = ring_sum([product(block_of(mixture, k), weight_out) for k in range(ranks)])
    hidden = own + branch + bias_out

    second_value, second_normal, second_inverse = normalize_parts(hidden, gain_two, shift_two)
    seconds = ring_gather(second_value.astype(LOW))
    upwards = [product(block, weight_up) + bias_up_here for block in seconds]
    activated = [jax.nn.gelu(block, approximate=True).astype(LOW) for block in upwards]
    dense_parts = [product(block, weight_down) for block in activated]

    reward_parts = [jnp.sum(part * reward_wide, axis=-1) for part in dense_parts]
    reward_parts[0] = reward_parts[0] + jnp.sum((hidden + bias_down) * reward_wide, axis=-1)
    rewards_all = lax.psum(to_ring(jnp.stack(reward_parts)), "seq")
    scored = (marks[:, 2] * (marks[:, 0] > 0)).astype(WIDE)
    error_all = scored * (jax.nn.sigmoid(rewards_all) - marks[:, 1].astype(WIDE)) / all_rows
    error_ring = to_ring(error_all)
    rewards = lax.dynamic_index_in_dim(rewards_all, rank, 0, keepdims=False)
    cotangents = ring_gather(cotangent[0])
    result_grads = [
        block.astype(WIDE) + error_ring[k][:, None] * reward_wide
        for k, block in enumerate(cotangents)
    ]
    dense_lows = [block.astype(LOW) for block in result_grads]
    result_grad = result_grads[0]
    result = hidden + ring_sum(dense_parts) + bias_down
    reward_weight_gradient = jnp.sum(error_ring[0][:, None] * result, axis=0)
    down_bias_gradient = jnp.sum(dense_lows[0].astype(WIDE), axis=0)

    upward_lows = []
    for k in range(ranks):
        _, pull = jax.vjp(partial(jax.nn.gelu, approximate=True), upwards[k])
        upward_lows.append(pull(against_rows(dense_lows[k], weight_down))[0].astype(LOW))
    second_grad = ring_sum([against_rows(block, weight_up) for block in upward_lows])
    activated_all = jnp.concatenate(activated)
    upward_all = jnp.concatenate(upward_lows)
    down_weight_gradient = scatter_groups(inner_rows(activated_all, jnp.concatenate(dense_lows)))
    up_weight_gradient = scatter_groups(inner_rows(jnp.concatenate(seconds), upward_all))
    up_weight_gradient = swap_ranks(
        up_weight_gradient.reshape(ranks, rows_in, groups * hidden_here)
    )
    up_weight_gradient = (
        up_weight_gradient.reshape(ranks, rows_in, groups, hidden_here)
        .transpose(1, 2, 0, 3)
        .reshape(up_weight.shape)
    )
    up_bias_gradient = jnp.sum(upward_all.astype(WIDE), axis=0)
    dense_gain_gradient = jnp.sum(second_grad * second_normal, axis=0)
    dense_shift_gradient = jnp.sum(second_grad, axis=0)
    hidden_grad = result_grad + normalize_back(second_grad, second_normal, second_inverse, gain_two)

    branch_low = hidden_grad.astype(LOW)
    branch_lows = ring_gather(branch_low)
    output_bias_gradient = jnp.sum(branch_low.astype(WIDE), axis=0)
    mixture_grad = jnp.concatenate([against_rows(block, weight_out) for block in branch_lows])
    mixture_grad = mixture_grad.astype(LOW)
    project_out_gradient = out_scatter(
        inner_rows(mixture, jnp.concatenate(branch_lows)), project_out.shape[0]
    )
    grad_heads = heads(mixture_grad)
    chance_grad = jnp.einsum("qhd,khd->hqk", grad_heads, values, preferred_element_type=WIDE)
    weighted = jnp.sum(chances * chance_grad, axis=-1, keepdims=True)
    score_grad = (chances * (chance_grad - weighted)).astype(LOW)
    query_grad = jnp.einsum("hqk,khd->qhd", score_grad, keys, preferred_element_type=WIDE)
    key_grad = jnp.einsum("hqk,qhd->khd", score_grad, queries, preferred_element_type=WIDE)
    value_grad = jnp.einsum("hqk,qhd->khd", chances_low, grad_heads, preferred_element_type=WIDE)
    projected_grad = jnp.concatenate(
        [
            (query_grad * score_scale).reshape(length, share).astype(LOW),
            (key_grad * score_scale).reshape(length, share).astype(LOW),
            value_grad.reshape(length, share).astype(LOW),
        ],
        axis=1,
    )
    first_grad = ring_sum(
        [against_rows(block_of(projected_grad, k), weight_in) for k in range(ranks)]
    )
    project_in_gradient = scatter_groups(inner_rows(first_low, projected_grad))
    project_in_gradient = swap_ranks(project_in_gradient.reshape(ranks, rows_in, 3 * share))
    project_in_gradient = project_in_gradient.reshape(ranks, rows_in, 3, heads_here, head_width)
    project_in_gradient = jnp.concatenate(
        [
            heads_from_rank(
                project_in_gradient[:, :, which].transpose(0, 2, 1, 3).reshape(ranks, -1)
            )
            .reshape(HEADS, rows_in, head_width)
            .transpose(1, 0, 2)
            .reshape(rows_in, width)
            for which in range(3)
        ],
        axis=1,
    )
    bias_sums = jnp.sum(projected_grad.astype(WIDE), axis=0)

    def place_heads(vector):
        table = jnp.zeros((ranks, share), WIDE)
        return heads_from_rank(
            lax.dynamic_update_index_in_dim(table, vector, rank, 0)
        ).reshape(-1)

    project_bias_gradient = jnp.concatenate(
        [place_heads(bias_sums[:share]), place_heads(bias_sums[2 * share :])]
    )
    up_bias_gradient = lax.dynamic_update_index_in_dim(
        jnp.zeros((groups, ranks, hidden_here), WIDE),
        up_bias_gradient.reshape(groups, hidden_here),
        rank,
        1,
    ).reshape(-1)
    attend_gain_gradient = jnp.sum(first_grad * first_normal, axis=0)
    attend_shift_gradient = jnp.sum(first_grad, axis=0)
    inputs_gradient = hidden_grad + normalize_back(
        first_grad, first_normal, first_inverse, gain_one
    )
    sums = (
        attend_gain_gradient,
        attend_shift_gradient,
        project_bias_gradient,
        output_bias_gradient,
        dense_gain_gradient,
        dense_shift_gradient,
        up_bias_gradient,
        down_bias_gradient,
        reward_weight_gradient,
    )
    table = jnp.concatenate([vector.reshape(groups * ranks, -1) for vector in sums], axis=1)
    summed = lax.psum_scatter(table, EVERY, scatter_dimension=0, tiled=True)[0]
    parts = []
    start = 0
    for size in sizes:
        parts.append(summed[start : start + size])
        start += size
    return (
        result.astype(LOW)[None],
        rewards[None],
        inputs_gradient[None],
        parts[0],
        parts[1],
        project_in_gradient.astype(WIDE),
        parts[2],
        project_out_gradient.astype(WIDE),
        parts[3],
        parts[4],
        parts[5],
        up_weight_gradient.astype(WIDE),
        parts[6],
        down_weight_gradient.astype(WIDE),
        parts[7],
        parts[8],
    )


def solution(mesh):
    row = P("dp", "seq")
    wide_row = P("dp", "seq", None)
    vector = P(("dp", "seq"))
    matrix = P(("dp", "seq"), None)
    in_specs = (
        wide_row,
        wide_row,
        row,
        row,
        row,
        vector,
        vector,
        matrix,
        vector,
        matrix,
        vector,
        vector,
        vector,
        matrix,
        vector,
        matrix,
        vector,
        vector,
    )
    out_specs = (
        wide_row,
        row,
        wide_row,
        vector,
        vector,
        matrix,
        vector,
        matrix,
        vector,
        vector,
        vector,
        matrix,
        vector,
        matrix,
        vector,
        vector,
    )
    return jax.shard_map(
        spread_path, mesh=mesh, in_specs=in_specs, out_specs=out_specs, check_vma=False
    )
```

```python
from functools import partial

import jax
import jax.numpy as jnp
from jax import lax
from jax.experimental import pallas as pl
from jax.experimental.pallas import tpu as pltpu
from jax.sharding import PartitionSpec as P

HEADS = 16
EPSILON = 1e-05
MASKED = -1e30
LOW = jnp.bfloat16
WIDE = jnp.float32
EVERY = ("dp", "seq")


def product(left, right):
    return jnp.dot(left, right, preferred_element_type=WIDE)


def inner_rows(left, right):
    return jnp.einsum("ta,tb->ab", left, right, preferred_element_type=WIDE)


def against_rows(left, right):
    return jnp.einsum("tb,ab->ta", left, right, preferred_element_type=WIDE)


def normalize_parts(field, gain, shift):
    center = field - jnp.mean(field, axis=-1, keepdims=True)
    spread = jnp.mean(center * center, axis=-1, keepdims=True)
    inverse = lax.rsqrt(spread + EPSILON)
    normal = center * inverse
    return (normal * gain + shift, normal, inverse)


def normalize_back(upstream, normal, inverse, gain):
    scaled = upstream * gain
    mean_scaled = jnp.mean(scaled, axis=-1, keepdims=True)
    mean_cross = jnp.mean(scaled * normal, axis=-1, keepdims=True)
    return inverse * (scaled - mean_scaled - normal * mean_cross)


def ring_next():
    size = lax.axis_size("seq")
    return [(place, (place + 1) % size) for place in range(size)]


def after(value, done):
    return lax.optimization_barrier((value, tuple(done)))[0]


class Task:
    def __init__(self, stages, *operands):
        self.gate = ()
        self.result = None
        self.stages = stages(self, *operands)

    def go(self, gate=()):
        self.gate = tuple(gate)
        return list(next(self.stages, []))

    def finish(self):
        for _ in self.stages:
            pass
        return self.result


def idle(gate):
    return []


def ring_gather(block, flights=(idle,) * 3, use=None, plan=()):
    blocks, results = [block], []
    for k in range(lax.axis_size("seq") - 1):
        moved = lax.ppermute(block, "seq", ring_next())
        done = []
        if use is not None:
            for _ in range(plan[k]):
                results.append(use(len(results), blocks[len(results)]))
                done += jax.tree.leaves(results[-1])
        done += flights[k]((block,))
        block = after(moved, done) if done else moved
        blocks.append(block)
    if use is None:
        return blocks
    while len(results) < len(blocks):
        results.append(use(len(results), blocks[len(results)]))
    return blocks, results


def ring_sum(part, flights=(idle,) * 3):
    total = part(1, ())
    for step, k in enumerate(list(range(2, lax.axis_size("seq"))) + [0]):
        sent = total.astype(LOW)
        moved = lax.ppermute(sent, "seq", ring_next())
        term = part(k, (sent,))
        total = after(moved, [term] + flights[step]((sent,))).astype(WIDE) + term
    return total


def ring_gather_task(task, block):
    task.result = [block]
    for _ in range(lax.axis_size("seq") - 1):
        moved = lax.ppermute(task.result[-1], "seq", ring_next())
        task.result.append(after(moved, task.gate))
        yield [moved]


def ring_sum_task(task, parts):
    total = parts[1]
    for part in parts[2:] + parts[:1]:
        moved = lax.ppermute(total.astype(LOW), "seq", ring_next())
        total = after(moved, task.gate).astype(WIDE) + part
        yield [moved]
    task.result = total


def deal_kernel(pieces, wide, riders, me_ref, from_ref, *refs):
    rider_refs, to_refs, packed = refs[:riders], refs[riders:-1], refs[-1]
    ranks = len(to_refs)
    columns = from_ref.shape[1] // ranks
    if riders:
        packed[...] = jnp.zeros_like(packed)
        row = 0
        for rider_ref in rider_refs:
            lines, width = rider_ref.shape
            packed[row : row + lines, :width] = rider_ref[...].astype(WIDE)
            row += lines
    for shift, to_ref in enumerate(to_refs):
        to = lax.rem(me_ref[0] + shift, ranks)
        for place in range(columns // wide):
            start = pl.multiple_of(pieces(to, place) * wide, wide)
            to_ref[:, place * wide : (place + 1) * wide] = from_ref[:, pl.ds(start, wide)]
        if riders:
            to_ref[:, columns:] = packed[...].astype(to_ref.dtype)


def deal(matrix, pieces, wide, riders=()):
    ranks, me = lax.axis_size("seq"), lax.axis_index("seq")
    rows, columns = matrix.shape
    if wide % 128 == 0:
        each = columns // ranks + (128 if riders else 0)
        return pl.pallas_call(
            partial(deal_kernel, pieces, wide, len(riders)),
            out_shape=[jax.ShapeDtypeStruct((rows, each), matrix.dtype)] * ranks,
            grid_spec=pltpu.PrefetchScalarGridSpec(
                num_scalar_prefetch=1,
                grid=(1,),
                in_specs=[pl.BlockSpec((rows, columns), lambda i, me: (0, 0))]
                + [pl.BlockSpec(rider.shape, lambda i, me: (0, 0)) for rider in riders],
                out_specs=[pl.BlockSpec((rows, each), lambda i, me: (0, 0))] * ranks,
                scratch_shapes=[pltpu.VMEM((rows, 128), WIDE)],
            ),
            name="deal",
        )(me[None], matrix, *riders)
    dealt = jnp.stack(
        [
            jnp.concatenate(
                [
                    matrix[:, pieces(to, place) * wide :][:, :wide]
                    for place in range(columns // ranks // wide)
                ],
                axis=1,
            )
            for to in range(ranks)
        ]
    )
    return [
        lax.dynamic_index_in_dim(dealt, (me + shift) % ranks, 0, keepdims=False)
        for shift in range(ranks)
    ]


def collect_kernel(pieces, wide, me_ref, *refs):
    from_refs, to_ref = refs[:-1], refs[-1]
    ranks = len(from_refs)
    for shift, from_ref in enumerate(from_refs):
        source = lax.rem(me_ref[0] + ranks - shift, ranks)
        for place in range(from_ref.shape[1] // wide):
            start = pl.multiple_of(pieces(source, place) * wide, wide)
            to_ref[:, pl.ds(start, wide)] = from_ref[:, place * wide : (place + 1) * wide].astype(
                to_ref.dtype
            )


def collect(blocks, pieces, wide):
    ranks, me = lax.axis_size("seq"), lax.axis_index("seq")
    rows, columns = blocks[0].shape
    if wide % 128 == 0:
        return pl.pallas_call(
            partial(collect_kernel, pieces, wide),
            out_shape=jax.ShapeDtypeStruct((rows, columns * ranks), WIDE),
            grid_spec=pltpu.PrefetchScalarGridSpec(
                num_scalar_prefetch=1,
                grid=(1,),
                in_specs=[pl.BlockSpec((rows, columns), lambda i, me: (0, 0))] * ranks,
                out_specs=pl.BlockSpec((rows, columns * ranks), lambda i, me: (0, 0)),
            ),
            name="collect",
        )(me[None], *blocks)
    held = by_number(blocks)
    found = {
        pieces(to, place): held[to, :, place * wide : (place + 1) * wide]
        for to in range(ranks)
        for place in range(columns // wide)
    }
    return jnp.concatenate([found[piece] for piece in sorted(found)], axis=1).astype(WIDE)


def place_kernel(sources, to_row_ref, *refs):
    from_refs, (to_ref, held, in_sem, out_sem) = refs[:-4], refs[-4:]
    loads, stores = [], []
    at = 0
    for number, (array, row, rows) in enumerate(sources):
        start = pl.multiple_of(to_row_ref[number], rows)
        piece = held.at[pl.ds(at, rows)]
        loads.append(
            pltpu.make_async_copy(from_refs[array].at[pl.ds(row, rows)], piece, in_sem.at[number])
        )
        stores.append(
            pltpu.make_async_copy(piece, to_ref.at[pl.ds(start, rows)], out_sem.at[number])
        )
        at += rows
    for load in loads:
        load.start()
    for load, store in zip(loads, stores):
        load.wait()
        store.start()
    for store in stores:
        store.wait()


def place_rows(arrays, sources, to_rows):
    total, width = sum(rows for _, _, rows in sources), arrays[0].shape[1]
    count = len(sources)
    if all(rows % 16 == 0 for _, _, rows in sources):
        return pl.pallas_call(
            partial(place_kernel, sources),
            out_shape=jax.ShapeDtypeStruct((total, width), arrays[0].dtype),
            grid_spec=pltpu.PrefetchScalarGridSpec(
                num_scalar_prefetch=1,
                grid=(1,),
                in_specs=[pl.BlockSpec(memory_space=pl.ANY)] * len(arrays),
                out_specs=pl.BlockSpec(memory_space=pl.ANY),
                scratch_shapes=[
                    pltpu.VMEM((total, width), arrays[0].dtype),
                    pltpu.SemaphoreType.DMA((count,)),
                    pltpu.SemaphoreType.DMA((count,)),
                ],
            ),
            compiler_params=pltpu.CompilerParams(
                vmem_limit_bytes=total * width * 2 + 4 * 2**20
            ),
            name="place_rows",
        )(to_rows, *arrays)
    whole = jnp.zeros((total, width), arrays[0].dtype)
    for number, (array, row, rows) in enumerate(sources):
        whole = lax.dynamic_update_slice_in_dim(
            whole, arrays[array][row : row + rows], to_rows[number], 0
        )
    return whole


def to_ring(table):
    size = lax.axis_size("seq")
    me = lax.axis_index("seq")
    return jnp.stack(
        [lax.dynamic_index_in_dim(table, (me - k) % size, 0, keepdims=False) for k in range(size)]
    )


def head_of(rank, place):
    groups, ranks = lax.axis_size("dp"), lax.axis_size("seq")
    blocks = groups * ranks // HEADS
    if blocks <= ranks:
        held = groups // blocks
        return (rank % blocks * held + place) * (ranks // blocks) + rank // blocks
    return place * ranks + rank


def heads_of():
    ranks = lax.axis_size("seq")
    return [[head_of(rank, place) for place in range(HEADS // ranks)] for rank in range(ranks)]


def head_pieces(rank, place):
    held = HEADS // lax.axis_size("seq")
    return place // held * HEADS + head_of(rank, place % held)


def hidden_pieces(rank, place):
    return place * lax.axis_size("seq") + rank


def own_heads():
    numbers = jnp.array(heads_of())
    mine = lax.dynamic_index_in_dim(numbers, lax.axis_index("seq"), 0, keepdims=False)
    return (mine[:, None] == jnp.arange(HEADS)[None, :]).astype(WIDE)


def exact(left, right):
    return jnp.dot(left, right, precision=lax.Precision.HIGHEST, preferred_element_type=WIDE)


def out_route():
    groups, ranks = lax.axis_size("dp"), lax.axis_size("seq")
    blocks = groups * ranks // HEADS
    route = []
    for group in range(groups):
        for rank in range(ranks):
            if blocks <= ranks:
                held = groups // blocks
                high, low = divmod(group, held)
                pair, part = divmod(rank, blocks)
                target = (part * held + low, pair * blocks + high)
            else:
                span = blocks // ranks
                head, extra = divmod(group, span)
                high, low = divmod(head, ranks)
                target = ((high * ranks + rank) * span + extra, low)
            route.append((group * ranks + rank, target[0] * ranks + target[1]))
    return route


def out_parts():
    groups, ranks = lax.axis_size("dp"), lax.axis_size("seq")
    blocks = groups * ranks // HEADS
    if blocks <= ranks:
        return ((blocks, groups // blocks), (1, 0))
    return ((HEADS // ranks, ranks, blocks // ranks), (0, 2, 1))


def out_gather(moved):
    whole = lax.all_gather(moved, "dp", axis=0, tiled=False)
    split, order = out_parts()
    tail = tuple(range(len(split), len(split) + 2))
    return whole.reshape(split + moved.shape).transpose(order + tail).reshape(-1, moved.shape[1])


def gather_groups(block):
    return lax.all_gather(block, "dp", axis=0, tiled=True)


def swap_bit(block, axis, bit):
    return lax.ppermute(
        block, axis, [(place, place ^ (1 << bit)) for place in range(lax.axis_size(axis))]
    )


def bits_of(axis):
    return range(lax.axis_size(axis).bit_length() - 1)


def pair_kernel(lefts, rights, kept, me_ref, *refs):
    left_refs, right_refs, rest = refs[:lefts], refs[lefts : lefts + rights], refs[lefts + rights :]
    left, right = joined(left_refs), joined(right_refs)
    total = lax.dot_general(left, right, (((0,), (0,)), ((), ())), preferred_element_type=WIDE)
    if not kept:
        rest[0][...] = total.astype(LOW)
        return
    total = (total + rest[0][...].astype(WIDE)).astype(LOW)
    half = total.shape[1] // 2
    for number in range(4):

        @pl.when(pl.program_id(0) == number)
        def _():
            rest[1 + number][...] = total[:, :half]
            rest[5 + number][...] = total[:, half:]


def pair_product(lefts, rights, rows, got=None):
    groups, me = lax.axis_size("dp"), lax.axis_index("dp")
    pairs, width = groups // 2, rights[0].shape[1]
    kept = got is not None

    def left_block(number, me):
        side = lax.rem(me[0], 2)
        return (0, (me[0] // 2 ^ number) * 2 + (side if kept else 1 - side))

    in_specs = [pl.BlockSpec((left.shape[0], rows), left_block) for left in lefts]
    once = pl.Buffered(1)
    in_specs += [
        pl.BlockSpec(right.shape, lambda number, me: (0, 0), pipeline_mode=once) for right in rights
    ]
    block = pl.BlockSpec((rows, width), lambda number, me: (number, 0))
    if kept:
        in_specs.append(block)
        shape = (rows, width // 2)
        out_specs = [pl.BlockSpec(shape, lambda number, me: (0, 0), pipeline_mode=once)] * (2 * pairs)
        out_shape = [pltpu.HBM(shape, LOW)] * (2 * pairs)
    else:
        out_specs = block
        out_shape = pltpu.HBM((pairs * rows, width), LOW)
    return pl.pallas_call(
        partial(pair_kernel, len(lefts), len(rights), kept),
        out_shape=out_shape,
        grid_spec=pltpu.PrefetchScalarGridSpec(
            num_scalar_prefetch=1, grid=(pairs,), in_specs=in_specs, out_specs=out_specs
        ),
        compiler_params=pltpu.CompilerParams(vmem_limit_bytes=18 * 2**20),
        cost_estimate=pl.CostEstimate(
            flops=4 * pairs * rows * width * sum(left.shape[0] for left in lefts),
            bytes_accessed=4 * pairs * rows * width,
            transcendentals=0,
        ),
        name="pair_product",
    )(me[None], *lefts, *rights, *([got] if kept else []))


GELU_SCALE = (2 / jnp.pi) ** 0.5
GELU_CUBE = 0.044715
PARAMETERS = dict(vmem_limit_bytes=16 * 2**20)


def gelu_parts(value):
    square = value * value
    bent = jnp.tanh(GELU_SCALE * value * (1 + GELU_CUBE * square))
    slope = 0.5 * (1 + bent) + 0.5 * value * (1 - bent * bent) * GELU_SCALE * (
        1 + 3 * GELU_CUBE * square
    )
    return 0.5 * value * (1 + bent), slope


def whole_block(array):
    return pl.BlockSpec(array.shape, lambda number: (0, 0), pipeline_mode=pl.Buffered(1))


def column_block(rows, wide):
    return pl.BlockSpec((rows, wide), lambda number: (0, number))


def joined(refs):
    return jnp.concatenate([ref[...] for ref in refs])


def estimate(rows, depth, width):
    return pl.CostEstimate(
        flops=4 * rows * depth * width, bytes_accessed=2 * depth * width, transcendentals=0
    )


def project_kernel(left_ref, weight_ref, bias_ref, to_ref):
    total = jnp.dot(left_ref[...], weight_ref[...], preferred_element_type=WIDE)
    to_ref[...] = (total + bias_ref[...]).astype(to_ref.dtype)


def project(left, weight, bias):
    (rows, depth), width, wide = left.shape, bias.shape[0], 256
    return pl.pallas_call(
        project_kernel,
        out_shape=jax.ShapeDtypeStruct((rows, width), LOW),
        grid=(width // wide,),
        in_specs=[whole_block(left), column_block(depth, wide), column_block(1, wide)],
        out_specs=column_block(rows, wide),
        compiler_params=pltpu.CompilerParams(**PARAMETERS),
        cost_estimate=estimate(rows, depth, width),
        name="project",
    )(left, weight, bias[None])


def upward_kernel(left_ref, weight_ref, bias_ref, upward_ref, active_ref):
    total = jnp.dot(left_ref[...], weight_ref[...], preferred_element_type=WIDE)
    total = total + bias_ref[...]
    upward_ref[...] = total
    active_ref[...] = gelu_parts(total)[0].astype(LOW)


def upward_product(left, weight, bias):
    (rows, depth), width, wide = left.shape, weight.shape[1], 256
    return pl.pallas_call(
        upward_kernel,
        out_shape=[
            jax.ShapeDtypeStruct((rows, width), WIDE),
            jax.ShapeDtypeStruct((rows, width), LOW),
        ],
        grid=(width // wide,),
        in_specs=[whole_block(left), column_block(depth, wide), column_block(1, wide)],
        out_specs=[column_block(rows, wide)] * 2,
        compiler_params=pltpu.CompilerParams(**PARAMETERS),
        cost_estimate=estimate(rows, depth, width),
        name="upward_product",
    )(left, weight, bias[None])


def dense_kernel(lefts, *refs):
    weight_ref, reward_ref, to_ref, reward_to_ref = refs[lefts:]
    total = jnp.dot(joined(refs[:lefts]), weight_ref[...], preferred_element_type=WIDE)
    to_ref[...] = total
    scaled = total * reward_ref[...]
    part = scaled[:, :128]
    for start in range(128, scaled.shape[1], 128):
        part = part + scaled[:, start : start + 128]

    @pl.when(pl.program_id(0) == 0)
    def _():
        reward_to_ref[...] = part

    @pl.when(pl.program_id(0) > 0)
    def _():
        reward_to_ref[...] += part


def dense_product(lefts, weight, reward):
    (depth, width), wide = weight.shape, 256
    rows = sum(left.shape[0] for left in lefts)
    return pl.pallas_call(
        partial(dense_kernel, len(lefts)),
        out_shape=[
            pltpu.HBM((rows, width), WIDE),
            jax.ShapeDtypeStruct((rows, 128), WIDE),
        ],
        grid=(width // wide,),
        in_specs=[whole_block(left) for left in lefts]
        + [column_block(depth, wide), column_block(1, wide)],
        out_specs=[column_block(rows, wide), pl.BlockSpec((rows, 128), lambda number: (0, 0))],
        compiler_params=pltpu.CompilerParams(**PARAMETERS),
        cost_estimate=estimate(rows, depth, width),
        name="dense_product",
    )(*lefts, weight, reward[None])


def against_dot(left, weight):
    return lax.dot_general(left, weight, (((1,), (1,)), ((), ())), preferred_element_type=WIDE)


def active_back_kernel(left_ref, weight_ref, upward_ref, to_ref):
    total = against_dot(left_ref[...], weight_ref[...])
    to_ref[...] = (total * gelu_parts(upward_ref[...])[1]).astype(LOW)


def active_back(left, weight, upward):
    (rows, depth), width, wide = left.shape, weight.shape[0], 256
    return pl.pallas_call(
        active_back_kernel,
        out_shape=jax.ShapeDtypeStruct((rows, width), LOW),
        grid=(width // wide,),
        in_specs=[
            whole_block(left),
            pl.BlockSpec((wide, depth), lambda number: (number, 0)),
            column_block(rows, wide),
        ],
        out_specs=column_block(rows, wide),
        compiler_params=pltpu.CompilerParams(**PARAMETERS),
        cost_estimate=estimate(rows, depth, width),
        name="active_back",
    )(left, weight, upward)


def against_kernel(left_ref, weight_ref, to_ref):
    to_ref[...] = against_dot(left_ref[...], weight_ref[...])


def against(left, weight):
    (rows, depth), width, wide = left.shape, weight.shape[0], 256
    return pl.pallas_call(
        against_kernel,
        out_shape=jax.ShapeDtypeStruct((rows, width), WIDE),
        grid=(width // wide,),
        in_specs=[whole_block(left), pl.BlockSpec((wide, depth), lambda number: (number, 0))],
        out_specs=column_block(rows, wide),
        compiler_params=pltpu.CompilerParams(**PARAMETERS),
        cost_estimate=estimate(rows, depth, width),
        name="against",
    )(left, weight)


def against_sums_kernel(left_ref, weight_ref, normal_ref, to_ref, sums_ref):
    total = against_dot(left_ref[...], weight_ref[...])
    to_ref[...] = total
    gain = jnp.sum(total * normal_ref[...], axis=0, keepdims=True)
    shift = jnp.sum(total, axis=0, keepdims=True)
    sums_ref[...] = jnp.concatenate([gain, shift, jnp.zeros((6, gain.shape[1]), WIDE)])


def against_sums(left, weight, normal):
    (rows, depth), width, wide = left.shape, weight.shape[0], 256
    return pl.pallas_call(
        against_sums_kernel,
        out_shape=[
            jax.ShapeDtypeStruct((rows, width), WIDE),
            jax.ShapeDtypeStruct((8, width), WIDE),
        ],
        grid=(width // wide,),
        in_specs=[
            whole_block(left),
            pl.BlockSpec((wide, depth), lambda number: (number, 0)),
            column_block(rows, wide),
        ],
        out_specs=[column_block(rows, wide), column_block(8, wide)],
        compiler_params=pltpu.CompilerParams(**PARAMETERS),
        cost_estimate=estimate(rows, depth, width),
        name="against_sums",
    )(left, weight, normal)


def rows_kernel(lefts, *refs):
    left, right = joined(refs[:lefts]), joined(refs[lefts:-1])
    total = lax.dot_general(left, right, (((0,), (0,)), ((), ())), preferred_element_type=WIDE)
    refs[-1][...] = total.astype(LOW)


def rows_product(lefts, rights):
    rows, width = lefts[0].shape[1], rights[0].shape[1]
    wide = 256
    if rows % wide:
        return inner_rows(jnp.concatenate(lefts), jnp.concatenate(rights)).astype(LOW)
    return pl.pallas_call(
        partial(rows_kernel, len(lefts)),
        out_shape=pltpu.HBM((rows, width), LOW),
        grid=(rows // wide,),
        in_specs=[pl.BlockSpec((left.shape[0], wide), lambda number: (0, number)) for left in lefts]
        + [
            pl.BlockSpec(right.shape, lambda number: (0, 0), pipeline_mode=pl.Buffered(1))
            for right in rights
        ],
        out_specs=pl.BlockSpec((wide, width), lambda number: (number, 0)),
        compiler_params=pltpu.CompilerParams(vmem_limit_bytes=16 * 2**20),
        cost_estimate=pl.CostEstimate(
            flops=4 * rows * width * sum(left.shape[0] for left in lefts),
            bytes_accessed=4 * rows * width,
            transcendentals=0,
        ),
        name="rows_product",
    )(*lefts, *rights)


def scatter_product(task, lefts, rights, rows):
    groups, me = lax.axis_size("dp"), lax.axis_index("dp")
    width = rights[0].shape[1]
    half = width // 2
    bits = list(bits_of("dp"))[1:]
    direct = rows % 128 == 0 and len(bits) == 2
    if direct:
        lefts, rights = after((lefts, rights), task.gate)
        sent = pair_product(lefts, rights, rows)
    else:
        whole = inner_rows(jnp.concatenate(after(lefts, task.gate)), jnp.concatenate(rights))
        whole = whole.astype(LOW).reshape(groups, rows, width)
        sent, kept = (
            jnp.concatenate(
                [
                    lax.dynamic_index_in_dim(whole, me ^ (2 * number + side), 0, keepdims=False)
                    for number in range(groups // 2)
                ]
            )
            for side in (1, 0)
        )
    yield [sent]
    got = swap_bit(sent, "dp", 0)
    yield [got]
    got = after(got, task.gate)
    if direct:
        table = pair_product(lefts, rights, rows, got)
        pieces = [list(table[: groups // 2]), list(table[groups // 2 :])]
    else:
        table = (kept.astype(WIDE) + got.astype(WIDE)).astype(LOW).reshape(-1, rows, width)
        pieces = [
            [table[number, :, piece * half : (piece + 1) * half] for number in range(groups // 2)]
            for piece in range(2)
        ]
    yield pieces[0] + pieces[1]
    done = [{}, {}]
    orders = [list(range(len(bits))), list(range(len(bits)))[::-1]]
    held = [list(range(groups // 2)), list(range(groups // 2))]
    late = [{}, {}]
    for step in range(len(bits)):
        soon = []
        for piece, order in enumerate(orders):
            bit = 1 << order[step]
            onward = 0 if step + 1 == len(bits) else 1 << order[step + 1]
            keep = [number for number in held[piece] if not number & bit]
            for number in keep:
                value = pieces[piece][number | bit]
                got = swap_bit(value.astype(LOW), "dp", bits[order[step]])
                if number & onward or not onward:
                    soon.append(got)
                    got = after(got, task.gate)
                    pieces[piece][number] = pieces[piece][number].astype(WIDE) + got.astype(WIDE)
                else:
                    late[piece].setdefault(number, []).append(got)
            held[piece] = keep
        yield soon
        if step + 1 < len(bits):
            yield [got for piece in range(2) for gots in late[piece].values() for got in gots]
        for piece in range(2):
            for number, gots in late[piece].items():
                for got in gots:
                    pieces[piece][number] = pieces[piece][number].astype(WIDE) + got.astype(WIDE)
            late[piece] = {}
    task.result = jnp.concatenate([pieces[0][0], pieces[1][0]], axis=1)


def scatter_groups(table):
    return lax.psum_scatter(table, "dp", scatter_dimension=0, tiled=True)


def out_product(left, right, rows):
    split, order = out_parts()
    count = left.shape[0]
    back = tuple(1 + order.index(axis) for axis in range(len(order)))
    moved = left.reshape((count,) + tuple(split[axis] for axis in order) + (rows,))
    moved = moved.transpose((0,) + back + (1 + len(split),)).reshape(count, -1)
    return inner_rows(moved, right).astype(LOW)


def rank_rows(table, rows):
    ranks, me = lax.axis_size("seq"), lax.axis_index("seq")
    return [
        lax.dynamic_slice_in_dim(table, (me + shift) % ranks * rows, rows, 0)
        for shift in range(ranks)
    ]


def swap_ranks(blocks):
    size = lax.axis_size("seq")
    return [blocks[0]] + [
        lax.ppermute(blocks[shift], "seq", [(place, (place + shift) % size) for place in range(size)])
        for shift in range(1, size)
    ]


def rows_by_rank(blocks):
    ranks, me = len(blocks), lax.axis_index("seq")
    rows = blocks[0].shape[0]
    return place_rows(
        blocks,
        [(number, 0, rows) for number in range(ranks)],
        (me + ranks - jnp.arange(ranks)) % ranks * rows,
    )


def by_number(blocks):
    return to_ring(jnp.stack(blocks))


def small_order():
    groups, ranks = lax.axis_size("dp"), lax.axis_size("seq")
    number = jnp.arange(groups * ranks)
    place = ((number // ranks) ^ lax.axis_index("dp")) * ranks + (
        (number % ranks) ^ lax.axis_index("seq")
    )
    return (place[:, None] == number[None, :]).astype(WIDE)


def scatter_small(table, done):
    table = jnp.dot(
        small_order().T, table, precision=lax.Precision.HIGHEST, preferred_element_type=WIDE
    )
    for axis in ("dp", "seq"):
        for bit in reversed(bits_of(axis)):
            half = table.shape[0] // 2
            table = table[:half] + swap_bit(table[half:], axis, bit)
        table = after(table, done)
    return table[0]


def sum_ranks(table):
    size = lax.axis_size("seq")
    total = table
    for shift in range(1, size):
        total = total + lax.ppermute(
            table, "seq", [(place, (place + shift) % size) for place in range(size)]
        )
    return total


def spread_path(
    inputs,
    cotangent,
    segments,
    labels,
    step_ends,
    attend_gain,
    attend_shift,
    project_in,
    project_bias,
    project_out,
    output_bias,
    dense_gain,
    dense_shift,
    up_weight,
    up_bias,
    down_weight,
    down_bias,
    reward_weight,
):
    groups, ranks = lax.axis_size("dp"), lax.axis_size("seq")
    rank = lax.axis_index("seq")
    rows_here, places_here, width = inputs.shape
    all_rows = rows_here * groups
    head_width = width // HEADS
    heads_here = HEADS // ranks
    share = heads_here * head_width
    rows_in = project_in.shape[0]
    hidden_here = down_weight.shape[0]
    length = ranks * places_here
    score_scale = head_width ** (-0.5)

    small = (
        attend_gain,
        attend_shift,
        project_bias,
        output_bias,
        dense_gain,
        dense_shift,
        up_bias,
        down_bias,
        reward_weight,
    )
    sizes = [vector.shape[0] for vector in small]
    riders = [vector.reshape(-(-vector.shape[0] // 128), -1) for vector in small]
    riders += [segments, labels, step_ends]
    out_moved = lax.ppermute(project_out, EVERY, out_route())
    weight_out = out_gather(out_moved)
    dealt_in = deal(project_in, head_pieces, head_width, riders)
    came_in = swap_ranks(dealt_in)
    rows_in_all = rows_by_rank(came_in)
    gathered = gather_groups(rows_in_all)
    inputs_ring = ring_gather(
        after(inputs[0], came_in), [idle, lambda gate: [weight_out], idle]
    )
    dealt_up = deal(after(up_weight, [rows_in_all]), hidden_pieces, hidden_here)
    came_up = swap_ranks(after(dealt_up, [inputs_ring[-1]]))
    riders = gathered[:, 3 * share :]
    riders = riders.reshape(groups * ranks, rows_in, 128).astype(WIDE)
    vectors = []
    row = 0
    for size in sizes + [places_here] * 3:
        lines = -(-size // 128)
        vectors.append(
            riders[:, row : row + lines].reshape(groups * ranks, -1)[:, :size].reshape(-1)
        )
        row += lines
    gain_one, shift_one, bias_in, bias_out, gain_two, shift_two, bias_up, bias_down, reward_wide = (
        vectors[: len(sizes)]
    )

    held = own_heads()
    bias_heads = exact(held, bias_in.reshape(2, HEADS, head_width).transpose(1, 0, 2).reshape(HEADS, -1))
    bias_heads = bias_heads.reshape(heads_here, 2, head_width)
    bias_full = jnp.concatenate(
        [bias_heads[:, 0].reshape(-1), jnp.zeros((share,), WIDE), bias_heads[:, 1].reshape(-1)]
    )
    bias_up_here = lax.dynamic_index_in_dim(
        bias_up.reshape(groups, ranks, hidden_here), rank, 1, keepdims=False
    ).reshape(-1)
    marks = jnp.stack(
        [
            lax.dynamic_index_in_dim(
                mark.reshape(groups, ranks, places_here), lax.axis_index("dp"), 0, keepdims=False
            )
            for mark in vectors[len(sizes) :]
        ],
        axis=1,
    )
    marks_ring = to_ring(marks)
    segments_ring = marks_ring[:, 0].reshape(-1)
    places_ring = to_ring(jnp.arange(length).reshape(ranks, places_here)).reshape(-1)

    own = inputs[0].astype(WIDE)
    firsts, first_normals = [], []
    for block in inputs_ring:
        value, normal, inverse = normalize_parts(block.astype(WIDE), gain_one, shift_one)
        if not firsts:
            first_inverse = inverse
        firsts.append(value.astype(LOW))
        first_normals.append(normal)
    first_low = jnp.concatenate(firsts)
    projected = project(first_low, gathered, bias_full)
    came_up, projected = lax.optimization_barrier((came_up, projected))
    rows_up_all = rows_by_rank(came_up)
    weight_up = gather_groups(rows_up_all)
    weight_down = gather_groups(after(down_weight, [rows_up_all]))

    def heads(block):
        return block.reshape(length, heads_here, head_width)

    queries, keys, values = (
        heads(projected[:, :share]),
        heads(projected[:, share : 2 * share]),
        heads(projected[:, 2 * share :]),
    )
    same = (segments_ring[None, :] == 0) | (segments_ring[None, :] == segments_ring[:, None])
    allowed = same & (places_ring[None, :] <= places_ring[:, None])
    scores = jnp.einsum("qhd,khd->hqk", queries, keys, preferred_element_type=WIDE) * score_scale
    scores = jnp.where(allowed[None], scores, MASKED)
    highest = jnp.max(scores, axis=-1, keepdims=True)
    exponent = jnp.exp(scores - highest)
    totals = jnp.sum(exponent, axis=-1, keepdims=True)
    chances = exponent / totals
    chances_low = chances.astype(LOW)
    mixture = jnp.einsum("hqk,khd->qhd", chances_low, values, preferred_element_type=WIDE)
    mixture = mixture.reshape(length, share).astype(LOW)

    def block_of(array, k):
        return array[k * places_here : (k + 1) * places_here]

    mixture_late = mixture
    branch = ring_sum(lambda k, gate: product(block_of(mixture, k), weight_out))
    hidden = own + branch + bias_out

    second_value, second_normal, second_inverse = normalize_parts(hidden, gain_two, shift_two)

    seconds, found = ring_gather(
        second_value.astype(LOW),
        use=lambda k, block: upward_product(block, weight_up, bias_up_here),
        plan=(1, 1, 1),
    )
    upwards, activated = map(list, zip(*found))
    cotangent_task = Task(ring_gather_task, after(cotangent[0], [seconds[-1]]))
    activated[-1] = after(activated[-1], cotangent_task.go())
    dense_all, reward_lanes = dense_product(activated, weight_down, reward_wide)
    dense_parts = [block_of(dense_all, k) for k in range(ranks)]
    reward_lanes = after(reward_lanes, cotangent_task.go())
    reward_parts = list(jnp.sum(reward_lanes, axis=-1).reshape(ranks, places_here))
    result_task = Task(ring_sum_task, dense_parts)

    reward_parts[0] = reward_parts[0] + jnp.sum((hidden + bias_down) * reward_wide, axis=-1)
    rewards_all = sum_ranks(to_ring(jnp.stack(reward_parts)))
    scored = marks[:, 2] * (marks[:, 0] > 0)
    error_all = scored * (jax.nn.sigmoid(rewards_all) - marks[:, 1]) / all_rows
    error_ring = to_ring(error_all)
    rewards = lax.dynamic_index_in_dim(rewards_all, rank, 0, keepdims=False)

    result_grads, dense_lows, upward_lows = [], [], [None] * ranks

    def dense_grad():
        k = len(result_grads)
        block = cotangent_task.result[k].astype(WIDE)
        result_grads.append(block + error_ring[k][:, None] * reward_wide)
        dense_lows.append(result_grads[-1].astype(LOW))

    def second_part(k, gate):
        while len(dense_lows) <= k:
            dense_grad()
        upward_lows[k] = active_back(after(dense_lows[k], gate), weight_down, upwards[k])
        return against(upward_lows[k], weight_up)

    reward_weight_gradient = jnp.sum(error_ring.reshape(-1)[:, None] * dense_all, axis=0)
    reward_weight_gradient += jnp.sum(error_ring[0][:, None] * (hidden + bias_down), axis=0)
    error_ring = after(error_ring, cotangent_task.go())
    down_table = None

    def down_start(gate):
        nonlocal down_table
        down_table = rows_product(after(activated, gate), dense_lows)
        return [down_table]

    second_grad = ring_sum(second_part, [idle, down_start, idle])
    down_weight_gradient = scatter_groups(down_table).astype(WIDE)
    result_grad = result_grads[0]
    down_bias_gradient = jnp.sum(dense_lows[0].astype(WIDE), axis=0)
    upward_all = jnp.concatenate(upward_lows)
    up_bias_gradient = jnp.sum(upward_all.astype(WIDE), axis=0)
    dense_gain_gradient = jnp.sum(second_grad * second_normal, axis=0)
    dense_shift_gradient = jnp.sum(second_grad, axis=0)
    hidden_grad = result_grad + normalize_back(second_grad, second_normal, second_inverse, gain_two)

    branch_low = hidden_grad.astype(LOW)
    up_task = Task(scatter_product, seconds, upward_lows, ranks * rows_in)
    branch_low = after(branch_low, up_task.go())
    output_bias_gradient = jnp.sum(branch_low.astype(WIDE), axis=0)
    up_bias_gradient = lax.dynamic_update_index_in_dim(
        jnp.zeros((groups, ranks, hidden_here), WIDE),
        up_bias_gradient.reshape(groups, hidden_here),
        rank,
        1,
    )

    def by_device(vectors):
        return jnp.concatenate([vector.reshape(groups * ranks, -1) for vector in vectors], axis=1)

    early = by_device(
        (
            output_bias_gradient,
            dense_gain_gradient,
            dense_shift_gradient,
            up_bias_gradient,
            down_bias_gradient,
            reward_weight_gradient,
        )
    )
    branch_lows = ring_gather(
        branch_low,
        [up_task.go, lambda gate: up_task.go(gate) + [early], up_task.go],
    )
    branch_lows[-1], early = lax.optimization_barrier((branch_lows[-1], early))
    branch_all = jnp.concatenate(branch_lows)
    mixture_grad = against_rows(branch_all, weight_out).astype(LOW)
    out_table = out_product(mixture_late, branch_all, project_out.shape[0])
    out_summed = scatter_groups(out_table)
    grad_heads = heads(mixture_grad)
    chance_grad = jnp.einsum("qhd,khd->hqk", grad_heads, values, preferred_element_type=WIDE)
    weighted = jnp.sum(chances * chance_grad, axis=-1, keepdims=True)
    score_grad = (chances * (chance_grad - weighted)).astype(LOW)
    score_grad = after(score_grad, result_task.go([mixture_grad]))
    query_grad = jnp.einsum("hqk,khd->qhd", score_grad, keys, preferred_element_type=WIDE)
    key_grad = jnp.einsum("hqk,qhd->khd", score_grad, queries, preferred_element_type=WIDE)
    value_grad = jnp.einsum("hqk,qhd->khd", chances_low, grad_heads, preferred_element_type=WIDE)
    projected_grad = jnp.concatenate(
        [
            (query_grad * score_scale).reshape(length, share).astype(LOW),
            (key_grad * score_scale).reshape(length, share).astype(LOW),
            value_grad.reshape(length, share).astype(LOW),
        ],
        axis=1,
    )
    in_task = Task(scatter_product, firsts, [projected_grad], ranks * rows_in)
    projected_grad = after(projected_grad, in_task.go() + result_task.go([score_grad]))
    first_sums = [None] * ranks

    def first_part(k, gate):
        block = after(block_of(projected_grad, k), gate)
        term, first_sums[k] = against_sums(block, gathered, first_normals[k])
        return term

    first_grad = ring_sum(
        first_part,
        [
            lambda gate: in_task.go(gate) + up_task.go(gate),
            lambda gate: in_task.go(gate) + up_task.go(gate),
            in_task.go,
        ],
    )
    came_up = swap_ranks(rank_rows(after(up_task.finish().astype(LOW), [first_grad]), rows_in))
    in_task.go([first_grad])
    in_task.go([first_grad])
    result_task.go([first_grad])
    result = hidden + result_task.finish() + bias_down
    result_low = result.astype(LOW)
    project_out_gradient = lax.ppermute(
        out_summed, EVERY, [(there, here) for here, there in out_route()]
    ).astype(WIDE)
    up_weight_gradient = collect(came_up, hidden_pieces, hidden_here)
    bias_sums = jnp.sum(projected_grad.astype(WIDE), axis=0)

    bias_heads = jnp.concatenate([bias_sums[:share], bias_sums[2 * share :]])
    bias_heads = bias_heads.reshape(2, heads_here, head_width)
    project_bias_gradient = jnp.concatenate(
        [exact(held.T, bias_heads[which]).reshape(-1) for which in range(2)]
    )
    attend_gain_gradient, attend_shift_gradient = sum(first_sums)[:2]
    inputs_gradient = hidden_grad + normalize_back(
        first_grad, first_normals[0], first_inverse, gain_one
    )
    late = by_device((attend_gain_gradient, attend_shift_gradient, project_bias_gradient))
    table = jnp.concatenate([late, early], axis=1)
    summed = scatter_small(table, came_up)
    in_summed = after(in_task.finish().astype(LOW), [summed] + came_up)
    came_in = swap_ranks(rank_rows(in_summed, rows_in))
    project_in_gradient = collect(came_in, head_pieces, head_width)
    parts = []
    start = 0
    for size in sizes:
        parts.append(summed[start : start + size])
        start += size
    return (
        result_low[None],
        rewards[None],
        inputs_gradient[None],
        parts[0],
        parts[1],
        project_in_gradient,
        parts[2],
        project_out_gradient,
        parts[3],
        parts[4],
        parts[5],
        up_weight_gradient,
        parts[6],
        down_weight_gradient,
        parts[7],
        parts[8],
    )


def solution(mesh):
    row = P("dp", "seq")
    wide_row = P("dp", "seq", None)
    vector = P(("dp", "seq"))
    matrix = P(("dp", "seq"), None)
    in_specs = (
        wide_row,
        wide_row,
        row,
        row,
        row,
        vector,
        vector,
        matrix,
        vector,
        matrix,
        vector,
        vector,
        vector,
        matrix,
        vector,
        matrix,
        vector,
        vector,
    )
    out_specs = (
        wide_row,
        row,
        wide_row,
        vector,
        vector,
        matrix,
        vector,
        matrix,
        vector,
        vector,
        vector,
        matrix,
        vector,
        matrix,
        vector,
        vector,
    )
    return jax.shard_map(
        spread_path, mesh=mesh, in_specs=in_specs, out_specs=out_specs, check_vma=False
    )
```

```python
from functools import partial

import jax
import jax.numpy as jnp
from jax import lax
from jax.experimental import pallas as pl
from jax.experimental.pallas import tpu as pltpu
from jax.sharding import PartitionSpec as P

HEADS = 16
EPSILON = 1e-05
MASKED = -1e30
LOW = jnp.bfloat16
WIDE = jnp.float32
EVERY = ("dp", "seq")


def product(left, right):
    return jnp.dot(left, right, preferred_element_type=WIDE)


def inner_rows(left, right):
    return jnp.einsum("ta,tb->ab", left, right, preferred_element_type=WIDE)


def against_rows(left, right):
    return jnp.einsum("tb,ab->ta", left, right, preferred_element_type=WIDE)


def normal_parts(field):
    center = field - jnp.mean(field, axis=-1, keepdims=True)
    spread = jnp.mean(center * center, axis=-1, keepdims=True)
    inverse = lax.rsqrt(spread + EPSILON)
    return center * inverse, inverse


def normalize_back(upstream, normal, inverse, gain):
    scaled = upstream * gain
    mean_scaled = jnp.mean(scaled, axis=-1, keepdims=True)
    mean_cross = jnp.mean(scaled * normal, axis=-1, keepdims=True)
    return inverse * (scaled - mean_scaled - normal * mean_cross)


def ring_next():
    size = lax.axis_size("seq")
    return [(place, (place + 1) % size) for place in range(size)]


def after(value, done):
    return lax.optimization_barrier((value, tuple(done)))[0]


def fence(steady, work, *operands):
    shapes = jax.eval_shape(work, *operands)
    return lax.cond(
        steady,
        work,
        lambda *_: jax.tree.map(lambda shape: jnp.zeros(shape.shape, shape.dtype), shapes),
        *operands,
    )


def idle(gate):
    return []


def pieces_of(block, cut):
    rows = block.shape[0] // cut
    return [block[piece * rows : (piece + 1) * rows] for piece in range(cut)]


def ring_move(halves):
    return [lax.ppermute(half, "seq", ring_next()) for half in halves]


def ring_gather(block, flights=(idle,) * 3, use=None, plan=(), cut=2):
    blocks, results = [pieces_of(block, cut)], []
    for k in range(lax.axis_size("seq") - 1):
        moved = ring_move(blocks[-1])
        done = []
        if use is not None:
            for _ in range(plan[k]):
                results.append(use(len(results), blocks[len(results)]))
                done += jax.tree.leaves(results[-1])
        done += flights[k](blocks[-1])
        if done:
            moved[-1] = after(moved[-1], done)
        blocks.append(moved)
    return blocks if use is None else (blocks, results)


def ring_sum(part, flights=(idle,) * 3, cut=2):
    size = lax.axis_size("seq")
    sent = pieces_of(part(1, ()).astype(LOW), cut)
    for step, k in enumerate(list(range(2, size)) + [0]):
        kind = LOW if step < size - 2 else WIDE
        moved = ring_move(sent)
        term = part(k, sent)
        done = [term] + flights[step](sent)
        total = []
        for piece, (came, own) in enumerate(zip(moved, pieces_of(term, cut))):
            came = after(came, total + (done if piece == cut - 1 else []))
            total.append((came.astype(WIDE) + own).astype(kind))
        sent = total
    return jnp.concatenate(sent) if cut > 1 else sent[0]


def ring_step(total, part):
    moved = lax.ppermute(total.astype(LOW), "seq", ring_next())
    return moved.astype(WIDE) + part.astype(WIDE)


def deal_kernel(pieces, wide, riders, me_ref, from_ref, *refs):
    rider_refs, to_refs, packed = refs[:riders], refs[riders:-1], refs[-1]
    ranks = len(to_refs)
    columns = from_ref.shape[1] // ranks
    if riders:
        packed[...] = jnp.zeros_like(packed)
        row = 0
        for rider_ref in rider_refs:
            lines, width = rider_ref.shape
            packed[row : row + lines, :width] = rider_ref[...].astype(WIDE)
            row += lines
    for shift, to_ref in enumerate(to_refs):
        to = lax.rem(me_ref[0] + shift, ranks)
        for place in range(columns // wide):
            start = pl.multiple_of(pieces(to, place) * wide, wide)
            to_ref[:, place * wide : (place + 1) * wide] = from_ref[:, pl.ds(start, wide)]
        if riders:
            to_ref[:, columns:] = packed[...].astype(to_ref.dtype)


def deal(matrix, pieces, wide, riders=()):
    ranks, me = lax.axis_size("seq"), lax.axis_index("seq")
    rows, columns = matrix.shape
    if wide % 128 == 0:
        each = columns // ranks + (128 if riders else 0)
        return pl.pallas_call(
            partial(deal_kernel, pieces, wide, len(riders)),
            out_shape=[jax.ShapeDtypeStruct((rows, each), matrix.dtype)] * ranks,
            grid_spec=pltpu.PrefetchScalarGridSpec(
                num_scalar_prefetch=1,
                grid=(1,),
                in_specs=[pl.BlockSpec((rows, columns), lambda i, me: (0, 0))]
                + [pl.BlockSpec(rider.shape, lambda i, me: (0, 0)) for rider in riders],
                out_specs=[pl.BlockSpec((rows, each), lambda i, me: (0, 0))] * ranks,
                scratch_shapes=[pltpu.VMEM((rows, 128), WIDE)],
            ),
            name="deal",
        )(me[None], matrix, *riders)
    dealt = jnp.stack(
        [
            jnp.concatenate(
                [
                    matrix[:, pieces(to, place) * wide :][:, :wide]
                    for place in range(columns // ranks // wide)
                ],
                axis=1,
            )
            for to in range(ranks)
        ]
    )
    return [
        lax.dynamic_index_in_dim(dealt, (me + shift) % ranks, 0, keepdims=False)
        for shift in range(ranks)
    ]


def collect_kernel(pieces, wide, me_ref, *refs):
    from_refs, to_ref = refs[:-1], refs[-1]
    ranks = len(from_refs)
    for shift, from_ref in enumerate(from_refs):
        source = lax.rem(me_ref[0] + ranks - shift, ranks)
        for place in range(from_ref.shape[1] // wide):
            start = pl.multiple_of(pieces(source, place) * wide, wide)
            to_ref[:, pl.ds(start, wide)] = from_ref[:, place * wide : (place + 1) * wide].astype(
                to_ref.dtype
            )


def collect(blocks, pieces, wide):
    ranks, me = lax.axis_size("seq"), lax.axis_index("seq")
    rows, columns = blocks[0].shape
    if wide % 128 == 0:
        return pl.pallas_call(
            partial(collect_kernel, pieces, wide),
            out_shape=jax.ShapeDtypeStruct((rows, columns * ranks), WIDE),
            grid_spec=pltpu.PrefetchScalarGridSpec(
                num_scalar_prefetch=1,
                grid=(1,),
                in_specs=[pl.BlockSpec((rows, columns), lambda i, me: (0, 0))] * ranks,
                out_specs=pl.BlockSpec((rows, columns * ranks), lambda i, me: (0, 0)),
            ),
            name="collect",
        )(me[None], *blocks)
    held = by_number(blocks)
    found = {
        pieces(to, place): held[to, :, place * wide : (place + 1) * wide]
        for to in range(ranks)
        for place in range(columns // wide)
    }
    return jnp.concatenate([found[piece] for piece in sorted(found)], axis=1).astype(WIDE)


def place_kernel(sources, to_row_ref, *refs):
    held, in_sem, out_sem = refs[-3:]
    from_refs, to_ref = refs[:-4], refs[-4]
    loads, stores = [], []
    at = 0
    for number, (array, row, rows, column, width, to_column) in enumerate(sources):
        start = pl.multiple_of(to_row_ref[number], rows)
        piece = held.at[pl.ds(at, rows), pl.ds(0, width)]
        source = from_refs[array].at[pl.ds(row, rows), pl.ds(column, width)]
        target = to_ref.at[pl.ds(start, rows), pl.ds(to_column, width)]
        loads.append(pltpu.make_async_copy(source, piece, in_sem.at[number]))
        stores.append(pltpu.make_async_copy(piece, target, out_sem.at[number]))
        at += rows
    for load in loads:
        load.start()
    for load, store in zip(loads, stores):
        load.wait()
        store.start()
    for store in stores:
        store.wait()


def place(arrays, sources, to_rows, shape):
    count = len(sources)
    wide = max(width for _, _, _, _, width, _ in sources)
    total = sum(rows for _, _, rows, _, _, _ in sources)
    return pl.pallas_call(
        partial(place_kernel, sources),
        out_shape=jax.ShapeDtypeStruct(shape, arrays[0].dtype),
        grid_spec=pltpu.PrefetchScalarGridSpec(
            num_scalar_prefetch=1,
            grid=(1,),
            in_specs=[pl.BlockSpec(memory_space=pl.ANY)] * len(arrays),
            out_specs=pl.BlockSpec(memory_space=pl.ANY),
            scratch_shapes=[
                pltpu.VMEM((total, wide), arrays[0].dtype),
                pltpu.SemaphoreType.DMA((count,)),
                pltpu.SemaphoreType.DMA((count,)),
            ],
        ),
        compiler_params=pltpu.CompilerParams(vmem_limit_bytes=total * wide * 2 + 4 * 2**20),
        name="place",
    )(to_rows, *arrays)


def to_ring(table):
    size = lax.axis_size("seq")
    me = lax.axis_index("seq")
    return jnp.stack(
        [lax.dynamic_index_in_dim(table, (me - k) % size, 0, keepdims=False) for k in range(size)]
    )


def head_of(rank, place):
    groups, ranks = lax.axis_size("dp"), lax.axis_size("seq")
    blocks = groups * ranks // HEADS
    if blocks <= ranks:
        held = groups // blocks
        return (rank % blocks * held + place) * (ranks // blocks) + rank // blocks
    return place * ranks + rank


def heads_of():
    ranks = lax.axis_size("seq")
    return [[head_of(rank, place) for place in range(HEADS // ranks)] for rank in range(ranks)]


def head_pieces(rank, place):
    held = HEADS // lax.axis_size("seq")
    return place // held * HEADS + head_of(rank, place % held)


def hidden_pieces(rank, place):
    return place * lax.axis_size("seq") + rank


def own_heads():
    numbers = jnp.array(heads_of())
    mine = lax.dynamic_index_in_dim(numbers, lax.axis_index("seq"), 0, keepdims=False)
    return (mine[:, None] == jnp.arange(HEADS)[None, :]).astype(WIDE)


def exact(left, right):
    return jnp.dot(left, right, precision=lax.Precision.HIGHEST, preferred_element_type=WIDE)


def out_route():
    groups, ranks = lax.axis_size("dp"), lax.axis_size("seq")
    blocks = groups * ranks // HEADS
    route = []
    for group in range(groups):
        for rank in range(ranks):
            if blocks <= ranks:
                held = groups // blocks
                high, low = divmod(group, held)
                pair, part = divmod(rank, blocks)
                target = (part * held + low, pair * blocks + high)
            else:
                span = blocks // ranks
                head, extra = divmod(group, span)
                high, low = divmod(head, ranks)
                target = ((high * ranks + rank) * span + extra, low)
            route.append((group * ranks + rank, target[0] * ranks + target[1]))
    return route


def out_parts():
    groups, ranks = lax.axis_size("dp"), lax.axis_size("seq")
    blocks = groups * ranks // HEADS
    if blocks <= ranks:
        return ((blocks, groups // blocks), (1, 0))
    return ((HEADS // ranks, ranks, blocks // ranks), (0, 2, 1))


def out_rows(table, rows):
    split, order = out_parts()
    ranks = lax.axis_size("seq")
    width = table.shape[1]
    whole = table.reshape(split + (ranks, rows, width))
    at = len(split)
    return whole.transpose(order + (at + 1, at, at + 2)).reshape(-1, ranks * width)


def gather_groups(block):
    return lax.all_gather(block, "dp", axis=0, tiled=True)


def swap_bit(block, axis, bit):
    return lax.ppermute(
        block, axis, [(place, place ^ (1 << bit)) for place in range(lax.axis_size(axis))]
    )


def bits_of(axis):
    return range(lax.axis_size(axis).bit_length() - 1)


def pair_kernel(lefts, rights, kept, me_ref, *refs):
    left_refs, right_refs, rest = refs[:lefts], refs[lefts : lefts + rights], refs[lefts + rights :]
    left, right = joined(left_refs), joined(right_refs)
    total = lax.dot_general(left, right, (((0,), (0,)), ((), ())), preferred_element_type=WIDE)
    if not kept:
        rest[0][...] = total.astype(LOW)
        return
    total = (total + rest[0][...].astype(WIDE)).astype(LOW)
    half = total.shape[1] // 2
    for number in range(4):

        @pl.when(pl.program_id(0) == number)
        def _():
            rest[1 + number][...] = total[:, :half]
            rest[5 + number][...] = total[:, half:]


def pair_product(lefts, rights, rows, got=None):
    groups, me = lax.axis_size("dp"), lax.axis_index("dp")
    pairs, width = groups // 2, rights[0].shape[1]
    kept = got is not None

    def left_block(number, me):
        side = lax.rem(me[0], 2)
        return (0, (me[0] // 2 ^ number) * 2 + (side if kept else 1 - side))

    in_specs = [pl.BlockSpec((left.shape[0], rows), left_block) for left in lefts]
    once = pl.Buffered(1)
    in_specs += [
        pl.BlockSpec(right.shape, lambda number, me: (0, 0), pipeline_mode=once) for right in rights
    ]
    block = pl.BlockSpec((rows, width), lambda number, me: (number, 0))
    if kept:
        in_specs.append(block)
        shape = (rows, width // 2)
        out_specs = [pl.BlockSpec(shape, lambda number, me: (0, 0), pipeline_mode=once)] * (2 * pairs)
        out_shape = [pltpu.HBM(shape, LOW)] * (2 * pairs)
    else:
        out_specs = block
        out_shape = pltpu.HBM((pairs * rows, width), LOW)
    return pl.pallas_call(
        partial(pair_kernel, len(lefts), len(rights), kept),
        out_shape=out_shape,
        grid_spec=pltpu.PrefetchScalarGridSpec(
            num_scalar_prefetch=1, grid=(pairs,), in_specs=in_specs, out_specs=out_specs
        ),
        compiler_params=pltpu.CompilerParams(vmem_limit_bytes=18 * 2**20),
        cost_estimate=pl.CostEstimate(
            flops=4 * pairs * rows * width * sum(left.shape[0] for left in lefts),
            bytes_accessed=4 * pairs * rows * width,
            transcendentals=0,
        ),
        name="pair_product",
    )(me[None], *lefts, *rights, *([got] if kept else []))


GELU_SCALE = (2 / jnp.pi) ** 0.5
GELU_CUBE = 0.044715


def gelu_parts(value):
    square = value * value
    bent = jnp.tanh(GELU_SCALE * value * (1 + GELU_CUBE * square))
    slope = 0.5 * (1 + bent) + 0.5 * value * (1 - bent * bent) * GELU_SCALE * (
        1 + 3 * GELU_CUBE * square
    )
    return 0.5 * value * (1 + bent), slope


def joined(refs):
    return jnp.concatenate([ref[...] for ref in refs])


CHUNK = 256


def stream_kernel(work, inputs, results, *refs):
    weight_ref, operands = refs[0], refs[1 : 1 + inputs]
    result_refs, (held, sem, *total) = refs[1 + inputs : 1 + inputs + results], refs[1 + inputs + results :]
    copies = []
    for number in range(held.shape[1] // CHUNK):
        part = pl.ds(number * CHUNK, CHUNK)
        copies.append(
            pltpu.make_async_copy(weight_ref.at[:, part], held.at[:, part], sem.at[number])
        )
    for copy in copies:
        copy.start()
    for number, copy in enumerate(copies):
        copy.wait()
        columns = slice(number * CHUNK, (number + 1) * CHUNK)
        work(number, columns, held[:, columns], operands, result_refs, *total)


def stream(name, work, weight, extent, operands, results, total=None):
    shape = (weight.shape[0], extent)
    scratch = [pltpu.VMEM(shape, weight.dtype), pltpu.SemaphoreType.DMA((extent // CHUNK,))]
    if total is not None:
        scratch.append(pltpu.VMEM(total, WIDE))
    return pl.pallas_call(
        partial(stream_kernel, work, len(operands), len(results)),
        out_shape=results,
        grid=(1,),
        in_specs=[pl.BlockSpec(memory_space=pl.ANY)]
        + [pl.BlockSpec(array.shape, lambda number: (0, 0)) for array in operands],
        out_specs=[pl.BlockSpec(result.shape, lambda number: (0, 0)) for result in results],
        scratch_shapes=scratch,
        compiler_params=pltpu.CompilerParams(vmem_limit_bytes=32 * 2**20),
        cost_estimate=pl.CostEstimate(
            flops=2 * operands[0].shape[0] * shape[0] * shape[1],
            bytes_accessed=2 * shape[0] * shape[1],
            transcendentals=0,
        ),
        name=name,
    )(pltpu.with_memory_space_constraint(weight, pltpu.HBM), *operands)


def column_block(rows, wide):
    return pl.BlockSpec((rows, wide), lambda number: (0, number))


def project_kernel(left_ref, weight_ref, bias_ref, to_ref):
    total = jnp.dot(left_ref[...], weight_ref[...], preferred_element_type=WIDE)
    to_ref[...] = (total + bias_ref[...]).astype(to_ref.dtype)


def project(left, weight, bias):
    (rows, depth), width = left.shape, bias.shape[0]
    return pl.pallas_call(
        project_kernel,
        out_shape=jax.ShapeDtypeStruct((rows, width), LOW),
        grid=(width // CHUNK,),
        in_specs=[whole_block(left), column_block(depth, CHUNK), column_block(1, CHUNK)],
        out_specs=column_block(rows, CHUNK),
        compiler_params=pltpu.CompilerParams(vmem_limit_bytes=16 * 2**20),
        name="project",
    )(left, pltpu.with_memory_space_constraint(weight, pltpu.HBM), bias[None])


def upward_product(lefts, weight, bias):
    def work(number, columns, chunk, operands, results):
        total = jnp.dot(joined(operands[:-1]), chunk, preferred_element_type=WIDE)
        total = total + operands[-1][:, columns]
        results[0][:, columns] = total
        results[1][:, columns] = gelu_parts(total)[0].astype(LOW)

    rows, width = sum(left.shape[0] for left in lefts), weight.shape[1]
    results = [jax.ShapeDtypeStruct((rows, width), kind) for kind in (WIDE, LOW)]
    return stream("upward_product", work, weight, width, [*lefts, bias[None]], results)


def dense_kernel(lefts, *refs):
    weight_ref, reward_ref, reward_to_ref = refs[lefts], refs[lefts + 1], refs[-1]
    total = jnp.dot(joined(refs[:lefts]), weight_ref[...], preferred_element_type=WIDE)
    row = 0
    for to_ref in refs[lefts + 2 : -1]:
        to_ref[...] = total[row : row + to_ref.shape[0]].astype(LOW)
        row += to_ref.shape[0]
    scaled = total * reward_ref[...]
    part = scaled[:, :128]
    for start in range(128, scaled.shape[1], 128):
        part = part + scaled[:, start : start + 128]

    @pl.when(pl.program_id(0) == 0)
    def _():
        reward_to_ref[...] = part

    @pl.when(pl.program_id(0) > 0)
    def _():
        reward_to_ref[...] += part


def dense_product(lefts, weight, reward):
    depth, width = weight.shape
    rows = sum(left.shape[0] for left in lefts)
    return pl.pallas_call(
        partial(dense_kernel, len(lefts)),
        out_shape=[jax.ShapeDtypeStruct((left.shape[0], width), LOW) for left in lefts]
        + [jax.ShapeDtypeStruct((rows, 128), WIDE)],
        grid=(width // CHUNK,),
        in_specs=[whole_block(left) for left in lefts]
        + [column_block(depth, CHUNK), column_block(1, CHUNK)],
        out_specs=[column_block(left.shape[0], CHUNK) for left in lefts]
        + [pl.BlockSpec((rows, 128), lambda number: (0, 0))],
        compiler_params=pltpu.CompilerParams(vmem_limit_bytes=16 * 2**20),
        name="dense_product",
    )(*lefts, weight, reward[None])


def against_dot(left, weight):
    return lax.dot_general(left, weight, (((1,), (1,)), ((), ())), preferred_element_type=WIDE)


def against_stream(name, lefts, weight, operands, results, finish):
    rows, depth = sum(left.shape[0] for left in lefts), lefts[0].shape[1]

    def work(number, columns, chunk, operand_refs, result_refs, total):
        left = jnp.concatenate([ref[:, columns] for ref in operand_refs[: len(lefts)]])
        part = against_dot(left, chunk)
        total[...] = part if number == 0 else total[...] + part
        if number == depth // CHUNK - 1:
            finish(total, operand_refs[len(lefts) :], result_refs)

    shape = (rows, weight.shape[0])
    return stream(name, work, weight, depth, [*lefts, *operands], results, shape)


def column_sums(*values):
    sums = [jnp.sum(value, axis=0, keepdims=True) for value in values]
    return jnp.concatenate(sums + [jnp.zeros((8 - len(sums), sums[0].shape[1]), WIDE)])


def by_chunk(width):
    return [slice(start, start + CHUNK) for start in range(0, width, CHUNK)]


def active_back(left, weight, upward):
    def finish(total, operands, results):
        for columns in by_chunk(upward.shape[1]):
            slope = gelu_parts(operands[0][:, columns])[1]
            low = (total[:, columns] * slope).astype(LOW)
            results[0][:, columns] = low
            results[1][:, columns] = column_sums(low.astype(WIDE))

    rows, width = upward.shape
    results = [jax.ShapeDtypeStruct((rows, width), LOW), jax.ShapeDtypeStruct((8, width), WIDE)]
    return against_stream("active_back", [left], weight, [upward], results, finish)


def against(lefts, weight, kind=WIDE):
    def finish(total, operands, results):
        results[0][...] = total[...].astype(kind)

    rows = sum(left.shape[0] for left in lefts)
    result = jax.ShapeDtypeStruct((rows, weight.shape[0]), kind)
    return against_stream("against", lefts, weight, [], [result], finish)[0]


def against_sums(left, weight, normal):
    def finish(total, operands, results):
        for columns in by_chunk(normal.shape[1]):
            value = total[:, columns]
            results[0][:, columns] = value
            results[1][:, columns] = column_sums(value * operands[0][:, columns], value)

    rows, width = normal.shape
    results = [jax.ShapeDtypeStruct((rows, width), WIDE), jax.ShapeDtypeStruct((8, width), WIDE)]
    return against_stream("against_sums", [left], weight, [normal], results, finish)


def masked_scores(query, key, queried_ref, keyed_ref, scale):
    scores = against_dot(query, key) * scale
    segment, place = queried_ref[:, 0:1], queried_ref[:, 1:2]
    other, before = keyed_ref[0:1, :], keyed_ref[1:2, :]
    allowed = ((other == 0) | (other == segment)) & (before <= place)
    return jnp.where(allowed, scores, MASKED)


def attend_kernel(scale, query_ref, key_ref, value_ref, queried_ref, keyed_ref, to_ref, log_ref):
    scores = masked_scores(query_ref[...], key_ref[...], queried_ref, keyed_ref, scale)
    highest = jnp.max(scores, axis=1, keepdims=True)
    exponent = jnp.exp(scores - highest)
    totals = jnp.sum(exponent, axis=1, keepdims=True)
    chances = (exponent / totals).astype(LOW)
    to_ref[...] = jnp.dot(chances, value_ref[...], preferred_element_type=WIDE).astype(LOW)
    log_ref[0] = highest + jnp.log(totals)


def head_blocks(length, wide, count):
    return [
        pl.BlockSpec((length, wide), lambda head, which=which: (0, which * count + head))
        for which in range(3)
    ]


def attend(projected, queried, keyed, wide, scale):
    length, columns = projected.shape
    count = columns // 3 // wide
    return pl.pallas_call(
        partial(attend_kernel, scale),
        out_shape=[
            jax.ShapeDtypeStruct((length, columns // 3), LOW),
            jax.ShapeDtypeStruct((count, length, 1), WIDE),
        ],
        grid=(count,),
        in_specs=head_blocks(length, wide, count)
        + [
            pl.BlockSpec((length, 2), lambda head: (0, 0)),
            pl.BlockSpec((2, length), lambda head: (0, 0)),
        ],
        out_specs=[
            pl.BlockSpec((length, wide), lambda head: (0, head)),
            pl.BlockSpec((1, length, 1), lambda head: (head, 0, 0)),
        ],
        compiler_params=pltpu.CompilerParams(vmem_limit_bytes=24 * 2**20),
        name="attend",
    )(projected, projected, projected, queried, keyed)


def attend_back_kernel(
    scale,
    count,
    query_ref,
    key_ref,
    value_ref,
    queried_ref,
    keyed_ref,
    log_ref,
    grad_ref,
    to_ref,
    sums_ref,
):
    query, key, grad = query_ref[...], key_ref[...], grad_ref[...]
    wide = query.shape[1]
    scores = masked_scores(query, key, queried_ref, keyed_ref, scale)
    chances = jnp.exp(scores - log_ref[0])
    chance_grad = against_dot(grad, value_ref[...])
    weighted = jnp.sum(chances * chance_grad, axis=1, keepdims=True)
    score_grad = (chances * (chance_grad - weighted)).astype(LOW)

    def across(left, right):
        return lax.dot_general(left, right, (((0,), (0,)), ((), ())), preferred_element_type=WIDE)

    grads = (
        jnp.dot(score_grad, key, preferred_element_type=WIDE) * scale,
        across(score_grad, query) * scale,
        across(chances.astype(LOW), grad),
    )
    for which, value in enumerate(grads):
        low = value.astype(LOW)
        start = pl.multiple_of((which * count + pl.program_id(0)) * wide, wide)
        to_ref[:, pl.ds(start, wide)] = low
        sums_ref[:, pl.ds(start, wide)] = column_sums(low.astype(WIDE))


def attend_back(projected, queried, keyed, log_rows, grad, wide, scale):
    length, columns = projected.shape
    count = columns // 3 // wide
    return pl.pallas_call(
        partial(attend_back_kernel, scale, count),
        out_shape=[
            jax.ShapeDtypeStruct((length, columns), LOW),
            jax.ShapeDtypeStruct((8, columns), WIDE),
        ],
        grid=(count,),
        in_specs=head_blocks(length, wide, count)
        + [
            pl.BlockSpec((length, 2), lambda head: (0, 0)),
            pl.BlockSpec((2, length), lambda head: (0, 0)),
            pl.BlockSpec((1, length, 1), lambda head: (head, 0, 0)),
            pl.BlockSpec((length, wide), lambda head: (0, head)),
        ],
        out_specs=[
            pl.BlockSpec((length, columns), lambda head: (0, 0)),
            pl.BlockSpec((8, columns), lambda head: (0, 0)),
        ],
        compiler_params=pltpu.CompilerParams(vmem_limit_bytes=32 * 2**20),
        name="attend_back",
    )(projected, projected, projected, queried, keyed, log_rows, grad)


def whole_block(array):
    return pl.BlockSpec(array.shape, lambda number: (0, 0), pipeline_mode=pl.Buffered(1))


def rows_kernel(lefts, *refs):
    left, right = joined(refs[:lefts]), joined(refs[lefts:-1])
    total = lax.dot_general(left, right, (((0,), (0,)), ((), ())), preferred_element_type=WIDE)
    refs[-1][...] = total.astype(LOW)


def rows_product(lefts, rights):
    rows, width = lefts[0].shape[1], rights[0].shape[1]
    wide = 256
    if rows % wide:
        return inner_rows(jnp.concatenate(lefts), jnp.concatenate(rights)).astype(LOW)
    return pl.pallas_call(
        partial(rows_kernel, len(lefts)),
        out_shape=pltpu.HBM((rows, width), LOW),
        grid=(rows // wide,),
        in_specs=[pl.BlockSpec((left.shape[0], wide), lambda number: (0, number)) for left in lefts]
        + [
            pl.BlockSpec(right.shape, lambda number: (0, 0), pipeline_mode=pl.Buffered(1))
            for right in rights
        ],
        out_specs=pl.BlockSpec((wide, width), lambda number: (number, 0)),
        compiler_params=pltpu.CompilerParams(vmem_limit_bytes=16 * 2**20),
        cost_estimate=pl.CostEstimate(
            flops=4 * rows * width * sum(left.shape[0] for left in lefts),
            bytes_accessed=4 * rows * width,
            transcendentals=0,
        ),
        name="rows_product",
    )(*lefts, *rights)


def scatter_product(lefts, rights):
    return scatter_groups(rows_product(lefts, rights))


def scatter_groups(table):
    return lax.psum_scatter(table, "dp", scatter_dimension=0, tiled=True)


def out_columns(left, rows):
    split, order = out_parts()
    count = left.shape[0]
    back = tuple(1 + order.index(axis) for axis in range(len(order)))
    moved = left.reshape((count,) + tuple(split[axis] for axis in order) + (rows,))
    return moved.transpose((0,) + back + (1 + len(split),)).reshape(count, -1)


def pair_onward(pieces):
    return [swap_bit(pieces[3], "dp", 1), swap_bit(pieces[7], "dp", 2)]


def pair_second(pieces, onward):
    one = pieces[2].astype(WIDE) + onward[0].astype(WIDE)
    two = pieces[5].astype(WIDE) + onward[1].astype(WIDE)
    return [swap_bit(one.astype(LOW), "dp", 2), swap_bit(two.astype(LOW), "dp", 1)]


def pair_staying(pieces):
    return [swap_bit(pieces[1], "dp", 1), swap_bit(pieces[6], "dp", 2)]


def pair_sum(pieces, staying, second):
    sums = [
        own.astype(WIDE) + one.astype(WIDE) + two.astype(WIDE)
        for own, one, two in zip((pieces[0], pieces[4]), staying, second)
    ]
    return jnp.concatenate(sums, axis=1)


def rank_rows(table, rows):
    ranks, me = lax.axis_size("seq"), lax.axis_index("seq")
    return [
        lax.dynamic_slice_in_dim(table, (me + shift) % ranks * rows, rows, 0)
        for shift in range(ranks)
    ]


def swap_ranks(blocks):
    size = lax.axis_size("seq")
    return [blocks[0]] + [
        lax.ppermute(blocks[shift], "seq", [(place, (place + shift) % size) for place in range(size)])
        for shift in range(1, size)
    ]


def rows_by_rank(blocks, beside=None):
    ranks, me = len(blocks), lax.axis_index("seq")
    rows, width = blocks[0].shape
    sources = [(number, 0, rows, 0, width, 0) for number in range(ranks)]
    to_rows = [(me + ranks - number) % ranks * rows for number in range(ranks)]
    arrays, more = list(blocks), 0
    if beside is not None:
        more = beside.shape[1] // ranks
        sources += [(ranks, 0, rows, number * more, more, width) for number in range(ranks)]
        to_rows += [number * rows for number in range(ranks)]
        arrays.append(beside)
    return place(arrays, sources, jnp.stack([jnp.int32(row) for row in to_rows]), (ranks * rows, width + more))


def by_number(blocks):
    return to_ring(jnp.stack(blocks))


def small_order():
    groups, ranks = lax.axis_size("dp"), lax.axis_size("seq")
    number = jnp.arange(groups * ranks)
    place = ((number // ranks) ^ lax.axis_index("dp")) * ranks + (
        (number % ranks) ^ lax.axis_index("seq")
    )
    return (place[:, None] == number[None, :]).astype(WIDE)


def scatter_small(table, gates=()):
    gates = list(gates)
    count = 0
    table = jnp.dot(
        small_order().T, table, precision=lax.Precision.HIGHEST, preferred_element_type=WIDE
    )
    for axis in ("dp", "seq"):
        for bit in reversed(bits_of(axis)):
            if count % 2 and gates:
                table = after(table, [gates.pop(0)])
            count += 1
            half = table.shape[0] // 2
            table = table[:half] + swap_bit(table[half:], axis, bit)
    return table[0]


def sum_ranks(table):
    size = lax.axis_size("seq")
    total = table
    for shift in range(1, size):
        total = total + lax.ppermute(
            table, "seq", [(place, (place + shift) % size) for place in range(size)]
        )
    return total


def spread_path(
    inputs,
    cotangent,
    segments,
    labels,
    step_ends,
    attend_gain,
    attend_shift,
    project_in,
    project_bias,
    project_out,
    output_bias,
    dense_gain,
    dense_shift,
    up_weight,
    up_bias,
    down_weight,
    down_bias,
    reward_weight,
):
    groups, ranks = lax.axis_size("dp"), lax.axis_size("seq")
    rank = lax.axis_index("seq")
    rows_here, places_here, width = inputs.shape
    all_rows = rows_here * groups
    head_width = width // HEADS
    heads_here = HEADS // ranks
    share = heads_here * head_width
    rows_in = project_in.shape[0]
    hidden_here = down_weight.shape[0]
    length = ranks * places_here
    score_scale = head_width ** (-0.5)

    small = (
        attend_gain,
        attend_shift,
        project_bias,
        output_bias,
        dense_gain,
        dense_shift,
        up_bias,
        down_bias,
        reward_weight,
    )
    sizes = [vector.shape[0] for vector in small]
    riders = [vector.reshape(-(-vector.shape[0] // 128), -1) for vector in small]
    riders += [segments, labels, step_ends]
    dealt_in = deal(project_in, head_pieces, head_width, riders)
    came_in = swap_ranks(dealt_in)
    out_moved = lax.ppermute(after(project_out, dealt_in), EVERY, out_route())
    rows_in_all = rows_by_rank(came_in, out_moved)
    gathered = gather_groups(rows_in_all)
    inputs_ring = ring_gather(
        after(inputs[0], came_in), [idle, idle, idle]
    )
    first_normals = []
    for halves in inputs_ring:
        normal, inverse = normal_parts(jnp.concatenate(halves).astype(WIDE))
        if not first_normals:
            first_inverse = inverse
        first_normals.append(normal)
    dealt_up = deal(after(up_weight, [rows_in_all]), hidden_pieces, hidden_here)
    came_up = swap_ranks(after(dealt_up, inputs_ring[-1]))
    gathered = after(gathered, first_normals)
    rows_up_all = rows_by_rank(came_up)
    weight_up = gather_groups(rows_up_all)
    weight_down = gather_groups(after(down_weight, [rows_up_all]))
    riders = gathered[:, 3 * share : 3 * share + 128]
    lines_all = sum(-(-size // 128) for size in sizes) + 3
    lines_all = -(-lines_all // 8) * 8
    riders = riders.reshape(groups * ranks, rows_in, 128)[:, :lines_all].astype(WIDE)
    vectors = []
    row = 0
    for size in sizes + [places_here] * 3:
        lines = -(-size // 128)
        vectors.append(
            riders[:, row : row + lines].reshape(groups * ranks, -1)[:, :size].reshape(-1)
        )
        row += lines
    gain_one, shift_one, bias_in, bias_out, gain_two, shift_two, bias_up, bias_down, reward_wide = (
        vectors[: len(sizes)]
    )

    held = own_heads()
    bias_heads = exact(held, bias_in.reshape(2, HEADS, head_width).transpose(1, 0, 2).reshape(HEADS, -1))
    bias_heads = bias_heads.reshape(heads_here, 2, head_width)
    bias_full = jnp.concatenate(
        [bias_heads[:, 0].reshape(-1), jnp.zeros((share,), WIDE), bias_heads[:, 1].reshape(-1)]
    )
    bias_up_here = lax.dynamic_index_in_dim(
        bias_up.reshape(groups, ranks, hidden_here), rank, 1, keepdims=False
    ).reshape(-1)
    marks = jnp.stack(
        [
            lax.dynamic_index_in_dim(
                mark.reshape(groups, ranks, places_here), lax.axis_index("dp"), 0, keepdims=False
            )
            for mark in vectors[len(sizes) :]
        ],
        axis=1,
    )
    marks_ring = to_ring(marks)
    segments_ring = marks_ring[:, 0].reshape(-1)
    places_ring = to_ring(jnp.arange(length).reshape(ranks, places_here)).reshape(-1)

    own = inputs[0].astype(WIDE)
    firsts = [(normal * gain_one + shift_one).astype(LOW) for normal in first_normals]
    projected = project(jnp.concatenate(firsts), gathered, bias_full)
    gathered, projected = lax.optimization_barrier((gathered, projected))
    weight_out = out_rows(gathered[:, 3 * share + 128 :], rows_in)
    queried, keyed = (
        jnp.stack([segments_ring.astype(WIDE), places_ring.astype(WIDE)], axis=axis)
        for axis in (1, 0)
    )
    mixture, log_rows = attend(projected, queried, keyed, head_width, score_scale)

    def block_of(array, k):
        return array[k * places_here : (k + 1) * places_here]

    weight_back = None

    def contiguous(gate):
        nonlocal weight_back
        weight_back = after(gathered, gate)[:, : 3 * share]
        return [weight_back]

    mixture_out = None

    def in_blocks(gate):
        nonlocal mixture_out
        mixture_out = out_columns(after(mixture, gate), project_out.shape[0])
        return [mixture_out]

    branch = ring_sum(
        lambda k, gate: product(block_of(mixture, k), weight_out), [contiguous, in_blocks, idle]
    )
    weight_back, mixture_out = lax.optimization_barrier((weight_back, mixture_out))
    hidden = own + branch + bias_out

    second_normal, second_inverse = normal_parts(hidden)
    second_value = second_normal * gain_two + shift_two

    rows_all = ranks * rows_in
    fenced = groups == 8 and rows_all % 128 == 0
    steady = (segments[0, 0] | 1) != 0

    def step(work, *operands):
        return fence(steady, work, *operands) if fenced else work(*operands)

    def upward_of(k, halves):
        return upward_product(halves, weight_up, bias_up_here)

    seconds, found = ring_gather(second_value.astype(LOW), use=upward_of, plan=(1, 1, 1))

    def dense_one(halves, block):
        return upward_of(None, halves), ring_move([block])[0]

    def dense_two(activated, block):
        return dense_product(activated, weight_down, reward_wide), ring_move([block])[0]

    cotangents = [cotangent[0]]
    last, block = step(dense_one, seconds[-1], cotangents[-1])
    cotangents.append(block)
    upwards, activated = map(list, zip(*found, last))
    (*dense_parts, reward_lanes), block = step(dense_two, activated, cotangents[-1])
    cotangents.append(block)
    dense_parts = lax.optimization_barrier(dense_parts)
    reward_parts = list(jnp.sum(reward_lanes, axis=-1).reshape(ranks, places_here))

    reward_parts[0] = reward_parts[0] + jnp.sum((hidden + bias_down) * reward_wide, axis=-1)
    rewards_all = sum_ranks(to_ring(jnp.stack(reward_parts)))
    scored = marks[:, 2] * (marks[:, 0] > 0)
    error_all = scored * (jax.nn.sigmoid(rewards_all) - marks[:, 1]) / all_rows
    error_ring = to_ring(error_all)
    rewards = lax.dynamic_index_in_dim(rewards_all, rank, 0, keepdims=False)

    def dense_grad(block, k):
        return block.astype(WIDE) + error_ring[k][:, None] * reward_wide

    dense_lows = [dense_grad(block, k).astype(LOW) for k, block in enumerate(cotangents)]

    def second_part(k, dense_low):
        upward_low, sums = active_back(dense_low, weight_down, upwards[k])
        return against([upward_low], weight_up), (upward_low, sums)

    def second_first(block, dense_low):
        term, upward_low = second_part(1, dense_low)
        return term.astype(LOW), upward_low, ring_move([block])[0]

    def second_step(k, sent, dense_low):
        moved = ring_move([sent])[0]
        term, upward_low = second_part(k, dense_low)
        total = moved.astype(WIDE) + term
        return total if k == 0 else total.astype(LOW), upward_low

    upward_lows = [None] * ranks
    sent, upward_lows[1], block = step(second_first, cotangents[-1], dense_lows[1])

    def second_next(sent, block):
        dense_low = dense_grad(block, ranks - 1).astype(LOW)
        table = rows_product(activated, [*dense_lows, dense_low])
        return second_step(2, sent, dense_lows[2]), dense_low, table

    (sent, upward_lows[2]), dense_low, down_table = step(second_next, sent, block)
    dense_lows.append(dense_low)
    down_summed = scatter_groups(down_table)
    for k in list(range(3, ranks)) + [0]:
        sent, upward_lows[k] = step(partial(second_step, k), sent, dense_lows[k])
    second_grad = sent
    result_grad = after(dense_grad(cotangents[0], 0), [sent])
    upward_lows, upward_sums = zip(*upward_lows)
    reward_weight_gradient = jnp.sum(error_ring[0][:, None] * (hidden + bias_down), axis=0)
    for k, part in enumerate(dense_parts):
        reward_weight_gradient += jnp.sum(error_ring[k][:, None] * part.astype(WIDE), axis=0)
    down_bias_gradient = jnp.sum(dense_lows[0].astype(WIDE), axis=0)
    up_bias_gradient = sum(upward_sums)[0]
    dense_gain_gradient = jnp.sum(second_grad * second_normal, axis=0)
    dense_shift_gradient = jnp.sum(second_grad, axis=0)
    hidden_grad = result_grad + normalize_back(second_grad, second_normal, second_inverse, gain_two)

    branch_low = hidden_grad.astype(LOW)
    seconds = sum(seconds, [])
    output_bias_gradient = jnp.sum(branch_low.astype(WIDE), axis=0)

    def by_device(vectors):
        return jnp.concatenate([vector.reshape(groups * ranks, -1) for vector in vectors], axis=1)

    def early_table():
        up_bias_all = lax.dynamic_update_index_in_dim(
            jnp.zeros((groups, ranks, hidden_here), WIDE),
            up_bias_gradient.reshape(groups, hidden_here),
            rank,
            1,
        )
        return by_device(
            (
                output_bias_gradient,
                dense_gain_gradient,
                dense_shift_gradient,
                up_bias_all,
                down_bias_gradient,
                reward_weight_gradient,
            )
        )

    def back(mixture_grad):
        return attend_back(
            projected, queried, keyed, log_rows, mixture_grad, head_width, score_scale
        )

    def first_part(projected_grad, k):
        return against_sums(block_of(projected_grad, k), weight_back, first_normals[k])

    def inputs_back(first_grad):
        return hidden_grad + normalize_back(
            first_grad, first_normals[0], first_inverse, gain_one
        )

    def small_table(bias_sums, first_sums, early):
        bias_heads = jnp.concatenate([bias_sums[0, :share], bias_sums[0, 2 * share :]])
        bias_heads = bias_heads.reshape(2, heads_here, head_width)
        bias_all = jnp.concatenate(
            [exact(held.T, bias_heads[which]).reshape(-1) for which in range(2)]
        )
        gain_sum, shift_sum = sum(first_sums)[:2]
        return jnp.concatenate([by_device((gain_sum, shift_sum, bias_all)), early], axis=1)

    def out_back(out_summed):
        back = [(there, here) for here, there in out_route()]
        return lax.ppermute(out_summed, EVERY, back).astype(WIDE)

    def result_back(dense_sum):
        return (hidden + dense_sum + bias_down).astype(LOW)

    def sent_rows(summed):
        return rank_rows(summed.astype(LOW), rows_in)

    if fenced:

        def gather_one(block):
            return ring_move([block])[0], pair_product(seconds, upward_lows, rows_all)

        def gather_two(block, up_sent):
            return ring_move([block])[0], swap_bit(up_sent, "dp", 0), early_table()

        def gather_three(block, up_got):
            return ring_move([block])[0], pair_product(seconds, upward_lows, rows_all, up_got)

        def attend_one(branch_lows, up_pieces):
            dense_sum = ring_step(dense_parts[1], dense_parts[2])
            up_onward = pair_onward(up_pieces)
            mixture_grad = against(branch_lows, weight_out, LOW)
            out_table = rows_product([mixture_out], branch_lows)
            return dense_sum, up_onward, mixture_grad, out_table

        def attend_two(dense_sum, up_pieces, up_onward, mixture_grad):
            dense_sum = ring_step(dense_sum, dense_parts[3])
            return dense_sum, pair_second(up_pieces, up_onward), back(mixture_grad)

        def attend_three(dense_sum, up_pieces, projected_grad):
            dense_sum = ring_step(dense_sum, dense_parts[0])
            up_staying = pair_staying(up_pieces)
            in_sent = pair_product(firsts, [projected_grad], rows_all)
            term, sums = first_part(projected_grad, 1)
            return result_back(dense_sum), up_staying, in_sent, term.astype(LOW), sums

        def first_one(sent, in_sent, projected_grad, up_pieces, up_staying, up_second):
            moved = ring_move([sent])[0]
            in_got = swap_bit(in_sent, "dp", 0)
            term, sums = first_part(projected_grad, 2)
            up_sent = sent_rows(pair_sum(up_pieces, up_staying, up_second))
            return (moved.astype(WIDE) + term).astype(LOW), in_got, up_sent, sums

        def first_two(sent, in_got, projected_grad):
            moved = ring_move([sent])[0]
            in_pieces = pair_product(firsts, [projected_grad], rows_all, in_got)
            term, sums = first_part(projected_grad, 3)
            return (moved.astype(WIDE) + term).astype(LOW), list(in_pieces), sums

        def first_three(sent, in_pieces, projected_grad, bias_sums, first_sums, early):
            moved = ring_move([sent])[0]
            in_onward = pair_onward(in_pieces)
            term, sums = first_part(projected_grad, 0)
            table = small_table(bias_sums, [sums, *first_sums], early)
            return moved.astype(WIDE) + term, in_onward, table

        def last_one(in_pieces, in_onward, up_sent, first_grad):
            came_up = swap_ranks(up_sent)
            in_second = pair_second(in_pieces, in_onward)
            in_staying = pair_staying(in_pieces)
            first_grad, down_late = after((first_grad, down_summed), [came_up[1]])
            in_sent = sent_rows(pair_sum(in_pieces, in_staying, in_second))
            return came_up, in_sent, inputs_back(first_grad), down_late.astype(WIDE)

        def last_two(in_sent, came_up, table):
            came_in = swap_ranks(in_sent)
            came_up, out_late = after((came_up, out_summed), [came_in[2]])
            return (
                collect(came_in, head_pieces, head_width),
                collect(came_up, hidden_pieces, hidden_here),
                scatter_small(table, came_in[1:]),
                out_back(out_late),
            )

        branch_lows = [branch_low]
        moved, up_sent = step(gather_one, branch_low)
        branch_lows.append(moved)
        moved, up_got, early = step(gather_two, moved, up_sent)
        branch_lows.append(moved)
        moved, up_pieces = step(gather_three, moved, up_got)
        branch_lows.append(moved)
        dense_sum, up_onward, mixture_grad, out_table = step(attend_one, branch_lows, up_pieces)
        out_summed = scatter_groups(out_table)
        dense_sum, up_second, (projected_grad, bias_sums) = step(
            attend_two, dense_sum, up_pieces, up_onward, mixture_grad
        )
        result_low, up_staying, in_sent, sent, sums_one = step(
            attend_three, dense_sum, up_pieces, projected_grad
        )
        sent, in_got, up_sent, sums_two = step(
            first_one, sent, in_sent, projected_grad, up_pieces, up_staying, up_second
        )
        sent, in_pieces, sums_three = step(first_two, sent, in_got, projected_grad)
        first_grad, in_onward, table = step(
            first_three,
            sent,
            in_pieces,
            projected_grad,
            bias_sums,
            [sums_one, sums_two, sums_three],
            early,
        )
        came_up, in_sent, inputs_gradient, down_weight_gradient = step(
            last_one, in_pieces, in_onward, up_sent, first_grad
        )
        project_in_gradient, up_weight_gradient, summed, project_out_gradient = step(
            last_two, in_sent, came_up, table
        )
    else:
        branch_lows = sum(ring_gather(branch_low, cut=1), [])
        projected_grad, bias_sums = back(against(branch_lows, weight_out, LOW))
        out_summed = scatter_groups(rows_product([mixture_out], branch_lows))
        first_sums = [None] * ranks

        def first_term(k, gate):
            term, first_sums[k] = first_part(projected_grad, k)
            return term

        first_grad = ring_sum(first_term, cut=1)
        dense_sum = dense_parts[1]
        for part in dense_parts[2:] + dense_parts[:1]:
            dense_sum = ring_step(dense_sum, part)
        up_summed = scatter_product(seconds, upward_lows)
        in_summed = scatter_product(firsts, [projected_grad])
        inputs_gradient, result_low = inputs_back(first_grad), result_back(dense_sum)
        summed = scatter_small(small_table(bias_sums, first_sums, early_table()))
        up_weight_gradient = collect(swap_ranks(sent_rows(up_summed)), hidden_pieces, hidden_here)
        project_in_gradient = collect(swap_ranks(sent_rows(in_summed)), head_pieces, head_width)
        project_out_gradient = out_back(out_summed)
        down_weight_gradient = down_summed.astype(WIDE)
    parts = []
    start = 0
    for size in sizes:
        parts.append(summed[start : start + size])
        start += size
    return (
        result_low[None],
        rewards[None],
        inputs_gradient[None],
        parts[0],
        parts[1],
        project_in_gradient,
        parts[2],
        project_out_gradient,
        parts[3],
        parts[4],
        parts[5],
        up_weight_gradient,
        parts[6],
        down_weight_gradient,
        parts[7],
        parts[8],
    )


def solution(mesh):
    row = P("dp", "seq")
    wide_row = P("dp", "seq", None)
    vector = P(("dp", "seq"))
    matrix = P(("dp", "seq"), None)
    in_specs = (
        wide_row,
        wide_row,
        row,
        row,
        row,
        vector,
        vector,
        matrix,
        vector,
        matrix,
        vector,
        vector,
        vector,
        matrix,
        vector,
        matrix,
        vector,
        vector,
    )
    out_specs = (
        wide_row,
        row,
        wide_row,
        vector,
        vector,
        matrix,
        vector,
        matrix,
        vector,
        vector,
        vector,
        matrix,
        vector,
        matrix,
        vector,
        vector,
    )
    return jax.shard_map(
        spread_path, mesh=mesh, in_specs=in_specs, out_specs=out_specs, check_vma=False
    )
```

```python
from functools import partial

import jax
import jax.numpy as jnp
from jax import lax
from jax.experimental import pallas as pl
from jax.experimental.pallas import tpu as pltpu
from jax.sharding import PartitionSpec as P

HEADS = 16
EPSILON = 1e-05
MASKED = -1e30
LOW = jnp.bfloat16
WIDE = jnp.float32
EVERY = ("dp", "seq")


def product(left, right):
    return jnp.dot(left, right, preferred_element_type=WIDE)


def inner_rows(left, right):
    return jnp.einsum("ta,tb->ab", left, right, preferred_element_type=WIDE)


def against_rows(left, right):
    return jnp.einsum("tb,ab->ta", left, right, preferred_element_type=WIDE)


def normal_parts(field):
    center = field - jnp.mean(field, axis=-1, keepdims=True)
    spread = jnp.mean(center * center, axis=-1, keepdims=True)
    inverse = lax.rsqrt(spread + EPSILON)
    return center * inverse, inverse


def normalize_back(upstream, normal, inverse, gain):
    scaled = upstream * gain
    mean_scaled = jnp.mean(scaled, axis=-1, keepdims=True)
    mean_cross = jnp.mean(scaled * normal, axis=-1, keepdims=True)
    return inverse * (scaled - mean_scaled - normal * mean_cross)


def ring_next():
    size = lax.axis_size("seq")
    return [(place, (place + 1) % size) for place in range(size)]


def after(value, done):
    return lax.optimization_barrier((value, tuple(done)))[0]


def fence(steady, work, *operands):
    shapes = jax.eval_shape(work, *operands)
    return lax.cond(
        steady,
        work,
        lambda *_: jax.tree.map(lambda shape: jnp.zeros(shape.shape, shape.dtype), shapes),
        *operands,
    )


def idle(gate):
    return []


def pieces_of(block, cut):
    rows = block.shape[0] // cut
    return [block[piece * rows : (piece + 1) * rows] for piece in range(cut)]


def ring_move(halves):
    return [lax.ppermute(half, "seq", ring_next()) for half in halves]


def ring_gather(block, flights=(idle,) * 3, use=None, plan=(), cut=2):
    blocks, results = [pieces_of(block, cut)], []
    for k in range(lax.axis_size("seq") - 1):
        moved = ring_move(blocks[-1])
        done = []
        if use is not None:
            for _ in range(plan[k]):
                results.append(use(len(results), blocks[len(results)]))
                done += jax.tree.leaves(results[-1])
        done += flights[k](blocks[-1])
        if done:
            moved[-1] = after(moved[-1], done)
        blocks.append(moved)
    return blocks if use is None else (blocks, results)


def ring_sum(part, flights=(idle,) * 3, cut=2):
    size = lax.axis_size("seq")
    sent = pieces_of(part(1, ()).astype(LOW), cut)
    for step, k in enumerate(list(range(2, size)) + [0]):
        kind = LOW if step < size - 2 else WIDE
        moved = ring_move(sent)
        term = part(k, sent)
        done = [term] + flights[step](sent)
        total = []
        for piece, (came, own) in enumerate(zip(moved, pieces_of(term, cut))):
            came = after(came, total + (done if piece == cut - 1 else []))
            total.append((came.astype(WIDE) + own).astype(kind))
        sent = total
    return jnp.concatenate(sent) if cut > 1 else sent[0]


def ring_step(total, part, kind=LOW):
    moved = lax.ppermute(total.astype(LOW), "seq", ring_next())
    return (moved.astype(WIDE) + part.astype(WIDE)).astype(kind)


def deal_kernel(pieces, wide, riders, me_ref, from_ref, *refs):
    rider_refs, to_refs, packed = refs[:riders], refs[riders:-1], refs[-1]
    ranks = len(to_refs)
    columns = from_ref.shape[1] // ranks
    if riders:
        packed[...] = jnp.zeros_like(packed)
        row = 0
        for rider_ref in rider_refs:
            lines, width = rider_ref.shape
            packed[row : row + lines, :width] = rider_ref[...].astype(WIDE)
            row += lines
    for shift, to_ref in enumerate(to_refs):
        to = lax.rem(me_ref[0] + shift, ranks)
        for place in range(columns // wide):
            start = pl.multiple_of(pieces(to, place) * wide, wide)
            to_ref[:, place * wide : (place + 1) * wide] = from_ref[:, pl.ds(start, wide)]
        if riders:
            to_ref[:, columns:] = packed[...].astype(to_ref.dtype)


def deal(matrix, pieces, wide, riders=()):
    ranks, me = lax.axis_size("seq"), lax.axis_index("seq")
    rows, columns = matrix.shape
    if wide % 128 == 0:
        each = columns // ranks + (128 if riders else 0)
        return pl.pallas_call(
            partial(deal_kernel, pieces, wide, len(riders)),
            out_shape=[jax.ShapeDtypeStruct((rows, each), matrix.dtype)] * ranks,
            grid_spec=pltpu.PrefetchScalarGridSpec(
                num_scalar_prefetch=1,
                grid=(1,),
                in_specs=[pl.BlockSpec((rows, columns), lambda i, me: (0, 0))]
                + [pl.BlockSpec(rider.shape, lambda i, me: (0, 0)) for rider in riders],
                out_specs=[pl.BlockSpec((rows, each), lambda i, me: (0, 0))] * ranks,
                scratch_shapes=[pltpu.VMEM((rows, 128), WIDE)],
            ),
            name="deal",
        )(me[None], matrix, *riders)
    dealt = jnp.stack(
        [
            jnp.concatenate(
                [
                    matrix[:, pieces(to, place) * wide :][:, :wide]
                    for place in range(columns // ranks // wide)
                ],
                axis=1,
            )
            for to in range(ranks)
        ]
    )
    return [
        lax.dynamic_index_in_dim(dealt, (me + shift) % ranks, 0, keepdims=False)
        for shift in range(ranks)
    ]


def collect_kernel(pieces, wide, me_ref, *refs):
    from_refs, to_ref = refs[:-1], refs[-1]
    ranks = len(from_refs)
    for shift, from_ref in enumerate(from_refs):
        source = lax.rem(me_ref[0] + ranks - shift, ranks)
        for place in range(from_ref.shape[1] // wide):
            start = pl.multiple_of(pieces(source, place) * wide, wide)
            to_ref[:, pl.ds(start, wide)] = from_ref[:, place * wide : (place + 1) * wide].astype(
                to_ref.dtype
            )


def collect(blocks, pieces, wide):
    ranks, me = lax.axis_size("seq"), lax.axis_index("seq")
    rows, columns = blocks[0].shape
    if wide % 128 == 0:
        return pl.pallas_call(
            partial(collect_kernel, pieces, wide),
            out_shape=jax.ShapeDtypeStruct((rows, columns * ranks), WIDE),
            grid_spec=pltpu.PrefetchScalarGridSpec(
                num_scalar_prefetch=1,
                grid=(1,),
                in_specs=[pl.BlockSpec((rows, columns), lambda i, me: (0, 0))] * ranks,
                out_specs=pl.BlockSpec((rows, columns * ranks), lambda i, me: (0, 0)),
            ),
            name="collect",
        )(me[None], *blocks)
    held = by_number(blocks)
    found = {
        pieces(to, place): held[to, :, place * wide : (place + 1) * wide]
        for to in range(ranks)
        for place in range(columns // wide)
    }
    return jnp.concatenate([found[piece] for piece in sorted(found)], axis=1).astype(WIDE)


def place_kernel(sources, to_row_ref, *refs):
    held, in_sem, out_sem = refs[-3:]
    from_refs, to_ref = refs[:-4], refs[-4]
    loads, stores = [], []
    at = 0
    for number, (array, row, rows, column, width, to_column) in enumerate(sources):
        start = pl.multiple_of(to_row_ref[number], rows)
        piece = held.at[pl.ds(at, rows), pl.ds(0, width)]
        source = from_refs[array].at[pl.ds(row, rows), pl.ds(column, width)]
        target = to_ref.at[pl.ds(start, rows), pl.ds(to_column, width)]
        loads.append(pltpu.make_async_copy(source, piece, in_sem.at[number]))
        stores.append(pltpu.make_async_copy(piece, target, out_sem.at[number]))
        at += rows
    for load in loads:
        load.start()
    for load, store in zip(loads, stores):
        load.wait()
        store.start()
    for store in stores:
        store.wait()


def place(arrays, sources, to_rows, shape):
    count = len(sources)
    wide = max(width for _, _, _, _, width, _ in sources)
    total = sum(rows for _, _, rows, _, _, _ in sources)
    return pl.pallas_call(
        partial(place_kernel, sources),
        out_shape=jax.ShapeDtypeStruct(shape, arrays[0].dtype),
        grid_spec=pltpu.PrefetchScalarGridSpec(
            num_scalar_prefetch=1,
            grid=(1,),
            in_specs=[pl.BlockSpec(memory_space=pl.ANY)] * len(arrays),
            out_specs=pl.BlockSpec(memory_space=pl.ANY),
            scratch_shapes=[
                pltpu.VMEM((total, wide), arrays[0].dtype),
                pltpu.SemaphoreType.DMA((count,)),
                pltpu.SemaphoreType.DMA((count,)),
            ],
        ),
        compiler_params=pltpu.CompilerParams(vmem_limit_bytes=total * wide * 2 + 4 * 2**20),
        name="place",
    )(to_rows, *arrays)


def to_ring(table):
    size = lax.axis_size("seq")
    me = lax.axis_index("seq")
    return jnp.stack(
        [lax.dynamic_index_in_dim(table, (me - k) % size, 0, keepdims=False) for k in range(size)]
    )


def head_of(rank, place):
    groups, ranks = lax.axis_size("dp"), lax.axis_size("seq")
    blocks = groups * ranks // HEADS
    if blocks <= ranks:
        held = groups // blocks
        return (rank % blocks * held + place) * (ranks // blocks) + rank // blocks
    return place * ranks + rank


def heads_of():
    ranks = lax.axis_size("seq")
    return [[head_of(rank, place) for place in range(HEADS // ranks)] for rank in range(ranks)]


def head_pieces(rank, place):
    held = HEADS // lax.axis_size("seq")
    return place // held * HEADS + head_of(rank, place % held)


def hidden_pieces(rank, place):
    return place * lax.axis_size("seq") + rank


def own_heads():
    numbers = jnp.array(heads_of())
    mine = lax.dynamic_index_in_dim(numbers, lax.axis_index("seq"), 0, keepdims=False)
    return (mine[:, None] == jnp.arange(HEADS)[None, :]).astype(WIDE)


def exact(left, right):
    return jnp.dot(left, right, precision=lax.Precision.HIGHEST, preferred_element_type=WIDE)


def out_route():
    groups, ranks = lax.axis_size("dp"), lax.axis_size("seq")
    blocks = groups * ranks // HEADS
    route = []
    for group in range(groups):
        for rank in range(ranks):
            if blocks <= ranks:
                held = groups // blocks
                high, low = divmod(group, held)
                pair, part = divmod(rank, blocks)
                target = (part * held + low, pair * blocks + high)
            else:
                span = blocks // ranks
                head, extra = divmod(group, span)
                high, low = divmod(head, ranks)
                target = ((high * ranks + rank) * span + extra, low)
            route.append((group * ranks + rank, target[0] * ranks + target[1]))
    return route


def out_parts():
    groups, ranks = lax.axis_size("dp"), lax.axis_size("seq")
    blocks = groups * ranks // HEADS
    if blocks <= ranks:
        return ((blocks, groups // blocks), (1, 0))
    return ((HEADS // ranks, ranks, blocks // ranks), (0, 2, 1))


def out_rows(table, rows):
    split, order = out_parts()
    ranks = lax.axis_size("seq")
    width = table.shape[1]
    whole = table.reshape(split + (ranks, rows, width))
    at = len(split)
    return whole.transpose(order + (at + 1, at, at + 2)).reshape(-1, ranks * width)


def gather_groups(block):
    return lax.all_gather(block, "dp", axis=0, tiled=True)


def swap_bit(block, axis, bit):
    return lax.ppermute(
        block, axis, [(place, place ^ (1 << bit)) for place in range(lax.axis_size(axis))]
    )


def bits_of(axis):
    return range(lax.axis_size(axis).bit_length() - 1)


def pair_kernel(lefts, rights, rows, kept, me_ref, *refs):
    left_refs, right_refs, rest = refs[:lefts], refs[lefts : lefts + rights], refs[lefts + rights :]
    side = lax.rem(me_ref[0], 2)
    blocks = []
    for number in range(left_refs[0].shape[1] // rows // 2):
        group = (me_ref[0] // 2 ^ number) * 2 + (side if kept else 1 - side)
        columns = pl.ds(pl.multiple_of(group * rows, rows), rows)
        blocks.append(jnp.concatenate([ref[:, columns] for ref in left_refs]))
    left, right = jnp.concatenate(blocks, axis=1), joined(right_refs)
    total = lax.dot_general(left, right, (((0,), (0,)), ((), ())), preferred_element_type=WIDE)
    if not kept:
        rest[0][...] = total.astype(LOW)
        return
    half = total.shape[1] // 2
    for number in range(len(blocks)):
        part = slice(number * rows, (number + 1) * rows)
        low = (total[part] + rest[0][part, :].astype(WIDE)).astype(LOW)
        rest[1 + number][...] = low[:, :half]
        rest[1 + len(blocks) + number][...] = low[:, half:]


def pair_product(lefts, rights, rows, got=None):
    groups, me = lax.axis_size("dp"), lax.axis_index("dp")
    pairs, width = groups // 2, rights[0].shape[1]
    kept = got is not None
    operands = [*lefts, *rights, *([got] if kept else [])]
    if kept:
        out_shape = [pltpu.HBM((rows, width // 2), LOW)] * (2 * pairs)
    else:
        out_shape = [pltpu.HBM((pairs * rows, width), LOW)]
    results = pl.pallas_call(
        partial(pair_kernel, len(lefts), len(rights), rows, kept),
        out_shape=out_shape,
        grid_spec=pltpu.PrefetchScalarGridSpec(
            num_scalar_prefetch=1,
            grid=(1,),
            in_specs=[whole_block(array) for array in operands],
            out_specs=[whole_block(result) for result in out_shape],
        ),
        compiler_params=pltpu.CompilerParams(vmem_limit_bytes=48 * 2**20),
        cost_estimate=SMALL,
        name="pair_product",
    )(me[None], *operands)
    return list(results) if kept else results[0]


GELU_SCALE = (2 / jnp.pi) ** 0.5
GELU_CUBE = 0.044715


def gelu_parts(value):
    square = value * value
    bent = jnp.tanh(GELU_SCALE * value * (1 + GELU_CUBE * square))
    slope = 0.5 * (1 + bent) + 0.5 * value * (1 - bent * bent) * GELU_SCALE * (
        1 + 3 * GELU_CUBE * square
    )
    return 0.5 * value * (1 + bent), slope


def joined(refs):
    return jnp.concatenate([ref[...] for ref in refs])


CHUNK = 256


def stream_kernel(work, inputs, results, *refs):
    weight_ref, operands = refs[0], refs[1 : 1 + inputs]
    result_refs, (held, sem, *total) = refs[1 + inputs : 1 + inputs + results], refs[1 + inputs + results :]
    copies = []
    for number in range(held.shape[1] // CHUNK):
        part = pl.ds(number * CHUNK, CHUNK)
        copies.append(
            pltpu.make_async_copy(weight_ref.at[:, part], held.at[:, part], sem.at[number])
        )
    for copy in copies:
        copy.start()
    for number, copy in enumerate(copies):
        copy.wait()
        columns = slice(number * CHUNK, (number + 1) * CHUNK)
        work(number, columns, held[:, columns], operands, result_refs, *total)


def stream(name, work, weight, extent, operands, results, total=None):
    shape = (weight.shape[0], extent)
    scratch = [pltpu.VMEM(shape, weight.dtype), pltpu.SemaphoreType.DMA((extent // CHUNK,))]
    if total is not None:
        scratch.append(pltpu.VMEM(total, WIDE))
    return pl.pallas_call(
        partial(stream_kernel, work, len(operands), len(results)),
        out_shape=results,
        grid=(1,),
        in_specs=[pl.BlockSpec(memory_space=pl.ANY)]
        + [pl.BlockSpec(array.shape, lambda number: (0, 0)) for array in operands],
        out_specs=[pl.BlockSpec(result.shape, lambda number: (0, 0)) for result in results],
        scratch_shapes=scratch,
        compiler_params=pltpu.CompilerParams(vmem_limit_bytes=32 * 2**20),
        cost_estimate=pl.CostEstimate(
            flops=2 * operands[0].shape[0] * shape[0] * shape[1],
            bytes_accessed=2 * shape[0] * shape[1],
            transcendentals=0,
        ),
        name=name,
    )(pltpu.with_memory_space_constraint(weight, pltpu.HBM), *operands)


def column_block(rows, wide):
    return pl.BlockSpec((rows, wide), lambda number: (0, number))


def project_kernel(left_ref, weight_ref, bias_ref, to_ref):
    total = jnp.dot(left_ref[...], weight_ref[...], preferred_element_type=WIDE)
    to_ref[...] = (total + bias_ref[...]).astype(to_ref.dtype)


def project(left, weight, bias):
    (rows, depth), width = left.shape, bias.shape[0]
    return pl.pallas_call(
        project_kernel,
        out_shape=jax.ShapeDtypeStruct((rows, width), LOW),
        grid=(width // CHUNK,),
        in_specs=[whole_block(left), column_block(depth, CHUNK), column_block(1, CHUNK)],
        out_specs=column_block(rows, CHUNK),
        compiler_params=pltpu.CompilerParams(vmem_limit_bytes=16 * 2**20),
        name="project",
    )(left, pltpu.with_memory_space_constraint(weight, pltpu.HBM), bias[None])


def upward_product(lefts, weight, bias):
    def work(number, columns, chunk, operands, results):
        total = jnp.dot(joined(operands[:-1]), chunk, preferred_element_type=WIDE)
        total = total + operands[-1][:, columns]
        results[0][:, columns] = total
        results[1][:, columns] = gelu_parts(total)[0].astype(LOW)

    rows, width = sum(left.shape[0] for left in lefts), weight.shape[1]
    results = [jax.ShapeDtypeStruct((rows, width), kind) for kind in (WIDE, LOW)]
    return stream("upward_product", work, weight, width, [*lefts, bias[None]], results)


def dense_kernel(lefts, *refs):
    weight_ref, reward_ref, reward_to_ref = refs[lefts], refs[lefts + 1], refs[-1]
    total = jnp.dot(joined(refs[:lefts]), weight_ref[...], preferred_element_type=WIDE)
    row = 0
    for to_ref in refs[lefts + 2 : -1]:
        to_ref[...] = total[row : row + to_ref.shape[0]].astype(LOW)
        row += to_ref.shape[0]
    scaled = total * reward_ref[...]
    part = scaled[:, :128]
    for start in range(128, scaled.shape[1], 128):
        part = part + scaled[:, start : start + 128]

    @pl.when(pl.program_id(0) == 0)
    def _():
        reward_to_ref[...] = part

    @pl.when(pl.program_id(0) > 0)
    def _():
        reward_to_ref[...] += part


def dense_product(lefts, weight, reward):
    depth, width = weight.shape
    rows = sum(left.shape[0] for left in lefts)
    return pl.pallas_call(
        partial(dense_kernel, len(lefts)),
        out_shape=[jax.ShapeDtypeStruct((left.shape[0], width), LOW) for left in lefts]
        + [jax.ShapeDtypeStruct((rows, 128), WIDE)],
        grid=(width // CHUNK,),
        in_specs=[whole_block(left) for left in lefts]
        + [column_block(depth, CHUNK), column_block(1, CHUNK)],
        out_specs=[column_block(left.shape[0], CHUNK) for left in lefts]
        + [pl.BlockSpec((rows, 128), lambda number: (0, 0))],
        compiler_params=pltpu.CompilerParams(vmem_limit_bytes=16 * 2**20),
        name="dense_product",
    )(*lefts, weight, reward[None])


def against_dot(left, weight):
    return lax.dot_general(left, weight, (((1,), (1,)), ((), ())), preferred_element_type=WIDE)


def against_stream(name, lefts, weight, operands, results, finish):
    rows, depth = sum(left.shape[0] for left in lefts), lefts[0].shape[1]

    def work(number, columns, chunk, operand_refs, result_refs, total):
        left = jnp.concatenate([ref[:, columns] for ref in operand_refs[: len(lefts)]])
        part = against_dot(left, chunk)
        total[...] = part if number == 0 else total[...] + part
        if number == depth // CHUNK - 1:
            finish(total, operand_refs[len(lefts) :], result_refs)

    shape = (rows, weight.shape[0])
    return stream(name, work, weight, depth, [*lefts, *operands], results, shape)


def column_sums(*values):
    sums = [jnp.sum(value, axis=0, keepdims=True) for value in values]
    return jnp.concatenate(sums + [jnp.zeros((8 - len(sums), sums[0].shape[1]), WIDE)])


def by_chunk(width):
    return [slice(start, start + CHUNK) for start in range(0, width, CHUNK)]


def second_kernel(down_ref, up_ref, left_ref, upward_ref, term_ref, low_ref, sums_ref, *scratch):
    down, up, down_sem, up_sem, total = scratch
    width = down.shape[1]
    copies = [
        [
            pltpu.make_async_copy(source.at[:, columns], held.at[:, columns], sem.at[number])
            for number, columns in enumerate(pl.ds(start, CHUNK) for start in range(0, width, CHUNK))
        ]
        for source, held, sem in ((down_ref, down, down_sem), (up_ref, up, up_sem))
    ]
    for copy in copies[0] + copies[1]:
        copy.start()
    for number, columns in enumerate(by_chunk(width)):
        copies[0][number].wait()
        part = against_dot(left_ref[:, columns], down[:, columns])
        total[...] = part if number == 0 else total[...] + part
    for number, columns in enumerate(by_chunk(width)):
        slope = gelu_parts(upward_ref[:, columns])[1]
        low = (total[:, columns] * slope).astype(LOW)
        low_ref[:, columns] = low
        sums_ref[:, columns] = column_sums(low.astype(WIDE))
        copies[1][number].wait()
        part = against_dot(low, up[:, columns])
        term_ref[...] = part if number == 0 else term_ref[...] + part


def second_product(left, weight_down, weight_up, upward):
    rows, width = upward.shape
    chunks = width // CHUNK
    results = [
        jax.ShapeDtypeStruct((rows, width), WIDE),
        jax.ShapeDtypeStruct((rows, width), LOW),
        jax.ShapeDtypeStruct((8, width), WIDE),
    ]
    return pl.pallas_call(
        second_kernel,
        out_shape=results,
        grid=(1,),
        in_specs=[pl.BlockSpec(memory_space=pl.ANY)] * 2
        + [pl.BlockSpec(array.shape, lambda number: (0, 0)) for array in (left, upward)],
        out_specs=[pl.BlockSpec(result.shape, lambda number: (0, 0)) for result in results],
        scratch_shapes=[pltpu.VMEM(weight.shape, LOW) for weight in (weight_down, weight_up)]
        + [pltpu.SemaphoreType.DMA((chunks,))] * 2
        + [pltpu.VMEM((rows, width), WIDE)],
        compiler_params=pltpu.CompilerParams(vmem_limit_bytes=48 * 2**20),
        cost_estimate=pl.CostEstimate(
            flops=4 * rows * width * width, bytes_accessed=4 * width * width, transcendentals=0
        ),
        name="second_product",
    )(
        *(pltpu.with_memory_space_constraint(weight, pltpu.HBM) for weight in (weight_down, weight_up)),
        left,
        upward,
    )


def against(lefts, weight, kind=WIDE):
    def finish(total, operands, results):
        results[0][...] = total[...].astype(kind)

    rows = sum(left.shape[0] for left in lefts)
    result = jax.ShapeDtypeStruct((rows, weight.shape[0]), kind)
    return against_stream("against", lefts, weight, [], [result], finish)[0]


def against_sums(left, weight, normal):
    def finish(total, operands, results):
        for columns in by_chunk(normal.shape[1]):
            value = total[:, columns]
            results[0][:, columns] = value
            results[1][:, columns] = column_sums(value * operands[0][:, columns], value)

    rows, width = normal.shape
    results = [jax.ShapeDtypeStruct((rows, width), WIDE), jax.ShapeDtypeStruct((8, width), WIDE)]
    return against_stream("against_sums", [left], weight, [normal], results, finish)


def masked_scores(query, key, queried_ref, keyed_ref, scale):
    scores = against_dot(query, key) * scale
    segment, place = queried_ref[:, 0:1], queried_ref[:, 1:2]
    other, before = keyed_ref[0:1, :], keyed_ref[1:2, :]
    allowed = ((other == 0) | (other == segment)) & (before <= place)
    return jnp.where(allowed, scores, MASKED)


def attend_kernel(scale, query_ref, key_ref, value_ref, queried_ref, keyed_ref, to_ref, log_ref):
    scores = masked_scores(query_ref[...], key_ref[...], queried_ref, keyed_ref, scale)
    highest = jnp.max(scores, axis=1, keepdims=True)
    exponent = jnp.exp(scores - highest)
    totals = jnp.sum(exponent, axis=1, keepdims=True)
    chances = (exponent / totals).astype(LOW)
    to_ref[...] = jnp.dot(chances, value_ref[...], preferred_element_type=WIDE).astype(LOW)
    log_ref[0] = highest + jnp.log(totals)


def head_blocks(length, wide, count):
    return [
        pl.BlockSpec((length, wide), lambda head, which=which: (0, which * count + head))
        for which in range(3)
    ]


def attend(projected, queried, keyed, wide, scale):
    length, columns = projected.shape
    count = columns // 3 // wide
    return pl.pallas_call(
        partial(attend_kernel, scale),
        out_shape=[
            jax.ShapeDtypeStruct((length, columns // 3), LOW),
            jax.ShapeDtypeStruct((count, length, 1), WIDE),
        ],
        grid=(count,),
        in_specs=head_blocks(length, wide, count)
        + [
            pl.BlockSpec((length, 2), lambda head: (0, 0)),
            pl.BlockSpec((2, length), lambda head: (0, 0)),
        ],
        out_specs=[
            pl.BlockSpec((length, wide), lambda head: (0, head)),
            pl.BlockSpec((1, length, 1), lambda head: (head, 0, 0)),
        ],
        compiler_params=pltpu.CompilerParams(vmem_limit_bytes=24 * 2**20),
        name="attend",
    )(projected, projected, projected, queried, keyed)


def attend_back_kernel(
    scale,
    count,
    query_ref,
    key_ref,
    value_ref,
    queried_ref,
    keyed_ref,
    log_ref,
    grad_ref,
    to_ref,
    sums_ref,
):
    query, key, grad = query_ref[...], key_ref[...], grad_ref[...]
    wide = query.shape[1]
    scores = masked_scores(query, key, queried_ref, keyed_ref, scale)
    chances = jnp.exp(scores - log_ref[0])
    chance_grad = against_dot(grad, value_ref[...])
    weighted = jnp.sum(chances * chance_grad, axis=1, keepdims=True)
    score_grad = (chances * (chance_grad - weighted)).astype(LOW)

    def across(left, right):
        return lax.dot_general(left, right, (((0,), (0,)), ((), ())), preferred_element_type=WIDE)

    grads = (
        jnp.dot(score_grad, key, preferred_element_type=WIDE) * scale,
        across(score_grad, query) * scale,
        across(chances.astype(LOW), grad),
    )
    for which, value in enumerate(grads):
        low = value.astype(LOW)
        start = pl.multiple_of((which * count + pl.program_id(0)) * wide, wide)
        to_ref[:, pl.ds(start, wide)] = low
        sums_ref[:, pl.ds(start, wide)] = column_sums(low.astype(WIDE))


def attend_back(projected, queried, keyed, log_rows, grad, wide, scale):
    length, columns = projected.shape
    count = columns // 3 // wide
    return pl.pallas_call(
        partial(attend_back_kernel, scale, count),
        out_shape=[
            jax.ShapeDtypeStruct((length, columns), LOW),
            jax.ShapeDtypeStruct((8, columns), WIDE),
        ],
        grid=(count,),
        in_specs=head_blocks(length, wide, count)
        + [
            pl.BlockSpec((length, 2), lambda head: (0, 0)),
            pl.BlockSpec((2, length), lambda head: (0, 0)),
            pl.BlockSpec((1, length, 1), lambda head: (head, 0, 0)),
            pl.BlockSpec((length, wide), lambda head: (0, head)),
        ],
        out_specs=[
            pl.BlockSpec((length, columns), lambda head: (0, 0)),
            pl.BlockSpec((8, columns), lambda head: (0, 0)),
        ],
        compiler_params=pltpu.CompilerParams(vmem_limit_bytes=32 * 2**20),
        name="attend_back",
    )(projected, projected, projected, queried, keyed, log_rows, grad)


SMALL = pl.CostEstimate(flops=1 << 30, bytes_accessed=1 << 22, transcendentals=0)


def whole_block(array):
    return pl.BlockSpec(array.shape, lambda *_: (0, 0), pipeline_mode=pl.Buffered(1))


def rows_kernel(lefts, *refs):
    left, right = joined(refs[:lefts]), joined(refs[lefts:-1])
    total = lax.dot_general(left, right, (((0,), (0,)), ((), ())), preferred_element_type=WIDE)
    refs[-1][...] = total.astype(LOW)


def rows_product(lefts, rights):
    rows, width = lefts[0].shape[1], rights[0].shape[1]
    wide = 512
    if rows % wide:
        return inner_rows(jnp.concatenate(lefts), jnp.concatenate(rights)).astype(LOW)
    return pl.pallas_call(
        partial(rows_kernel, len(lefts)),
        out_shape=pltpu.HBM((rows, width), LOW),
        grid=(rows // wide,),
        in_specs=[pl.BlockSpec((left.shape[0], wide), lambda number: (0, number)) for left in lefts]
        + [
            pl.BlockSpec(right.shape, lambda number: (0, 0), pipeline_mode=pl.Buffered(1))
            for right in rights
        ],
        out_specs=pl.BlockSpec((wide, width), lambda number: (number, 0)),
        compiler_params=pltpu.CompilerParams(vmem_limit_bytes=32 * 2**20),
        cost_estimate=pl.CostEstimate(
            flops=4 * rows * width * sum(left.shape[0] for left in lefts),
            bytes_accessed=4 * rows * width,
            transcendentals=0,
        ),
        name="rows_product",
    )(*lefts, *rights)


def scatter_product(lefts, rights):
    return scatter_groups(rows_product(lefts, rights))


def scatter_groups(table):
    return lax.psum_scatter(table, "dp", scatter_dimension=0, tiled=True)


def out_columns(left, rows):
    split, order = out_parts()
    count = left.shape[0]
    back = tuple(1 + order.index(axis) for axis in range(len(order)))
    moved = left.reshape((count,) + tuple(split[axis] for axis in order) + (rows,))
    return moved.transpose((0,) + back + (1 + len(split),)).reshape(count, -1)


def pair_onward(pieces):
    return [swap_bit(pieces[3], "dp", 1), swap_bit(pieces[7], "dp", 2)]


def sums_kernel(counts, *refs):
    at = 0
    for count, to_ref in zip(counts, refs[sum(counts) :]):
        total = refs[at][...].astype(WIDE)
        for ref in refs[at + 1 : at + count]:
            total = total + ref[...].astype(WIDE)
        to_ref[...] = total.astype(LOW)
        at += count


def sums_of(*groups):
    rows, width = groups[0][0].shape
    block = pl.BlockSpec((rows // 2, width), lambda number: (number, 0))
    return pl.pallas_call(
        partial(sums_kernel, [len(group) for group in groups]),
        out_shape=[jax.ShapeDtypeStruct((rows, width), LOW)] * len(groups),
        grid=(2,),
        in_specs=[block] * sum(len(group) for group in groups),
        out_specs=[block] * len(groups),
        cost_estimate=SMALL,
        name="sums_of",
    )(*(array for group in groups for array in group))


def pair_second(pieces, onward):
    return sums_of([pieces[2], onward[0]], [pieces[5], onward[1]])


def pair_last(sent):
    return [swap_bit(sent[0], "dp", 2), swap_bit(sent[1], "dp", 1)]


def pair_staying(pieces):
    return [swap_bit(pieces[1], "dp", 1), swap_bit(pieces[6], "dp", 2)]


def pair_sum(pieces, staying, second):
    groups = zip((pieces[0], pieces[4]), staying, second)
    return jnp.concatenate(sums_of(*(list(group) for group in groups)), axis=1)


def rank_rows(table, rows):
    ranks, me = lax.axis_size("seq"), lax.axis_index("seq")
    return [
        lax.dynamic_slice_in_dim(table, (me + shift) % ranks * rows, rows, 0)
        for shift in range(ranks)
    ]


def swap_rank(block, shift):
    size = lax.axis_size("seq")
    return lax.ppermute(block, "seq", [(place, (place + shift) % size) for place in range(size)])


def swap_ranks(blocks):
    return [blocks[0]] + [swap_rank(blocks[shift], shift) for shift in range(1, len(blocks))]


def rows_by_rank(blocks, beside=None):
    ranks, me = len(blocks), lax.axis_index("seq")
    rows, width = blocks[0].shape
    sources = [(number, 0, rows, 0, width, 0) for number in range(ranks)]
    to_rows = [(me + ranks - number) % ranks * rows for number in range(ranks)]
    arrays, more = list(blocks), 0
    if beside is not None:
        more = beside.shape[1] // ranks
        sources += [(ranks, 0, rows, number * more, more, width) for number in range(ranks)]
        to_rows += [number * rows for number in range(ranks)]
        arrays.append(beside)
    return place(arrays, sources, jnp.stack([jnp.int32(row) for row in to_rows]), (ranks * rows, width + more))


def by_number(blocks):
    return to_ring(jnp.stack(blocks))


def small_order():
    groups, ranks = lax.axis_size("dp"), lax.axis_size("seq")
    number = jnp.arange(groups * ranks)
    place = ((number // ranks) ^ lax.axis_index("dp")) * ranks + (
        (number % ranks) ^ lax.axis_index("seq")
    )
    return (place[:, None] == number[None, :]).astype(WIDE)


def small_groups(table):
    for bit in reversed(bits_of("dp")):
        half = table.shape[0] // 2
        table = table[:half] + swap_bit(table[half:], "dp", bit)
    return table


def small_ranks(table):
    size, me = lax.axis_size("seq"), lax.axis_index("seq")
    total = table[0]
    for shift in range(1, size):
        sent = lax.dynamic_index_in_dim(table, me ^ ((me + shift) % size), 0, keepdims=True)
        perm = [(place, (place + shift) % size) for place in range(size)]
        total = total + lax.ppermute(sent, "seq", perm)[0]
    return total


def small_rows(table):
    return jnp.dot(
        small_order().T, table, precision=lax.Precision.HIGHEST, preferred_element_type=WIDE
    )


def sum_ranks(table):
    size = lax.axis_size("seq")
    total = table
    for shift in range(1, size):
        total = total + lax.ppermute(
            table, "seq", [(place, (place + shift) % size) for place in range(size)]
        )
    return total


def spread_path(
    inputs,
    cotangent,
    segments,
    labels,
    step_ends,
    attend_gain,
    attend_shift,
    project_in,
    project_bias,
    project_out,
    output_bias,
    dense_gain,
    dense_shift,
    up_weight,
    up_bias,
    down_weight,
    down_bias,
    reward_weight,
):
    groups, ranks = lax.axis_size("dp"), lax.axis_size("seq")
    rank = lax.axis_index("seq")
    rows_here, places_here, width = inputs.shape
    all_rows = rows_here * groups
    head_width = width // HEADS
    heads_here = HEADS // ranks
    share = heads_here * head_width
    rows_in = project_in.shape[0]
    hidden_here = down_weight.shape[0]
    length = ranks * places_here
    score_scale = head_width ** (-0.5)

    small = (
        attend_gain,
        attend_shift,
        project_bias,
        output_bias,
        dense_gain,
        dense_shift,
        up_bias,
        down_bias,
        reward_weight,
    )
    sizes = [vector.shape[0] for vector in small]
    riders = [vector.reshape(-(-vector.shape[0] // 128), -1) for vector in small]
    riders += [segments, labels, step_ends]
    dealt_in = deal(project_in, head_pieces, head_width, riders)
    came_in = swap_ranks(dealt_in)
    out_moved = lax.ppermute(after(project_out, dealt_in), EVERY, out_route())
    rows_in_all = rows_by_rank(came_in, out_moved)
    gathered = gather_groups(rows_in_all)
    inputs_ring = ring_gather(
        after(inputs[0], came_in), [idle, idle, idle]
    )
    first_normals = []
    for halves in inputs_ring:
        normal, inverse = normal_parts(jnp.concatenate(halves).astype(WIDE))
        if not first_normals:
            first_inverse = inverse
        first_normals.append(normal)
    dealt_up = deal(after(up_weight, [rows_in_all]), hidden_pieces, hidden_here)
    came_up = swap_ranks(after(dealt_up, inputs_ring[-1]))
    gathered = after(gathered, first_normals)
    rows_up_all = rows_by_rank(came_up)
    weight_up = gather_groups(rows_up_all)
    weight_down = gather_groups(after(down_weight, [rows_up_all]))
    riders = gathered[:, 3 * share : 3 * share + 128]
    lines_all = sum(-(-size // 128) for size in sizes) + 3
    lines_all = -(-lines_all // 8) * 8
    riders = riders.reshape(groups * ranks, rows_in, 128)[:, :lines_all].astype(WIDE)
    vectors = []
    row = 0
    for size in sizes + [places_here] * 3:
        lines = -(-size // 128)
        vectors.append(
            riders[:, row : row + lines].reshape(groups * ranks, -1)[:, :size].reshape(-1)
        )
        row += lines
    gain_one, shift_one, bias_in, bias_out, gain_two, shift_two, bias_up, bias_down, reward_wide = (
        vectors[: len(sizes)]
    )

    held = own_heads()
    bias_heads = exact(held, bias_in.reshape(2, HEADS, head_width).transpose(1, 0, 2).reshape(HEADS, -1))
    bias_heads = bias_heads.reshape(heads_here, 2, head_width)
    bias_full = jnp.concatenate(
        [bias_heads[:, 0].reshape(-1), jnp.zeros((share,), WIDE), bias_heads[:, 1].reshape(-1)]
    )
    bias_up_here = lax.dynamic_index_in_dim(
        bias_up.reshape(groups, ranks, hidden_here), rank, 1, keepdims=False
    ).reshape(-1)
    marks = jnp.stack(
        [
            lax.dynamic_index_in_dim(
                mark.reshape(groups, ranks, places_here), lax.axis_index("dp"), 0, keepdims=False
            )
            for mark in vectors[len(sizes) :]
        ],
        axis=1,
    )
    marks_ring = to_ring(marks)
    segments_ring = marks_ring[:, 0].reshape(-1)
    places_ring = to_ring(jnp.arange(length).reshape(ranks, places_here)).reshape(-1)

    own = inputs[0].astype(WIDE)
    firsts = [(normal * gain_one + shift_one).astype(LOW) for normal in first_normals]
    projected = project(jnp.concatenate(firsts), gathered, bias_full)
    gathered, projected = lax.optimization_barrier((gathered, projected))
    weight_out = out_rows(gathered[:, 3 * share + 128 :], rows_in)
    queried, keyed = (
        jnp.stack([segments_ring.astype(WIDE), places_ring.astype(WIDE)], axis=axis)
        for axis in (1, 0)
    )
    mixture, log_rows = attend(projected, queried, keyed, head_width, score_scale)

    def block_of(array, k):
        return array[k * places_here : (k + 1) * places_here]

    weight_back = None

    def contiguous(gate):
        nonlocal weight_back
        weight_back = after(gathered, gate)[:, : 3 * share]
        return [weight_back]

    mixture_out = None

    def in_blocks(gate):
        nonlocal mixture_out
        mixture_out = out_columns(after(mixture, gate), project_out.shape[0])
        return [mixture_out]

    branch = ring_sum(
        lambda k, gate: product(block_of(mixture, k), weight_out), [contiguous, in_blocks, idle]
    )
    weight_back, mixture_out = lax.optimization_barrier((weight_back, mixture_out))
    hidden = own + branch + bias_out

    second_normal, second_inverse = normal_parts(hidden)
    second_value = second_normal * gain_two + shift_two

    rows_all = ranks * rows_in
    fenced = groups == 8 and rows_all % 128 == 0
    steady = (segments[0, 0] | 1) != 0

    def step(work, *operands):
        return fence(steady, work, *operands) if fenced else work(*operands)

    def upward_of(k, halves):
        return upward_product(halves, weight_up, bias_up_here)

    seconds, found = ring_gather(second_value.astype(LOW), use=upward_of, plan=(1, 1, 1))

    def dense_one(halves, block):
        return upward_of(None, halves), ring_move([block])[0]

    def dense_two(activated, block):
        return dense_product(activated, weight_down, reward_wide), ring_move([block])[0]

    cotangents = [cotangent[0]]
    last, block = step(dense_one, seconds[-1], cotangents[-1])
    cotangents.append(block)
    upwards, activated = map(list, zip(*found, last))
    (*dense_parts, reward_lanes), block = step(dense_two, activated, cotangents[-1])
    cotangents.append(block)
    dense_parts = lax.optimization_barrier(dense_parts)
    reward_parts = list(jnp.sum(reward_lanes, axis=-1).reshape(ranks, places_here))

    reward_parts[0] = reward_parts[0] + jnp.sum((hidden + bias_down) * reward_wide, axis=-1)
    rewards_all = sum_ranks(to_ring(jnp.stack(reward_parts)))
    scored = marks[:, 2] * (marks[:, 0] > 0)
    error_all = scored * (jax.nn.sigmoid(rewards_all) - marks[:, 1]) / all_rows
    error_ring = to_ring(error_all)
    rewards = lax.dynamic_index_in_dim(rewards_all, rank, 0, keepdims=False)

    def dense_grad(block, k):
        return block.astype(WIDE) + error_ring[k][:, None] * reward_wide

    dense_lows = [dense_grad(block, k).astype(LOW) for k, block in enumerate(cotangents)]

    def second_part(k, dense_low):
        term, *low = second_product(dense_low, weight_down, weight_up, upwards[k])
        return term, tuple(low)

    def second_first(block, dense_low):
        term, upward_low = second_part(1, dense_low)
        return term.astype(LOW), upward_low, ring_move([block])[0]

    def second_step(k, sent, dense_low):
        moved = ring_move([sent])[0]
        term, upward_low = second_part(k, dense_low)
        total = moved.astype(WIDE) + term
        return total if k == 0 else total.astype(LOW), upward_low

    upward_lows = [None] * ranks
    sent, upward_lows[1], block = step(second_first, cotangents[-1], dense_lows[1])

    def second_next(sent, block):
        dense_low = dense_grad(block, ranks - 1).astype(LOW)
        table = rows_product(activated, [*dense_lows, dense_low])
        return second_step(2, sent, dense_lows[2]), dense_low, table

    (sent, upward_lows[2]), dense_low, down_table = step(second_next, sent, block)
    dense_lows.append(dense_low)
    down_summed = scatter_groups(down_table)
    for k in list(range(3, ranks)) + [0]:
        sent, upward_lows[k] = step(partial(second_step, k), sent, dense_lows[k])
    second_grad = sent
    result_grad = after(dense_grad(cotangents[0], 0), [sent])
    upward_lows, upward_sums = zip(*upward_lows)
    reward_weight_gradient = jnp.sum(error_ring[0][:, None] * (hidden + bias_down), axis=0)
    for k, part in enumerate(dense_parts):
        reward_weight_gradient += jnp.sum(error_ring[k][:, None] * part.astype(WIDE), axis=0)
    down_bias_gradient = jnp.sum(dense_lows[0].astype(WIDE), axis=0)
    up_bias_gradient = sum(upward_sums)[0]
    dense_gain_gradient = jnp.sum(second_grad * second_normal, axis=0)
    dense_shift_gradient = jnp.sum(second_grad, axis=0)
    hidden_grad = result_grad + normalize_back(second_grad, second_normal, second_inverse, gain_two)

    branch_low = hidden_grad.astype(LOW)
    seconds = sum(seconds, [])
    output_bias_gradient = jnp.sum(branch_low.astype(WIDE), axis=0)

    def by_device(vectors):
        return jnp.concatenate([vector.reshape(groups * ranks, -1) for vector in vectors], axis=1)

    def early_table():
        up_bias_all = lax.dynamic_update_index_in_dim(
            jnp.zeros((groups, ranks, hidden_here), WIDE),
            up_bias_gradient.reshape(groups, hidden_here),
            rank,
            1,
        )
        return by_device(
            (
                output_bias_gradient,
                dense_gain_gradient,
                dense_shift_gradient,
                up_bias_all,
                down_bias_gradient,
                reward_weight_gradient,
            )
        )

    def back(mixture_grad):
        return attend_back(
            projected, queried, keyed, log_rows, mixture_grad, head_width, score_scale
        )

    def first_part(projected_grad, k):
        return against_sums(block_of(projected_grad, k), weight_back, first_normals[k])

    def inputs_back(first_grad):
        return hidden_grad + normalize_back(
            first_grad, first_normals[0], first_inverse, gain_one
        )

    def small_table(bias_sums, first_sums, early):
        bias_heads = jnp.concatenate([bias_sums[0, :share], bias_sums[0, 2 * share :]])
        bias_heads = bias_heads.reshape(2, heads_here, head_width)
        bias_all = jnp.concatenate(
            [exact(held.T, bias_heads[which]).reshape(-1) for which in range(2)]
        )
        gain_sum, shift_sum = sum(first_sums)[:2]
        return jnp.concatenate([by_device((gain_sum, shift_sum, bias_all)), early], axis=1)

    def out_back(out_summed):
        back = [(there, here) for here, there in out_route()]
        return lax.ppermute(out_summed, EVERY, back).astype(WIDE)

    def result_back(dense_sum):
        return (hidden + dense_sum + bias_down).astype(LOW)

    def sent_rows(summed):
        return rank_rows(summed.astype(LOW), rows_in)

    if fenced:

        def gather_one(block):
            return ring_move([block])[0], pair_product(seconds, upward_lows, rows_all)

        def gather_two(block, up_sent):
            return ring_move([block])[0], swap_bit(up_sent, "dp", 0), early_table()

        def gather_three(block, up_got):
            return ring_move([block])[0], pair_product(seconds, upward_lows, rows_all, up_got)

        def attend_one(branch_lows, up_pieces):
            dense_sum = ring_step(dense_parts[1], dense_parts[2])
            up_second = pair_second(up_pieces, pair_onward(up_pieces))
            mixture_grad = against(branch_lows, weight_out, LOW)
            out_table = rows_product([mixture_out], branch_lows)
            return dense_sum, up_second, mixture_grad, out_table

        def attend_two(dense_sum, up_second, mixture_grad):
            dense_sum = ring_step(dense_sum, dense_parts[3])
            return dense_sum, pair_last(up_second), back(mixture_grad)

        def attend_three(dense_sum, up_pieces, projected_grad):
            dense_sum = ring_step(dense_sum, dense_parts[0], WIDE)
            up_staying = pair_staying(up_pieces)
            in_sent = pair_product(firsts, [projected_grad], rows_all)
            term, sums = first_part(projected_grad, 1)
            return result_back(dense_sum), up_staying, in_sent, term.astype(LOW), sums

        def first_one(sent, in_sent, projected_grad, up_pieces, up_staying, up_second):
            moved = ring_move([sent])[0]
            in_got = swap_bit(in_sent, "dp", 0)
            term, sums = first_part(projected_grad, 2)
            up_sent = sent_rows(pair_sum(up_pieces, up_staying, up_second))
            in_pieces = list(pair_product(firsts, [projected_grad], rows_all, in_got))
            moved = after(moved, in_pieces)
            return (moved.astype(WIDE) + term).astype(LOW), in_pieces, up_sent, sums

        def first_two(sent, in_pieces, projected_grad, bias_sums, first_sums, early, up_near):
            moved = ring_move([sent])[0]
            in_staying, in_onward = pair_staying(in_pieces), pair_onward(in_pieces)
            in_second = pair_second(in_pieces, in_onward)
            up_near = swap_rank(after(up_near, in_onward[:1]), near[0])
            term, sums = first_part(projected_grad, 3)
            last_term, last_sums = first_part(projected_grad, 0)
            table = small_rows(small_table(bias_sums, [sums, last_sums, *first_sums], early))
            sent = (moved.astype(WIDE) + term).astype(LOW)
            return sent, in_staying, in_second, up_near, last_term, table

        def first_three(sent, in_pieces, in_staying, in_second, term, table, up_far):
            moved = ring_move([sent])[0]
            up_far = swap_rank(up_far, far)
            in_second = pair_last(in_second)
            summed = small_ranks(small_groups(after(table, in_second[:1])))
            in_sent = sent_rows(pair_sum(in_pieces, in_staying, in_second))
            moved, up_far = after((moved, up_far), [up_far])
            return moved.astype(WIDE) + term, in_sent, summed, up_far

        def last(in_sent, came_up, up_near, first_grad):
            for shift, block in zip(near[1:], up_near):
                came_up[shift] = swap_rank(block, shift)
            came_up = [came_up[shift] for shift in range(ranks)]
            came_in = swap_ranks(in_sent)
            first_grad, down_late = after((first_grad, down_early), [came_in[1]])
            done = inputs_back(first_grad), down_late.astype(WIDE), out_back(out_early)
            came_in, came_up, done = lax.optimization_barrier((came_in, came_up, done))
            return (
                collect(came_in, head_pieces, head_width),
                collect(came_up, hidden_pieces, hidden_here),
                *done,
            )

        branch_lows = [branch_low]
        moved, up_sent = step(gather_one, branch_low)
        branch_lows.append(moved)
        moved, up_got, early = step(gather_two, moved, up_sent)
        branch_lows.append(moved)
        moved, up_pieces = step(gather_three, moved, up_got)
        branch_lows.append(moved)
        dense_sum, up_second, mixture_grad, out_table = step(attend_one, branch_lows, up_pieces)
        out_summed = scatter_groups(out_table)
        dense_sum, up_second, (projected_grad, bias_sums) = step(
            attend_two, dense_sum, up_second, mixture_grad
        )
        result_low, up_staying, in_sent, sent, sums_one = step(
            attend_three, dense_sum, up_pieces, projected_grad
        )
        sent, down_early = after((sent, down_summed), [down_summed])
        sent, in_pieces, up_sent, sums_two = step(
            first_one, sent, in_sent, projected_grad, up_pieces, up_staying, up_second
        )
        far = ranks // 2
        near = [shift for shift in range(1, ranks) if shift != far]
        sent, in_staying, in_second, up_near, last_term, table = step(
            first_two,
            sent,
            in_pieces,
            projected_grad,
            bias_sums,
            [sums_one, sums_two],
            early,
            up_sent[near[0]],
        )
        sent, out_early = after((sent, out_summed), [out_summed])
        first_grad, in_sent, summed, up_far = step(
            first_three, sent, in_pieces, in_staying, in_second, last_term, table, up_sent[far]
        )
        came_up = {0: up_sent[0], far: up_far, near[0]: up_near}
        up_near = [up_sent[shift] for shift in near[1:]]
        (
            project_in_gradient,
            up_weight_gradient,
            inputs_gradient,
            down_weight_gradient,
            project_out_gradient,
        ) = step(last, in_sent, came_up, up_near, first_grad)
    else:
        branch_lows = sum(ring_gather(branch_low, cut=1), [])
        projected_grad, bias_sums = back(against(branch_lows, weight_out, LOW))
        out_summed = scatter_groups(rows_product([mixture_out], branch_lows))
        first_sums = [None] * ranks

        def first_term(k, gate):
            term, first_sums[k] = first_part(projected_grad, k)
            return term

        first_grad = ring_sum(first_term, cut=1)
        dense_sum = dense_parts[1]
        for part in dense_parts[2:] + dense_parts[:1]:
            dense_sum = ring_step(dense_sum, part, WIDE)
        up_summed = scatter_product(seconds, upward_lows)
        in_summed = scatter_product(firsts, [projected_grad])
        inputs_gradient, result_low = inputs_back(first_grad), result_back(dense_sum)
        table = small_rows(small_table(bias_sums, first_sums, early_table()))
        summed = small_ranks(small_groups(table))
        up_weight_gradient = collect(swap_ranks(sent_rows(up_summed)), hidden_pieces, hidden_here)
        project_in_gradient = collect(swap_ranks(sent_rows(in_summed)), head_pieces, head_width)
        project_out_gradient = out_back(out_summed)
        down_weight_gradient = down_summed.astype(WIDE)
    parts = []
    start = 0
    for size in sizes:
        parts.append(summed[start : start + size])
        start += size
    return (
        result_low[None],
        rewards[None],
        inputs_gradient[None],
        parts[0],
        parts[1],
        project_in_gradient,
        parts[2],
        project_out_gradient,
        parts[3],
        parts[4],
        parts[5],
        up_weight_gradient,
        parts[6],
        down_weight_gradient,
        parts[7],
        parts[8],
    )


def solution(mesh):
    row = P("dp", "seq")
    wide_row = P("dp", "seq", None)
    vector = P(("dp", "seq"))
    matrix = P(("dp", "seq"), None)
    in_specs = (
        wide_row,
        wide_row,
        row,
        row,
        row,
        vector,
        vector,
        matrix,
        vector,
        matrix,
        vector,
        vector,
        vector,
        matrix,
        vector,
        matrix,
        vector,
        vector,
    )
    out_specs = (
        wide_row,
        row,
        wide_row,
        vector,
        vector,
        matrix,
        vector,
        matrix,
        vector,
        vector,
        vector,
        matrix,
        vector,
        matrix,
        vector,
        vector,
    )
    return jax.shard_map(
        spread_path, mesh=mesh, in_specs=in_specs, out_specs=out_specs, check_vma=False
    )
```

```python
from functools import partial

import jax
import jax.numpy as jnp
from jax import lax
from jax.experimental import pallas as pl
from jax.experimental.pallas import tpu as pltpu
from jax.sharding import PartitionSpec as P

HEADS = 16
EPSILON = 1e-05
MASKED = -1e30
LOW = jnp.bfloat16
WIDE = jnp.float32
EVERY = ("dp", "seq")


def product(left, right):
    return jnp.dot(left, right, preferred_element_type=WIDE)


def inner_rows(left, right):
    return jnp.einsum("ta,tb->ab", left, right, preferred_element_type=WIDE)


def against_rows(left, right):
    return jnp.einsum("tb,ab->ta", left, right, preferred_element_type=WIDE)


def normal_parts(field):
    center = field - jnp.mean(field, axis=-1, keepdims=True)
    spread = jnp.mean(center * center, axis=-1, keepdims=True)
    inverse = lax.rsqrt(spread + EPSILON)
    return center * inverse, inverse


def normalize_back(upstream, normal, inverse, gain):
    scaled = upstream * gain
    mean_scaled = jnp.mean(scaled, axis=-1, keepdims=True)
    mean_cross = jnp.mean(scaled * normal, axis=-1, keepdims=True)
    return inverse * (scaled - mean_scaled - normal * mean_cross)


def ring_next():
    size = lax.axis_size("seq")
    return [(place, (place + 1) % size) for place in range(size)]


def after(value, done):
    return lax.optimization_barrier((value, tuple(done)))[0]


def fence(steady, work, *operands):
    shapes = jax.eval_shape(work, *operands)
    return lax.cond(
        steady,
        work,
        lambda *_: jax.tree.map(lambda shape: jnp.zeros(shape.shape, shape.dtype), shapes),
        *operands,
    )


def idle(gate):
    return []


def pieces_of(block, cut):
    rows = block.shape[0] // cut
    return [block[piece * rows : (piece + 1) * rows] for piece in range(cut)]


def ring_move(halves):
    return [lax.ppermute(half, "seq", ring_next()) for half in halves]


def ring_gather(block, flights=(idle,) * 3, use=None, plan=(), cut=2):
    blocks, results = [pieces_of(block, cut)], []
    for k in range(lax.axis_size("seq") - 1):
        moved = ring_move(blocks[-1])
        done = []
        if use is not None:
            for _ in range(plan[k]):
                results.append(use(len(results), blocks[len(results)]))
                done += jax.tree.leaves(results[-1])
        done += flights[k](blocks[-1])
        if done:
            moved[-1] = after(moved[-1], done)
        blocks.append(moved)
    return blocks if use is None else (blocks, results)


def ring_sum(part, flights=(idle,) * 3, cut=2):
    size = lax.axis_size("seq")
    sent = pieces_of(part(1, ()).astype(LOW), cut)
    for step, k in enumerate(list(range(2, size)) + [0]):
        kind = LOW if step < size - 2 else WIDE
        moved = ring_move(sent)
        term = part(k, sent)
        done = [term] + flights[step](sent)
        total = []
        for piece, (came, own) in enumerate(zip(moved, pieces_of(term, cut))):
            came = after(came, total + (done if piece == cut - 1 else []))
            total.append((came.astype(WIDE) + own).astype(kind))
        sent = total
    return jnp.concatenate(sent) if cut > 1 else sent[0]


def ring_step(total, part, kind=LOW):
    moved = lax.ppermute(total.astype(LOW), "seq", ring_next())
    return (moved.astype(WIDE) + part.astype(WIDE)).astype(kind)


def deal_kernel(pieces, wide, riders, me_ref, from_ref, *refs):
    rider_refs, to_refs, packed = refs[:riders], refs[riders:-1], refs[-1]
    ranks = len(to_refs)
    columns = from_ref.shape[1] // ranks
    if riders:
        packed[...] = jnp.zeros_like(packed)
        row = 0
        for rider_ref in rider_refs:
            lines, width = rider_ref.shape
            packed[row : row + lines, :width] = rider_ref[...].astype(WIDE)
            row += lines
    for shift, to_ref in enumerate(to_refs):
        to = lax.rem(me_ref[0] + shift, ranks)
        for place in range(columns // wide):
            start = pl.multiple_of(pieces(to, place) * wide, wide)
            to_ref[:, place * wide : (place + 1) * wide] = from_ref[:, pl.ds(start, wide)]
        if riders:
            to_ref[:, columns:] = packed[...].astype(to_ref.dtype)


def deal(matrix, pieces, wide, riders=()):
    ranks, me = lax.axis_size("seq"), lax.axis_index("seq")
    rows, columns = matrix.shape
    if wide % 128 == 0:
        each = columns // ranks + (128 if riders else 0)
        return pl.pallas_call(
            partial(deal_kernel, pieces, wide, len(riders)),
            out_shape=[jax.ShapeDtypeStruct((rows, each), matrix.dtype)] * ranks,
            grid_spec=pltpu.PrefetchScalarGridSpec(
                num_scalar_prefetch=1,
                grid=(1,),
                in_specs=[pl.BlockSpec((rows, columns), lambda i, me: (0, 0))]
                + [pl.BlockSpec(rider.shape, lambda i, me: (0, 0)) for rider in riders],
                out_specs=[pl.BlockSpec((rows, each), lambda i, me: (0, 0))] * ranks,
                scratch_shapes=[pltpu.VMEM((rows, 128), WIDE)],
            ),
            name="deal",
        )(me[None], matrix, *riders)
    dealt = jnp.stack(
        [
            jnp.concatenate(
                [
                    matrix[:, pieces(to, place) * wide :][:, :wide]
                    for place in range(columns // ranks // wide)
                ],
                axis=1,
            )
            for to in range(ranks)
        ]
    )
    return [
        lax.dynamic_index_in_dim(dealt, (me + shift) % ranks, 0, keepdims=False)
        for shift in range(ranks)
    ]


def collect_kernel(pieces, wide, me_ref, *refs):
    from_refs, to_ref = refs[:-1], refs[-1]
    ranks = len(from_refs)
    for shift, from_ref in enumerate(from_refs):
        source = lax.rem(me_ref[0] + ranks - shift, ranks)
        for place in range(from_ref.shape[1] // wide):
            start = pl.multiple_of(pieces(source, place) * wide, wide)
            to_ref[:, pl.ds(start, wide)] = from_ref[:, place * wide : (place + 1) * wide].astype(
                to_ref.dtype
            )


def collect(blocks, pieces, wide):
    ranks, me = lax.axis_size("seq"), lax.axis_index("seq")
    rows, columns = blocks[0].shape
    if wide % 128 == 0:
        return pl.pallas_call(
            partial(collect_kernel, pieces, wide),
            out_shape=jax.ShapeDtypeStruct((rows, columns * ranks), WIDE),
            grid_spec=pltpu.PrefetchScalarGridSpec(
                num_scalar_prefetch=1,
                grid=(1,),
                in_specs=[pl.BlockSpec((rows, columns), lambda i, me: (0, 0))] * ranks,
                out_specs=pl.BlockSpec((rows, columns * ranks), lambda i, me: (0, 0)),
            ),
            name="collect",
        )(me[None], *blocks)
    held = by_number(blocks)
    found = {
        pieces(to, place): held[to, :, place * wide : (place + 1) * wide]
        for to in range(ranks)
        for place in range(columns // wide)
    }
    return jnp.concatenate([found[piece] for piece in sorted(found)], axis=1).astype(WIDE)


def place_kernel(sources, to_row_ref, *refs):
    held, in_sem, out_sem = refs[-3:]
    from_refs, to_ref = refs[:-4], refs[-4]
    loads, stores = [], []
    at = 0
    for number, (array, row, rows, column, width, to_column) in enumerate(sources):
        start = pl.multiple_of(to_row_ref[number], rows)
        piece = held.at[pl.ds(at, rows), pl.ds(0, width)]
        source = from_refs[array].at[pl.ds(row, rows), pl.ds(column, width)]
        target = to_ref.at[pl.ds(start, rows), pl.ds(to_column, width)]
        loads.append(pltpu.make_async_copy(source, piece, in_sem.at[number]))
        stores.append(pltpu.make_async_copy(piece, target, out_sem.at[number]))
        at += rows
    for load in loads:
        load.start()
    for load, store in zip(loads, stores):
        load.wait()
        store.start()
    for store in stores:
        store.wait()


def place(arrays, sources, to_rows, shape):
    count = len(sources)
    wide = max(width for _, _, _, _, width, _ in sources)
    total = sum(rows for _, _, rows, _, _, _ in sources)
    return pl.pallas_call(
        partial(place_kernel, sources),
        out_shape=jax.ShapeDtypeStruct(shape, arrays[0].dtype),
        grid_spec=pltpu.PrefetchScalarGridSpec(
            num_scalar_prefetch=1,
            grid=(1,),
            in_specs=[pl.BlockSpec(memory_space=pl.ANY)] * len(arrays),
            out_specs=pl.BlockSpec(memory_space=pl.ANY),
            scratch_shapes=[
                pltpu.VMEM((total, wide), arrays[0].dtype),
                pltpu.SemaphoreType.DMA((count,)),
                pltpu.SemaphoreType.DMA((count,)),
            ],
        ),
        compiler_params=pltpu.CompilerParams(vmem_limit_bytes=total * wide * 2 + 4 * 2**20),
        name="place",
    )(to_rows, *arrays)


def to_ring(table):
    size = lax.axis_size("seq")
    me = lax.axis_index("seq")
    return jnp.stack(
        [lax.dynamic_index_in_dim(table, (me - k) % size, 0, keepdims=False) for k in range(size)]
    )


def head_of(rank, place):
    groups, ranks = lax.axis_size("dp"), lax.axis_size("seq")
    blocks = groups * ranks // HEADS
    if blocks <= ranks:
        held = groups // blocks
        return (rank % blocks * held + place) * (ranks // blocks) + rank // blocks
    return place * ranks + rank


def heads_of():
    ranks = lax.axis_size("seq")
    return [[head_of(rank, place) for place in range(HEADS // ranks)] for rank in range(ranks)]


def head_pieces(rank, place):
    held = HEADS // lax.axis_size("seq")
    return place // held * HEADS + head_of(rank, place % held)


def hidden_pieces(rank, place):
    return place * lax.axis_size("seq") + rank


def own_heads():
    numbers = jnp.array(heads_of())
    mine = lax.dynamic_index_in_dim(numbers, lax.axis_index("seq"), 0, keepdims=False)
    return (mine[:, None] == jnp.arange(HEADS)[None, :]).astype(WIDE)


def exact(left, right):
    return jnp.dot(left, right, precision=lax.Precision.HIGHEST, preferred_element_type=WIDE)


def out_route():
    groups, ranks = lax.axis_size("dp"), lax.axis_size("seq")
    blocks = groups * ranks // HEADS
    route = []
    for group in range(groups):
        for rank in range(ranks):
            if blocks <= ranks:
                held = groups // blocks
                high, low = divmod(group, held)
                pair, part = divmod(rank, blocks)
                target = (part * held + low, pair * blocks + high)
            else:
                span = blocks // ranks
                head, extra = divmod(group, span)
                high, low = divmod(head, ranks)
                target = ((high * ranks + rank) * span + extra, low)
            route.append((group * ranks + rank, target[0] * ranks + target[1]))
    return route


def out_parts():
    groups, ranks = lax.axis_size("dp"), lax.axis_size("seq")
    blocks = groups * ranks // HEADS
    if blocks <= ranks:
        return ((blocks, groups // blocks), (1, 0))
    return ((HEADS // ranks, ranks, blocks // ranks), (0, 2, 1))


def out_rows(table, rows):
    split, order = out_parts()
    ranks = lax.axis_size("seq")
    width = table.shape[1]
    whole = table.reshape(split + (ranks, rows, width))
    at = len(split)
    return whole.transpose(order + (at + 1, at, at + 2)).reshape(-1, ranks * width)


def gather_groups(block):
    return lax.all_gather(block, "dp", axis=0, tiled=True)


def swap_bit(block, axis, bit):
    return lax.ppermute(
        block, axis, [(place, place ^ (1 << bit)) for place in range(lax.axis_size(axis))]
    )


def bits_of(axis):
    return range(lax.axis_size(axis).bit_length() - 1)


def pair_kernel(lefts, rights, rows, kept, me_ref, *refs):
    left_refs, right_refs, rest = refs[:lefts], refs[lefts : lefts + rights], refs[lefts + rights :]
    side = lax.rem(me_ref[0], 2)
    blocks = []
    for number in range(left_refs[0].shape[1] // rows // 2):
        group = (me_ref[0] // 2 ^ number) * 2 + (side if kept else 1 - side)
        columns = pl.ds(pl.multiple_of(group * rows, rows), rows)
        blocks.append(jnp.concatenate([ref[:, columns] for ref in left_refs]))
    left, right = jnp.concatenate(blocks, axis=1), joined(right_refs)
    total = lax.dot_general(left, right, (((0,), (0,)), ((), ())), preferred_element_type=WIDE)
    if not kept:
        rest[0][...] = total.astype(LOW)
        return
    half = total.shape[1] // 2
    for number in range(len(blocks)):
        part = slice(number * rows, (number + 1) * rows)
        low = (total[part] + rest[0][part, :].astype(WIDE)).astype(LOW)
        rest[1 + number][...] = low[:, :half]
        rest[1 + len(blocks) + number][...] = low[:, half:]


def pair_product(lefts, rights, rows, got=None):
    groups, me = lax.axis_size("dp"), lax.axis_index("dp")
    pairs, width = groups // 2, rights[0].shape[1]
    kept = got is not None
    operands = [*lefts, *rights, *([got] if kept else [])]
    if kept:
        out_shape = [pltpu.HBM((rows, width // 2), LOW)] * (2 * pairs)
    else:
        out_shape = [pltpu.HBM((pairs * rows, width), LOW)]
    results = pl.pallas_call(
        partial(pair_kernel, len(lefts), len(rights), rows, kept),
        out_shape=out_shape,
        grid_spec=pltpu.PrefetchScalarGridSpec(
            num_scalar_prefetch=1,
            grid=(1,),
            in_specs=[whole_block(array) for array in operands],
            out_specs=[whole_block(result) for result in out_shape],
        ),
        compiler_params=pltpu.CompilerParams(vmem_limit_bytes=48 * 2**20),
        cost_estimate=SMALL,
        name="pair_product",
    )(me[None], *operands)
    return list(results) if kept else results[0]


GELU_SCALE = (2 / jnp.pi) ** 0.5
GELU_CUBE = 0.044715


def gelu_parts(value):
    square = value * value
    bent = jnp.tanh(GELU_SCALE * value * (1 + GELU_CUBE * square))
    slope = 0.5 * (1 + bent) + 0.5 * value * (1 - bent * bent) * GELU_SCALE * (
        1 + 3 * GELU_CUBE * square
    )
    return 0.5 * value * (1 + bent), slope


def joined(refs):
    return jnp.concatenate([ref[...] for ref in refs])


CHUNK = 256


def stream_kernel(work, inputs, results, *refs):
    weight_ref, operands = refs[0], refs[1 : 1 + inputs]
    result_refs, (held, sem, *total) = refs[1 + inputs : 1 + inputs + results], refs[1 + inputs + results :]
    copies = []
    for number in range(held.shape[1] // CHUNK):
        part = pl.ds(number * CHUNK, CHUNK)
        copies.append(
            pltpu.make_async_copy(weight_ref.at[:, part], held.at[:, part], sem.at[number])
        )
    for copy in copies:
        copy.start()
    for number, copy in enumerate(copies):
        copy.wait()
        columns = slice(number * CHUNK, (number + 1) * CHUNK)
        work(number, columns, held[:, columns], operands, result_refs, *total)


def stream(name, work, weight, extent, operands, results, total=None):
    shape = (weight.shape[0], extent)
    scratch = [pltpu.VMEM(shape, weight.dtype), pltpu.SemaphoreType.DMA((extent // CHUNK,))]
    if total is not None:
        scratch.append(pltpu.VMEM(total, WIDE))
    return pl.pallas_call(
        partial(stream_kernel, work, len(operands), len(results)),
        out_shape=results,
        grid=(1,),
        in_specs=[pl.BlockSpec(memory_space=pl.ANY)]
        + [pl.BlockSpec(array.shape, lambda number: (0, 0)) for array in operands],
        out_specs=[pl.BlockSpec(result.shape, lambda number: (0, 0)) for result in results],
        scratch_shapes=scratch,
        compiler_params=pltpu.CompilerParams(vmem_limit_bytes=32 * 2**20),
        cost_estimate=pl.CostEstimate(
            flops=2 * operands[0].shape[0] * shape[0] * shape[1],
            bytes_accessed=2 * shape[0] * shape[1],
            transcendentals=0,
        ),
        name=name,
    )(pltpu.with_memory_space_constraint(weight, pltpu.HBM), *operands)


def column_block(rows, wide):
    return pl.BlockSpec((rows, wide), lambda number: (0, number))


def project_kernel(left_ref, weight_ref, bias_ref, to_ref):
    total = jnp.dot(left_ref[...], weight_ref[...], preferred_element_type=WIDE)
    to_ref[...] = (total + bias_ref[...]).astype(to_ref.dtype)


def project(left, weight, bias):
    (rows, depth), width = left.shape, bias.shape[0]
    return pl.pallas_call(
        project_kernel,
        out_shape=jax.ShapeDtypeStruct((rows, width), LOW),
        grid=(width // CHUNK,),
        in_specs=[whole_block(left), column_block(depth, CHUNK), column_block(1, CHUNK)],
        out_specs=column_block(rows, CHUNK),
        compiler_params=pltpu.CompilerParams(vmem_limit_bytes=16 * 2**20),
        name="project",
    )(left, pltpu.with_memory_space_constraint(weight, pltpu.HBM), bias[None])


def upward_product(lefts, weight, bias):
    def work(number, columns, chunk, operands, results):
        total = jnp.dot(joined(operands[:-1]), chunk, preferred_element_type=WIDE)
        total = total + operands[-1][:, columns]
        results[0][:, columns] = total
        results[1][:, columns] = gelu_parts(total)[0].astype(LOW)

    rows, width = sum(left.shape[0] for left in lefts), weight.shape[1]
    results = [jax.ShapeDtypeStruct((rows, width), kind) for kind in (WIDE, LOW)]
    return stream("upward_product", work, weight, width, [*lefts, bias[None]], results)


def dense_kernel(lefts, *refs):
    weight_ref, reward_ref, reward_to_ref = refs[lefts], refs[lefts + 1], refs[-1]
    total = jnp.dot(joined(refs[:lefts]), weight_ref[...], preferred_element_type=WIDE)
    row = 0
    for to_ref in refs[lefts + 2 : -1]:
        to_ref[...] = total[row : row + to_ref.shape[0]].astype(LOW)
        row += to_ref.shape[0]
    scaled = total * reward_ref[...]
    part = scaled[:, :128]
    for start in range(128, scaled.shape[1], 128):
        part = part + scaled[:, start : start + 128]

    @pl.when(pl.program_id(0) == 0)
    def _():
        reward_to_ref[...] = part

    @pl.when(pl.program_id(0) > 0)
    def _():
        reward_to_ref[...] += part


def dense_product(lefts, weight, reward):
    depth, width = weight.shape
    rows = sum(left.shape[0] for left in lefts)
    return pl.pallas_call(
        partial(dense_kernel, len(lefts)),
        out_shape=[jax.ShapeDtypeStruct((left.shape[0], width), LOW) for left in lefts]
        + [jax.ShapeDtypeStruct((rows, 128), WIDE)],
        grid=(width // CHUNK,),
        in_specs=[whole_block(left) for left in lefts]
        + [column_block(depth, CHUNK), column_block(1, CHUNK)],
        out_specs=[column_block(left.shape[0], CHUNK) for left in lefts]
        + [pl.BlockSpec((rows, 128), lambda number: (0, 0))],
        compiler_params=pltpu.CompilerParams(vmem_limit_bytes=16 * 2**20),
        name="dense_product",
    )(*lefts, weight, reward[None])


def against_dot(left, weight):
    return lax.dot_general(left, weight, (((1,), (1,)), ((), ())), preferred_element_type=WIDE)


def against_stream(name, lefts, weight, operands, results, finish):
    rows, depth = sum(left.shape[0] for left in lefts), lefts[0].shape[1]

    def work(number, columns, chunk, operand_refs, result_refs, total):
        left = jnp.concatenate([ref[:, columns] for ref in operand_refs[: len(lefts)]])
        part = against_dot(left, chunk)
        total[...] = part if number == 0 else total[...] + part
        if number == depth // CHUNK - 1:
            finish(total, operand_refs[len(lefts) :], result_refs)

    shape = (rows, weight.shape[0])
    return stream(name, work, weight, depth, [*lefts, *operands], results, shape)


def column_sums(*values):
    sums = [jnp.sum(value, axis=0, keepdims=True) for value in values]
    return jnp.concatenate(sums + [jnp.zeros((8 - len(sums), sums[0].shape[1]), WIDE)])


def by_chunk(width):
    return [slice(start, start + CHUNK) for start in range(0, width, CHUNK)]


def second_kernel(down_ref, up_ref, left_ref, upward_ref, term_ref, low_ref, sums_ref, *scratch):
    down, up, down_sem, up_sem, total = scratch
    width = down.shape[1]
    copies = [
        [
            pltpu.make_async_copy(source.at[:, columns], held.at[:, columns], sem.at[number])
            for number, columns in enumerate(pl.ds(start, CHUNK) for start in range(0, width, CHUNK))
        ]
        for source, held, sem in ((down_ref, down, down_sem), (up_ref, up, up_sem))
    ]
    for copy in copies[0] + copies[1]:
        copy.start()
    for number, columns in enumerate(by_chunk(width)):
        copies[0][number].wait()
        part = against_dot(left_ref[:, columns], down[:, columns])
        total[...] = part if number == 0 else total[...] + part
    for number, columns in enumerate(by_chunk(width)):
        slope = gelu_parts(upward_ref[:, columns])[1]
        low = (total[:, columns] * slope).astype(LOW)
        low_ref[:, columns] = low
        sums_ref[:, columns] = column_sums(low.astype(WIDE))
        copies[1][number].wait()
        part = against_dot(low, up[:, columns])
        term_ref[...] = part if number == 0 else term_ref[...] + part


def second_product(left, weight_down, weight_up, upward):
    rows, width = upward.shape
    chunks = width // CHUNK
    results = [
        jax.ShapeDtypeStruct((rows, width), WIDE),
        jax.ShapeDtypeStruct((rows, width), LOW),
        jax.ShapeDtypeStruct((8, width), WIDE),
    ]
    return pl.pallas_call(
        second_kernel,
        out_shape=results,
        grid=(1,),
        in_specs=[pl.BlockSpec(memory_space=pl.ANY)] * 2
        + [pl.BlockSpec(array.shape, lambda number: (0, 0)) for array in (left, upward)],
        out_specs=[pl.BlockSpec(result.shape, lambda number: (0, 0)) for result in results],
        scratch_shapes=[pltpu.VMEM(weight.shape, LOW) for weight in (weight_down, weight_up)]
        + [pltpu.SemaphoreType.DMA((chunks,))] * 2
        + [pltpu.VMEM((rows, width), WIDE)],
        compiler_params=pltpu.CompilerParams(vmem_limit_bytes=48 * 2**20),
        cost_estimate=pl.CostEstimate(
            flops=4 * rows * width * width, bytes_accessed=4 * width * width, transcendentals=0
        ),
        name="second_product",
    )(
        *(pltpu.with_memory_space_constraint(weight, pltpu.HBM) for weight in (weight_down, weight_up)),
        left,
        upward,
    )


def against(lefts, weight, kind=WIDE):
    def finish(total, operands, results):
        results[0][...] = total[...].astype(kind)

    rows = sum(left.shape[0] for left in lefts)
    result = jax.ShapeDtypeStruct((rows, weight.shape[0]), kind)
    return against_stream("against", lefts, weight, [], [result], finish)[0]


def against_sums(left, weight, normal):
    def finish(total, operands, results):
        for columns in by_chunk(normal.shape[1]):
            value = total[:, columns]
            results[0][:, columns] = value
            results[1][:, columns] = column_sums(value * operands[0][:, columns], value)

    rows, width = normal.shape
    results = [jax.ShapeDtypeStruct((rows, width), WIDE), jax.ShapeDtypeStruct((8, width), WIDE)]
    return against_stream("against_sums", [left], weight, [normal], results, finish)


def masked_scores(query, key, queried_ref, keyed_ref, scale):
    scores = against_dot(query, key) * scale
    segment, place = queried_ref[:, 0:1], queried_ref[:, 1:2]
    other, before = keyed_ref[0:1, :], keyed_ref[1:2, :]
    allowed = ((other == 0) | (other == segment)) & (before <= place)
    return jnp.where(allowed, scores, MASKED)


def attend_kernel(scale, query_ref, key_ref, value_ref, queried_ref, keyed_ref, to_ref, log_ref):
    scores = masked_scores(query_ref[...], key_ref[...], queried_ref, keyed_ref, scale)
    highest = jnp.max(scores, axis=1, keepdims=True)
    exponent = jnp.exp(scores - highest)
    totals = jnp.sum(exponent, axis=1, keepdims=True)
    chances = (exponent / totals).astype(LOW)
    to_ref[...] = jnp.dot(chances, value_ref[...], preferred_element_type=WIDE).astype(LOW)
    log_ref[0] = highest + jnp.log(totals)


def head_blocks(length, wide, count):
    return [
        pl.BlockSpec((length, wide), lambda head, which=which: (0, which * count + head))
        for which in range(3)
    ]


def attend(projected, queried, keyed, wide, scale):
    length, columns = projected.shape
    count = columns // 3 // wide
    return pl.pallas_call(
        partial(attend_kernel, scale),
        out_shape=[
            jax.ShapeDtypeStruct((length, columns // 3), LOW),
            jax.ShapeDtypeStruct((count, length, 1), WIDE),
        ],
        grid=(count,),
        in_specs=head_blocks(length, wide, count)
        + [
            pl.BlockSpec((length, 2), lambda head: (0, 0)),
            pl.BlockSpec((2, length), lambda head: (0, 0)),
        ],
        out_specs=[
            pl.BlockSpec((length, wide), lambda head: (0, head)),
            pl.BlockSpec((1, length, 1), lambda head: (head, 0, 0)),
        ],
        compiler_params=pltpu.CompilerParams(vmem_limit_bytes=24 * 2**20),
        name="attend",
    )(projected, projected, projected, queried, keyed)


def attend_back_kernel(
    scale,
    count,
    query_ref,
    key_ref,
    value_ref,
    queried_ref,
    keyed_ref,
    log_ref,
    grad_ref,
    to_ref,
    sums_ref,
):
    query, key, grad = query_ref[...], key_ref[...], grad_ref[...]
    wide = query.shape[1]
    scores = masked_scores(query, key, queried_ref, keyed_ref, scale)
    chances = jnp.exp(scores - log_ref[0])
    chance_grad = against_dot(grad, value_ref[...])
    weighted = jnp.sum(chances * chance_grad, axis=1, keepdims=True)
    score_grad = (chances * (chance_grad - weighted)).astype(LOW)

    def across(left, right):
        return lax.dot_general(left, right, (((0,), (0,)), ((), ())), preferred_element_type=WIDE)

    grads = (
        jnp.dot(score_grad, key, preferred_element_type=WIDE) * scale,
        across(score_grad, query) * scale,
        across(chances.astype(LOW), grad),
    )
    for which, value in enumerate(grads):
        low = value.astype(LOW)
        start = pl.multiple_of((which * count + pl.program_id(0)) * wide, wide)
        to_ref[:, pl.ds(start, wide)] = low
        sums_ref[:, pl.ds(start, wide)] = column_sums(low.astype(WIDE))


def attend_back(projected, queried, keyed, log_rows, grad, wide, scale):
    length, columns = projected.shape
    count = columns // 3 // wide
    return pl.pallas_call(
        partial(attend_back_kernel, scale, count),
        out_shape=[
            jax.ShapeDtypeStruct((length, columns), LOW),
            jax.ShapeDtypeStruct((8, columns), WIDE),
        ],
        grid=(count,),
        in_specs=head_blocks(length, wide, count)
        + [
            pl.BlockSpec((length, 2), lambda head: (0, 0)),
            pl.BlockSpec((2, length), lambda head: (0, 0)),
            pl.BlockSpec((1, length, 1), lambda head: (head, 0, 0)),
            pl.BlockSpec((length, wide), lambda head: (0, head)),
        ],
        out_specs=[
            pl.BlockSpec((length, columns), lambda head: (0, 0)),
            pl.BlockSpec((8, columns), lambda head: (0, 0)),
        ],
        compiler_params=pltpu.CompilerParams(vmem_limit_bytes=32 * 2**20),
        name="attend_back",
    )(projected, projected, projected, queried, keyed, log_rows, grad)


SMALL = pl.CostEstimate(flops=1 << 30, bytes_accessed=1 << 22, transcendentals=0)


def whole_block(array):
    return pl.BlockSpec(array.shape, lambda *_: (0, 0), pipeline_mode=pl.Buffered(1))


def rows_kernel(lefts, *refs):
    left, right = joined(refs[:lefts]), joined(refs[lefts:-1])
    total = lax.dot_general(left, right, (((0,), (0,)), ((), ())), preferred_element_type=WIDE)
    refs[-1][...] = total.astype(LOW)


def rows_product(lefts, rights):
    rows, width = lefts[0].shape[1], rights[0].shape[1]
    wide = 512
    if rows % wide:
        return inner_rows(jnp.concatenate(lefts), jnp.concatenate(rights)).astype(LOW)
    return pl.pallas_call(
        partial(rows_kernel, len(lefts)),
        out_shape=pltpu.HBM((rows, width), LOW),
        grid=(rows // wide,),
        in_specs=[pl.BlockSpec((left.shape[0], wide), lambda number: (0, number)) for left in lefts]
        + [
            pl.BlockSpec(right.shape, lambda number: (0, 0), pipeline_mode=pl.Buffered(1))
            for right in rights
        ],
        out_specs=pl.BlockSpec((wide, width), lambda number: (number, 0)),
        compiler_params=pltpu.CompilerParams(vmem_limit_bytes=32 * 2**20),
        cost_estimate=pl.CostEstimate(
            flops=4 * rows * width * sum(left.shape[0] for left in lefts),
            bytes_accessed=4 * rows * width,
            transcendentals=0,
        ),
        name="rows_product",
    )(*lefts, *rights)


def scatter_product(lefts, rights):
    return scatter_groups(rows_product(lefts, rights))


def scatter_groups(table):
    return lax.psum_scatter(table, "dp", scatter_dimension=0, tiled=True)


def out_columns(left, rows):
    split, order = out_parts()
    count = left.shape[0]
    back = tuple(1 + order.index(axis) for axis in range(len(order)))
    moved = left.reshape((count,) + tuple(split[axis] for axis in order) + (rows,))
    return moved.transpose((0,) + back + (1 + len(split),)).reshape(count, -1)


def pair_onward(pieces):
    return [swap_bit(pieces[3], "dp", 1), swap_bit(pieces[7], "dp", 2)]


def sums_kernel(counts, *refs):
    at = 0
    for count, to_ref in zip(counts, refs[sum(counts) :]):
        total = refs[at][...].astype(WIDE)
        for ref in refs[at + 1 : at + count]:
            total = total + ref[...].astype(WIDE)
        to_ref[...] = total.astype(LOW)
        at += count


def sums_of(*groups):
    rows, width = groups[0][0].shape
    block = pl.BlockSpec((rows // 2, width), lambda number: (number, 0))
    return pl.pallas_call(
        partial(sums_kernel, [len(group) for group in groups]),
        out_shape=[jax.ShapeDtypeStruct((rows, width), LOW)] * len(groups),
        grid=(2,),
        in_specs=[block] * sum(len(group) for group in groups),
        out_specs=[block] * len(groups),
        cost_estimate=SMALL,
        name="sums_of",
    )(*(array for group in groups for array in group))


def pair_second(pieces, onward):
    return sums_of([pieces[2], onward[0]], [pieces[5], onward[1]])


def pair_last(sent):
    return [swap_bit(sent[0], "dp", 2), swap_bit(sent[1], "dp", 1)]


def pair_staying(pieces):
    return [swap_bit(pieces[1], "dp", 1), swap_bit(pieces[6], "dp", 2)]


def pair_sum(pieces, staying, second):
    groups = zip((pieces[0], pieces[4]), staying, second)
    return jnp.concatenate(sums_of(*(list(group) for group in groups)), axis=1)


def rank_rows(table, rows):
    ranks, me = lax.axis_size("seq"), lax.axis_index("seq")
    return [
        lax.dynamic_slice_in_dim(table, (me + shift) % ranks * rows, rows, 0)
        for shift in range(ranks)
    ]


def swap_rank(block, shift):
    size = lax.axis_size("seq")
    return lax.ppermute(block, "seq", [(place, (place + shift) % size) for place in range(size)])


def swap_ranks(blocks):
    return [blocks[0]] + [swap_rank(blocks[shift], shift) for shift in range(1, len(blocks))]


def rows_by_rank(blocks, beside=None):
    ranks, me = len(blocks), lax.axis_index("seq")
    rows, width = blocks[0].shape
    sources = [(number, 0, rows, 0, width, 0) for number in range(ranks)]
    to_rows = [(me + ranks - number) % ranks * rows for number in range(ranks)]
    arrays, more = list(blocks), 0
    if beside is not None:
        more = beside.shape[1] // ranks
        sources += [(ranks, 0, rows, number * more, more, width) for number in range(ranks)]
        to_rows += [number * rows for number in range(ranks)]
        arrays.append(beside)
    return place(arrays, sources, jnp.stack([jnp.int32(row) for row in to_rows]), (ranks * rows, width + more))


def by_number(blocks):
    return to_ring(jnp.stack(blocks))


def small_order():
    groups, ranks = lax.axis_size("dp"), lax.axis_size("seq")
    number = jnp.arange(groups * ranks)
    place = ((number // ranks) ^ lax.axis_index("dp")) * ranks + (
        (number % ranks) ^ lax.axis_index("seq")
    )
    return (place[:, None] == number[None, :]).astype(WIDE)


def small_groups(table):
    for bit in reversed(bits_of("dp")):
        half = table.shape[0] // 2
        table = table[:half] + swap_bit(table[half:], "dp", bit)
    return table


def small_ranks(table):
    size, me = lax.axis_size("seq"), lax.axis_index("seq")
    total = table[0]
    for shift in range(1, size):
        sent = lax.dynamic_index_in_dim(table, me ^ ((me + shift) % size), 0, keepdims=True)
        perm = [(place, (place + shift) % size) for place in range(size)]
        total = total + lax.ppermute(sent, "seq", perm)[0]
    return total


def small_rows(table):
    return jnp.dot(
        small_order().T, table, precision=lax.Precision.HIGHEST, preferred_element_type=WIDE
    )


def sum_ranks(table):
    size = lax.axis_size("seq")
    total = table
    for shift in range(1, size):
        total = total + lax.ppermute(
            table, "seq", [(place, (place + shift) % size) for place in range(size)]
        )
    return total


def spread_path(
    inputs,
    cotangent,
    segments,
    labels,
    step_ends,
    attend_gain,
    attend_shift,
    project_in,
    project_bias,
    project_out,
    output_bias,
    dense_gain,
    dense_shift,
    up_weight,
    up_bias,
    down_weight,
    down_bias,
    reward_weight,
):
    groups, ranks = lax.axis_size("dp"), lax.axis_size("seq")
    rank = lax.axis_index("seq")
    rows_here, places_here, width = inputs.shape
    all_rows = rows_here * groups
    head_width = width // HEADS
    heads_here = HEADS // ranks
    share = heads_here * head_width
    rows_in = project_in.shape[0]
    hidden_here = down_weight.shape[0]
    length = ranks * places_here
    score_scale = head_width ** (-0.5)

    small = (
        attend_gain,
        attend_shift,
        project_bias,
        output_bias,
        dense_gain,
        dense_shift,
        up_bias,
        down_bias,
        reward_weight,
    )
    sizes = [vector.shape[0] for vector in small]
    riders = [vector.reshape(-(-vector.shape[0] // 128), -1) for vector in small]
    riders += [segments, labels, step_ends]
    dealt_in = deal(project_in, head_pieces, head_width, riders)
    came_in = swap_ranks(dealt_in)
    out_moved = lax.ppermute(after(project_out, dealt_in), EVERY, out_route())
    rows_in_all = rows_by_rank(came_in, out_moved)
    gathered = gather_groups(rows_in_all)
    inputs_ring = ring_gather(
        after(inputs[0], came_in), [idle, idle, idle]
    )
    first_normals = []
    for halves in inputs_ring:
        normal, inverse = normal_parts(jnp.concatenate(halves).astype(WIDE))
        if not first_normals:
            first_inverse = inverse
        first_normals.append(normal)
    dealt_up = deal(after(up_weight, [rows_in_all]), hidden_pieces, hidden_here)
    came_up = swap_ranks(after(dealt_up, inputs_ring[-1]))
    gathered = after(gathered, first_normals)
    rows_up_all = rows_by_rank(came_up)
    weight_up = gather_groups(rows_up_all)
    weight_down = gather_groups(after(down_weight, [rows_up_all]))
    riders = gathered[:, 3 * share : 3 * share + 128]
    lines_all = sum(-(-size // 128) for size in sizes) + 3
    lines_all = -(-lines_all // 8) * 8
    riders = riders.reshape(groups * ranks, rows_in, 128)[:, :lines_all].astype(WIDE)
    vectors = []
    row = 0
    for size in sizes + [places_here] * 3:
        lines = -(-size // 128)
        vectors.append(
            riders[:, row : row + lines].reshape(groups * ranks, -1)[:, :size].reshape(-1)
        )
        row += lines
    gain_one, shift_one, bias_in, bias_out, gain_two, shift_two, bias_up, bias_down, reward_wide = (
        vectors[: len(sizes)]
    )

    held = own_heads()
    bias_heads = exact(held, bias_in.reshape(2, HEADS, head_width).transpose(1, 0, 2).reshape(HEADS, -1))
    bias_heads = bias_heads.reshape(heads_here, 2, head_width)
    bias_full = jnp.concatenate(
        [bias_heads[:, 0].reshape(-1), jnp.zeros((share,), WIDE), bias_heads[:, 1].reshape(-1)]
    )
    bias_up_here = lax.dynamic_index_in_dim(
        bias_up.reshape(groups, ranks, hidden_here), rank, 1, keepdims=False
    ).reshape(-1)
    marks = jnp.stack(
        [
            lax.dynamic_index_in_dim(
                mark.reshape(groups, ranks, places_here), lax.axis_index("dp"), 0, keepdims=False
            )
            for mark in vectors[len(sizes) :]
        ],
        axis=1,
    )
    marks_ring = to_ring(marks)
    segments_ring = marks_ring[:, 0].reshape(-1)
    places_ring = to_ring(jnp.arange(length).reshape(ranks, places_here)).reshape(-1)

    own = inputs[0].astype(WIDE)
    firsts = [(normal * gain_one + shift_one).astype(LOW) for normal in first_normals]
    projected = project(jnp.concatenate(firsts), gathered, bias_full)
    gathered, projected = lax.optimization_barrier((gathered, projected))
    weight_out = out_rows(gathered[:, 3 * share + 128 :], rows_in)
    queried, keyed = (
        jnp.stack([segments_ring.astype(WIDE), places_ring.astype(WIDE)], axis=axis)
        for axis in (1, 0)
    )
    mixture, log_rows = attend(projected, queried, keyed, head_width, score_scale)

    def block_of(array, k):
        return array[k * places_here : (k + 1) * places_here]

    weight_back = None

    def contiguous(gate):
        nonlocal weight_back
        weight_back = after(gathered, gate)[:, : 3 * share]
        return [weight_back]

    mixture_out = None

    def in_blocks(gate):
        nonlocal mixture_out
        mixture_out = out_columns(after(mixture, gate), project_out.shape[0])
        return [mixture_out]

    branch = ring_sum(
        lambda k, gate: product(block_of(mixture, k), weight_out), [contiguous, in_blocks, idle]
    )
    weight_back, mixture_out = lax.optimization_barrier((weight_back, mixture_out))
    hidden = own + branch + bias_out

    second_normal, second_inverse = normal_parts(hidden)
    second_value = second_normal * gain_two + shift_two

    rows_all = ranks * rows_in
    fenced = groups == 8 and rows_all % 128 == 0
    steady = (segments[0, 0] | 1) != 0

    def step(work, *operands):
        return fence(steady, work, *operands) if fenced else work(*operands)

    def upward_of(k, halves):
        return upward_product(halves, weight_up, bias_up_here)

    seconds, found = ring_gather(second_value.astype(LOW), use=upward_of, plan=(1, 1, 1))

    def dense_one(halves, block):
        return upward_of(None, halves), ring_move([block])[0]

    def dense_two(activated, block):
        return dense_product(activated, weight_down, reward_wide), ring_move([block])[0]

    cotangents = [cotangent[0]]
    last, block = step(dense_one, seconds[-1], cotangents[-1])
    cotangents.append(block)
    upwards, activated = map(list, zip(*found, last))
    (*dense_parts, reward_lanes), block = step(dense_two, activated, cotangents[-1])
    cotangents.append(block)
    dense_parts = lax.optimization_barrier(dense_parts)
    reward_parts = list(jnp.sum(reward_lanes, axis=-1).reshape(ranks, places_here))

    reward_parts[0] = reward_parts[0] + jnp.sum((hidden + bias_down) * reward_wide, axis=-1)
    rewards_all = sum_ranks(to_ring(jnp.stack(reward_parts)))
    scored = marks[:, 2] * (marks[:, 0] > 0)
    error_all = scored * (jax.nn.sigmoid(rewards_all) - marks[:, 1]) / all_rows
    error_ring = to_ring(error_all)
    rewards = lax.dynamic_index_in_dim(rewards_all, rank, 0, keepdims=False)

    def dense_grad(block, k):
        return block.astype(WIDE) + error_ring[k][:, None] * reward_wide

    dense_lows = [dense_grad(block, k).astype(LOW) for k, block in enumerate(cotangents)]

    def second_part(k, dense_low):
        term, *low = second_product(dense_low, weight_down, weight_up, upwards[k])
        return term, tuple(low)

    def second_first(block, dense_low):
        term, upward_low = second_part(1, dense_low)
        return term.astype(LOW), upward_low, ring_move([block])[0]

    def second_step(k, sent, dense_low):
        moved = ring_move([sent])[0]
        term, upward_low = second_part(k, dense_low)
        total = moved.astype(WIDE) + term
        return total if k == 0 else total.astype(LOW), upward_low

    upward_lows = [None] * ranks
    sent, upward_lows[1], block = step(second_first, cotangents[-1], dense_lows[1])

    def second_next(sent, block):
        dense_low = dense_grad(block, ranks - 1).astype(LOW)
        table = rows_product(activated, [*dense_lows, dense_low])
        return second_step(2, sent, dense_lows[2]), dense_low, table

    (sent, upward_lows[2]), dense_low, down_table = step(second_next, sent, block)
    dense_lows.append(dense_low)
    down_summed = scatter_groups(down_table)
    for k in list(range(3, ranks)) + [0]:
        sent, upward_lows[k] = step(partial(second_step, k), sent, dense_lows[k])
    second_grad = sent
    result_grad = after(dense_grad(cotangents[0], 0), [sent])
    upward_lows, upward_sums = zip(*upward_lows)
    reward_weight_gradient = jnp.sum(error_ring[0][:, None] * (hidden + bias_down), axis=0)
    for k, part in enumerate(dense_parts):
        reward_weight_gradient += jnp.sum(error_ring[k][:, None] * part.astype(WIDE), axis=0)
    down_bias_gradient = jnp.sum(dense_lows[0].astype(WIDE), axis=0)
    up_bias_gradient = sum(upward_sums)[0]
    dense_gain_gradient = jnp.sum(second_grad * second_normal, axis=0)
    dense_shift_gradient = jnp.sum(second_grad, axis=0)
    hidden_grad = result_grad + normalize_back(second_grad, second_normal, second_inverse, gain_two)

    branch_low = hidden_grad.astype(LOW)
    seconds = sum(seconds, [])
    output_bias_gradient = jnp.sum(branch_low.astype(WIDE), axis=0)

    def by_device(vectors):
        return jnp.concatenate([vector.reshape(groups * ranks, -1) for vector in vectors], axis=1)

    def early_table():
        up_bias_all = lax.dynamic_update_index_in_dim(
            jnp.zeros((groups, ranks, hidden_here), WIDE),
            up_bias_gradient.reshape(groups, hidden_here),
            rank,
            1,
        )
        return by_device(
            (
                output_bias_gradient,
                dense_gain_gradient,
                dense_shift_gradient,
                up_bias_all,
                down_bias_gradient,
                reward_weight_gradient,
            )
        )

    def back(mixture_grad):
        return attend_back(
            projected, queried, keyed, log_rows, mixture_grad, head_width, score_scale
        )

    def first_part(projected_grad, k):
        return against_sums(block_of(projected_grad, k), weight_back, first_normals[k])

    def inputs_back(first_grad):
        return hidden_grad + normalize_back(
            first_grad, first_normals[0], first_inverse, gain_one
        )

    def small_table(bias_sums, first_sums, early):
        bias_heads = jnp.concatenate([bias_sums[0, :share], bias_sums[0, 2 * share :]])
        bias_heads = bias_heads.reshape(2, heads_here, head_width)
        bias_all = jnp.concatenate(
            [exact(held.T, bias_heads[which]).reshape(-1) for which in range(2)]
        )
        gain_sum, shift_sum = sum(first_sums)[:2]
        return jnp.concatenate([by_device((gain_sum, shift_sum, bias_all)), early], axis=1)

    def out_back(out_summed):
        back = [(there, here) for here, there in out_route()]
        return lax.ppermute(out_summed, EVERY, back).astype(WIDE)

    def result_back(dense_sum):
        return (hidden + dense_sum + bias_down).astype(LOW)

    def sent_rows(summed):
        return rank_rows(summed.astype(LOW), rows_in)

    if fenced:

        def gather_one(block):
            return ring_move([block])[0], pair_product(seconds, upward_lows, rows_all)

        def gather_two(block, up_sent):
            return ring_move([block])[0], swap_bit(up_sent, "dp", 0), early_table()

        def gather_three(block, up_got):
            return ring_move([block])[0], pair_product(seconds, upward_lows, rows_all, up_got)

        def attend_one(branch_lows, up_pieces):
            dense_sum = ring_step(dense_parts[1], dense_parts[2])
            up_onward = pair_onward(up_pieces)
            mixture_grad = against(branch_lows, weight_out, LOW)
            out_table = rows_product([mixture_out], branch_lows)
            return dense_sum, up_onward, mixture_grad, out_table

        def attend_two(dense_sum, up_pieces, up_onward, mixture_grad):
            dense_sum = ring_step(dense_sum, dense_parts[3])
            up_second = pair_last(pair_second(up_pieces, up_onward))
            return dense_sum, up_second, back(mixture_grad)

        def attend_three(dense_sum, up_pieces, projected_grad):
            dense_sum = ring_step(dense_sum, dense_parts[0], WIDE)
            up_staying = pair_staying(up_pieces)
            in_sent = pair_product(firsts, [projected_grad], rows_all)
            term, sums = first_part(projected_grad, 1)
            return result_back(dense_sum), up_staying, in_sent, term.astype(LOW), sums

        def first_one(sent, in_sent, projected_grad, up_pieces, up_staying, up_second):
            moved = ring_move([sent])[0]
            in_got = swap_bit(in_sent, "dp", 0)
            term, sums = first_part(projected_grad, 2)
            up_sent = sent_rows(pair_sum(up_pieces, up_staying, up_second))
            in_pieces = list(pair_product(firsts, [projected_grad], rows_all, in_got))
            moved = after(moved, in_pieces)
            return (moved.astype(WIDE) + term).astype(LOW), in_pieces, up_sent, sums

        def first_two(sent, in_pieces, projected_grad, bias_sums, first_sums, early, up_near):
            moved = ring_move([sent])[0]
            in_staying, in_onward = pair_staying(in_pieces), pair_onward(in_pieces)
            in_second = pair_second(in_pieces, in_onward)
            up_near = swap_rank(after(up_near, in_onward[:1]), near[0])
            term, sums = first_part(projected_grad, 3)
            last_term, last_sums = first_part(projected_grad, 0)
            table = small_rows(small_table(bias_sums, [sums, last_sums, *first_sums], early))
            sent = (moved.astype(WIDE) + term).astype(LOW)
            return sent, in_staying, in_second, up_near, last_term, table

        def first_three(sent, in_pieces, in_staying, in_second, term, table, up_far):
            moved = ring_move([sent])[0]
            up_far = swap_rank(up_far, far)
            in_second = pair_last(in_second)
            summed = small_ranks(small_groups(after(table, in_second[:1])))
            in_sent = sent_rows(pair_sum(in_pieces, in_staying, in_second))
            moved, up_far = after((moved, up_far), [up_far])
            return moved.astype(WIDE) + term, in_sent, summed, up_far

        def last(in_sent, came_up, up_near, first_grad):
            for shift, block in zip(near[1:], up_near):
                came_up[shift] = swap_rank(block, shift)
            came_up = [came_up[shift] for shift in range(ranks)]
            came_in = swap_ranks(in_sent)
            first_grad, down_late = after((first_grad, down_early), [came_in[1]])
            done = (
                collect(came_up, hidden_pieces, hidden_here),
                inputs_back(first_grad),
                down_late.astype(WIDE),
                out_back(out_early),
            )
            came_in, done = lax.optimization_barrier((came_in, done))
            return collect(came_in, head_pieces, head_width), *done

        branch_lows = [branch_low]
        moved, up_sent = step(gather_one, branch_low)
        branch_lows.append(moved)
        moved, up_got, early = step(gather_two, moved, up_sent)
        branch_lows.append(moved)
        moved, up_pieces = step(gather_three, moved, up_got)
        branch_lows.append(moved)
        dense_sum, up_onward, mixture_grad, out_table = step(attend_one, branch_lows, up_pieces)
        out_summed = scatter_groups(out_table)
        dense_sum, up_second, (projected_grad, bias_sums) = step(
            attend_two, dense_sum, up_pieces, up_onward, mixture_grad
        )
        result_low, up_staying, in_sent, sent, sums_one = step(
            attend_three, dense_sum, up_pieces, projected_grad
        )
        sent, down_early = after((sent, down_summed), [down_summed])
        sent, in_pieces, up_sent, sums_two = step(
            first_one, sent, in_sent, projected_grad, up_pieces, up_staying, up_second
        )
        far = ranks // 2
        near = [shift for shift in range(1, ranks) if shift != far]
        sent, in_staying, in_second, up_near, last_term, table = step(
            first_two,
            sent,
            in_pieces,
            projected_grad,
            bias_sums,
            [sums_one, sums_two],
            early,
            up_sent[near[0]],
        )
        sent, out_early = after((sent, out_summed), [out_summed])
        first_grad, in_sent, summed, up_far = step(
            first_three, sent, in_pieces, in_staying, in_second, last_term, table, up_sent[far]
        )
        came_up = {0: up_sent[0], far: up_far, near[0]: up_near}
        up_near = [up_sent[shift] for shift in near[1:]]
        (
            project_in_gradient,
            up_weight_gradient,
            inputs_gradient,
            down_weight_gradient,
            project_out_gradient,
        ) = step(last, in_sent, came_up, up_near, first_grad)
    else:
        branch_lows = sum(ring_gather(branch_low, cut=1), [])
        projected_grad, bias_sums = back(against(branch_lows, weight_out, LOW))
        out_summed = scatter_groups(rows_product([mixture_out], branch_lows))
        first_sums = [None] * ranks

        def first_term(k, gate):
            term, first_sums[k] = first_part(projected_grad, k)
            return term

        first_grad = ring_sum(first_term, cut=1)
        dense_sum = dense_parts[1]
        for part in dense_parts[2:] + dense_parts[:1]:
            dense_sum = ring_step(dense_sum, part, WIDE)
        up_summed = scatter_product(seconds, upward_lows)
        in_summed = scatter_product(firsts, [projected_grad])
        inputs_gradient, result_low = inputs_back(first_grad), result_back(dense_sum)
        table = small_rows(small_table(bias_sums, first_sums, early_table()))
        summed = small_ranks(small_groups(table))
        up_weight_gradient = collect(swap_ranks(sent_rows(up_summed)), hidden_pieces, hidden_here)
        project_in_gradient = collect(swap_ranks(sent_rows(in_summed)), head_pieces, head_width)
        project_out_gradient = out_back(out_summed)
        down_weight_gradient = down_summed.astype(WIDE)
    parts = []
    start = 0
    for size in sizes:
        parts.append(summed[start : start + size])
        start += size
    return (
        result_low[None],
        rewards[None],
        inputs_gradient[None],
        parts[0],
        parts[1],
        project_in_gradient,
        parts[2],
        project_out_gradient,
        parts[3],
        parts[4],
        parts[5],
        up_weight_gradient,
        parts[6],
        down_weight_gradient,
        parts[7],
        parts[8],
    )


def solution(mesh):
    row = P("dp", "seq")
    wide_row = P("dp", "seq", None)
    vector = P(("dp", "seq"))
    matrix = P(("dp", "seq"), None)
    in_specs = (
        wide_row,
        wide_row,
        row,
        row,
        row,
        vector,
        vector,
        matrix,
        vector,
        matrix,
        vector,
        vector,
        vector,
        matrix,
        vector,
        matrix,
        vector,
        vector,
    )
    out_specs = (
        wide_row,
        row,
        wide_row,
        vector,
        vector,
        matrix,
        vector,
        matrix,
        vector,
        vector,
        vector,
        matrix,
        vector,
        matrix,
        vector,
        vector,
    )
    return jax.shard_map(
        spread_path, mesh=mesh, in_specs=in_specs, out_specs=out_specs, check_vma=False
    )
```
